256 devices in a mesh: dp: 32 (over x_lo, z, core), section: 8 (over y, x_hi).
Axes of the slice: x: 4 (x_hi: 2, x_lo: 2; x = x_hi * 2 + x_lo), y: 4, z: 8, core: 2. Of those that a mesh axis runs over, the one named last changes fastest.
Arguments:
- noise: bfloat16 [128, 64, 1536], P('dp'), may hold values from -6 to 6
- sched_index: int32 [128, 3], P('dp'), may hold values from 0 to 1000, as said below
- text_ids: int32 [128, 77], replicated, may hold values from 0 to 49407
- text_table: bfloat16 [49408, 1536], P('dp'), may hold values from -24 to 24
- time_weight: bfloat16 [256, 1536], replicated, may hold values from -0.375 to 0.375
- block_weight: bfloat16 [8, 1536, 1536], P('section', 'dp'), may hold values from -0.15625 to 0.15625
- block_mod: float32 [8, 3, 1536], P('section'), may hold values from -3 to 3
- student_weight: bfloat16 [1536, 1536], P('dp', 'section'), may hold values from -0.15625 to 0.15625
- student_mod: float32 [3, 1536], replicated, may hold values from -3 to 3
- feature_weight: bfloat16 [1536, 512], P('section'), may hold values from -0.15625 to 0.15625
- lin_weight: float32 [512], replicated, may hold values from 0.01 to 0.1
- token_weight: float32 [8192], P('dp'), may hold values from 0.5 to 2
Outputs:
- teacher_latents: bfloat16 [128, 64, 1536], P('dp')
- student_grad: float32 [1536, 1536], P(None, 'section')
- token_distance: float32 [8192], P(('dp', 'section'))
The draws below stay inside these ranges and needn't reach their ends.
Inputs may be any that keep to these rules, and one draw needn't show every extreme that they name: `sched_index`: each row falls strictly from left to right, by 62 to 250 a step, and starts at 500 or higher.
All inputs are finite; a program needn't handle non-finite values.
Results may differ from the reference program's by a relative error of at most 0.024.
Values may be sent and summed in bfloat16 or wider, within the bound.
A program may use at most 64 MiB of HBM per device.

```python
import math
import jax
import jax.numpy as jnp
import numpy as np
from jax import lax

D = 1536
VOCAB = 49408
FEAT = 512
TXT = 77
FREQ = 256
TOK = 64
STEPS = 2
LEVELS = 1000
SAMPLES = 128
N_SECTION = 8


def draw_sched_index(key, part):
    key_first = jax.random.fold_in(key, 11)
    key_falls = jax.random.fold_in(key, 23)
    first_index = jax.random.randint(key_first, (SAMPLES, 1), LEVELS // 2, LEVELS + 1)
    drops = jax.random.randint(key_falls, (SAMPLES, STEPS), LEVELS // 16, LEVELS // 4 + 1)
    return jnp.concatenate([first_index, first_index - jnp.cumsum(drops, axis=1)], axis=1).astype(jnp.int32)


def with_ends(values, rng, smallest, largest):
    shape = values.shape
    place = [jax.random.randint(jax.random.fold_in(rng, axis), (), 0, shape[axis]) for axis in range(len(shape))]
    values = values.at[tuple(place)].set(smallest)
    longest = shape.index(max(shape))
    place[longest] = (place[longest] + 1) % shape[longest]
    return values.at[tuple(place)].set(largest)


def shard_levels(key, extent, cuts, least, high):
    factor_of = 1.0
    for dim, parts in cuts:
        draws = jax.random.uniform(jax.random.fold_in(jax.random.fold_in(key, 6), dim), (parts,), jnp.float32, least / len(cuts), high / len(cuts))
        factor_of = factor_of * jnp.repeat(jnp.exp(draws), extent[dim] // parts).reshape((-1,) + (1,) * (len(extent) - 1 - dim))
    return factor_of


def rank_bounds(number_of, lean):
    loads = [(1 << 20) // math.isqrt(grade ** lean) + 1 for grade in range(1, number_of + 1)]
    width = 1 + sum(loads) // (1 << 30)
    return np.cumsum(np.array([max(1, weight // width) for weight in loads]))


def ranked_ids(key, dims, number_of, lean):
    table = rank_bounds(number_of, lean)
    ticket = jax.random.randint(jax.random.fold_in(key, 1), dims, 0, int(table[number_of - 1]))
    standing = jnp.searchsorted(jnp.asarray(table, jnp.int32), ticket, side="right")
    return jax.random.permutation(jax.random.fold_in(key, 2), number_of)[standing].astype(jnp.int32)


def normal_values(stream_key, extent, spread, limit, shards=(), kind=jnp.bfloat16):
    loudness = shard_levels(stream_key, extent, shards, -0.22, 0.18) if shards else 1.0
    result = jax.random.normal(stream_key, extent, jnp.float32) * spread * loudness
    return jnp.minimum(jnp.maximum(result, -limit), limit).astype(kind)


def setup_inputs(seed: int = 0) -> dict:
    streams_of = jax.random.split(jax.random.key(seed), 13)
    return {
        "noise": normal_values(streams_of[0], (SAMPLES, TOK, D), 1.0, 6.0, ((0, 32),)),
        "sched_index": draw_sched_index(jax.random.fold_in(streams_of[12], 71), 0),
        "text_ids": with_ends(ranked_ids(streams_of[2], (SAMPLES, TXT), VOCAB, 2), jax.random.fold_in(streams_of[2], 3), 0, VOCAB - 1).astype(jnp.int32),
        "text_table": normal_values(streams_of[3], (VOCAB, D), 4.0, 24.0, ((0, 32),)),
        "time_weight": normal_values(streams_of[4], (FREQ, D), FREQ ** -0.5, 0.375),
        "block_weight": normal_values(streams_of[5], (N_SECTION, D, D), D ** -0.5, 0.15625, ((0, 8), (1, 32))),
        "block_mod": normal_values(streams_of[6], (N_SECTION, 3, D), 0.5, 3.0, ((0, 8),), jnp.float32),
        "student_weight": normal_values(streams_of[7], (D, D), D ** -0.5, 0.15625, ((0, 32), (1, 8))),
        "student_mod": normal_values(streams_of[8], (3, D), 0.5, 3.0, (), jnp.float32),
        "feature_weight": normal_values(streams_of[9], (D, FEAT), D ** -0.5, 0.15625, ((0, 8),)),
        "lin_weight": jnp.clip(jnp.exp(jax.random.uniform(streams_of[10], (FEAT,), jnp.float32, math.log(0.01), math.log(0.1))), 0.01, 0.1),
        "token_weight": jnp.clip(0.5 + 1.5 * jax.random.uniform(streams_of[11], (SAMPLES * TOK,), jnp.float32) ** shard_levels(streams_of[11], (SAMPLES * TOK,), ((0, 32),), -0.2, 0.2), 0.5, 2.0),
    }


def modulated(hidden_f, cond_vec, gains):
    mean_sq = lax.optimization_barrier(jnp.mean(hidden_f * hidden_f, axis=-1, keepdims=True))
    normed = hidden_f * lax.rsqrt(mean_sq + 1e-06)
    return normed * (1.0 + cond_vec * gains[0]) + cond_vec * gains[1]

def teacher_block(hidden, weight, gains, cond_vec):
    hidden_f = hidden.astype(jnp.float32)
    inputs = modulated(hidden_f, cond_vec, gains).astype(jnp.bfloat16)
    mixed = jnp.dot(inputs.reshape(-1, hidden.shape[-1]), weight, preferred_element_type=jnp.float32)
    mixed = mixed.reshape(hidden.shape)
    return (hidden_f + (1.0 + cond_vec * gains[2]) * jax.nn.gelu(mixed)).astype(jnp.bfloat16)

def distance(feat_student, feat_teacher, lin_weight):
    relu_s = jax.nn.relu(feat_student)
    relu_t = jax.nn.relu(feat_teacher)
    unit_s = relu_s * lax.rsqrt(lax.optimization_barrier(jnp.mean(relu_s * relu_s, axis=-1, keepdims=True)) + 1e-06)
    unit_t = relu_t * lax.rsqrt(lax.optimization_barrier(jnp.mean(relu_t * relu_t, axis=-1, keepdims=True)) + 1e-06)
    gap = unit_s - unit_t
    return lax.optimization_barrier(jnp.sum(lin_weight * gap * gap, axis=-1))

def reference(noise, sched_index, text_ids, text_table, time_weight, block_weight, block_mod, student_weight, student_mod, feature_weight, lin_weight, token_weight):
    indices_f = sched_index.astype(jnp.float32)
    half_freq = FREQ // 2
    frequency = jnp.exp(-math.log(10000.0) * jnp.arange(half_freq, dtype=jnp.float32) / half_freq)
    angles = indices_f[:, :, None] * frequency
    embedding = jnp.concatenate([jnp.cos(angles), jnp.sin(angles)], axis=-1).astype(jnp.bfloat16)
    time_embed = jnp.dot(embedding.reshape(-1, FREQ), time_weight, preferred_element_type=jnp.float32)
    time_embed = time_embed.reshape(SAMPLES, STEPS + 1, D)
    pooled = lax.optimization_barrier(jnp.sum(jnp.take(text_table, text_ids, axis=0).astype(jnp.float32), axis=1)) / TXT
    conditions = jax.nn.silu(time_embed + pooled[:, None, :])
    deltas = (indices_f[:, 1:] - indices_f[:, :-1]) / LEVELS
    latents = noise
    for pass_id in range(STEPS):
        hidden = latents
        for section_id in range(N_SECTION):
            hidden = teacher_block(hidden, block_weight[section_id], block_mod[section_id], conditions[:, pass_id][:, None, :])
        latents = (latents.astype(jnp.float32) + deltas[:, pass_id][:, None, None] * hidden.astype(jnp.float32)).astype(jnp.bfloat16)
    teacher = latents
    cond_zero = conditions[:, 0][:, None, :]
    time_zero = (indices_f[:, 0] / LEVELS)[:, None, None]
    noise_f = noise.astype(jnp.float32)
    inputs = modulated(noise_f, cond_zero, student_mod).astype(jnp.bfloat16).reshape(-1, D)
    mixed = jnp.dot(inputs, student_weight, preferred_element_type=jnp.float32).reshape(noise.shape)
    gate_rows = 1.0 + cond_zero * student_mod[2]

    def advance(mixed_in):
        return noise_f - time_zero * (noise_f + gate_rows * jax.nn.gelu(mixed_in))
    moved, pull_back = jax.vjp(advance, mixed)
    feat_student = jnp.dot(moved.astype(jnp.bfloat16).reshape(-1, D), feature_weight, preferred_element_type=jnp.float32)
    feat_teacher = jnp.dot(teacher.reshape(-1, D), feature_weight, preferred_element_type=jnp.float32)

    def objective(feat_in):
        token_dist = distance(feat_in, feat_teacher, lin_weight)
        return (jnp.sum(token_weight * token_dist), token_dist)
    total, pull_feat, token_dist = jax.vjp(objective, feat_student, has_aux=True)
    grad_feat = pull_feat(jnp.ones_like(total))[0].astype(jnp.bfloat16)
    out_grad = lax.dot_general(grad_feat, feature_weight, (((1,), (1,)), ((), ())), preferred_element_type=jnp.float32)
    mixed_grad = pull_back(out_grad.reshape(noise.shape))[0].astype(jnp.bfloat16).reshape(-1, D)
    student_grad = lax.dot_general(inputs, mixed_grad, (((0,), (0,)), ((), ())), preferred_element_type=jnp.float32)
    return (teacher, student_grad, token_dist)
```

```python
import math

import jax
import jax.numpy as jnp
from jax import lax
from jax.experimental import pallas as pl
from jax.experimental.pallas import tpu as pltpu
from jax.sharding import Mesh
from jax.sharding import PartitionSpec as P

LEVELS = 1000
DP = ("dp_x", "dp_z", "dp_c")
DP_SECTION = ("dp_x", "dp_z", "dp_c", "section")
MESH = pl.DeviceIdType.MESH


def in_blocks(x, dim, count):
    shape = x.shape
    blocks = x.reshape(*shape[:dim], count, shape[dim] // count, *shape[dim + 1 :])
    return jnp.moveaxis(blocks, dim, 0)


def summed_on_arrival(x, axis, dim):
    blocks = in_blocks(x, dim, lax.axis_size(axis))
    arrived = lax.all_to_all(blocks, axis, split_axis=0, concat_axis=0, tiled=True)
    return arrived.sum(axis=0)


def in_order(blocks, dim):
    blocks = jnp.moveaxis(blocks, 0, dim)
    shape = blocks.shape
    return blocks.reshape(*shape[:dim], shape[dim] * shape[dim + 1], *shape[dim + 2 :])


def from_everyone(x, axis):
    copies = jnp.broadcast_to(x, (lax.axis_size(axis), *x.shape))
    return lax.all_to_all(copies, axis, split_axis=0, concat_axis=0, tiled=True)


def collect(x, axis, dim):
    return in_order(from_everyone(x, axis), dim)


def sum_at_owner(x, axis, dim):
    blocks = in_blocks(x, dim, lax.axis_size(axis))
    arrived = lax.all_to_all(blocks, axis, split_axis=0, concat_axis=0, tiled=True)
    return arrived.astype(jnp.float32).sum(axis=0)


def side_by_side(arrays, axis, dim, along):
    widths = [a.shape[along] for a in arrays]
    both = jnp.concatenate(arrays, axis=along)
    result = sum_at_owner(both, axis, dim)
    return tuple(jnp.split(result, [sum(widths[:k]) for k in range(1, len(widths))], axis=along))


def filled_up(lines, count):
    spare = -len(lines) % count
    return jnp.pad(lines, [(0, spare)] + [(0, 0)] * (lines.ndim - 1))


def gather_axes(x, axes, dim):
    far, near = axes
    initial = from_everyone(x, far)
    blocks = jnp.swapaxes(from_everyone(initial, near), 0, 1)
    return in_order(blocks.reshape(-1, *x.shape), dim)


def summed_rows(x, axes, dim):
    far, near = axes
    own = sum_at_owner(in_blocks(x, dim, lax.axis_size(far)), near, dim + 1)
    return jnp.sum(
        lax.all_to_all(own.astype(jnp.bfloat16), far, 0, 0, tiled=True).astype(jnp.float32), axis=0
    )


def sum_by_parts(x, axes):
    lines = x.reshape(-1, x.shape[-1])
    padded = filled_up(lines, lax.axis_size(axes[0]) * lax.axis_size(axes[1]))
    whole = gather_axes(summed_rows(padded, axes, 0).astype(jnp.bfloat16), axes, 0)
    return lax.slice_in_dim(whole, 0, len(lines)).reshape(x.shape).astype(jnp.float32)


def modulated(hidden_f, cond_vec, gains):
    mean_sq = jnp.mean(hidden_f * hidden_f, axis=-1, keepdims=True)
    normed = hidden_f * lax.rsqrt(mean_sq + 1e-06)
    return normed * (1.0 + cond_vec * gains[0]) + cond_vec * gains[1]


def teacher_block(hidden, weight, gains, cond_vec):
    hidden_f = hidden.astype(jnp.float32)
    inputs = modulated(hidden_f, cond_vec, gains).astype(jnp.bfloat16)
    mixed = jnp.dot(inputs, weight, preferred_element_type=jnp.float32)
    return (hidden_f + (1.0 + cond_vec * gains[2]) * jax.nn.gelu(mixed)).astype(jnp.bfloat16)


def distance(feat_student, feat_teacher, lin_weight):
    relu_s = jax.nn.relu(feat_student)
    relu_t = jax.nn.relu(feat_teacher)
    unit_s = relu_s * lax.rsqrt(jnp.mean(relu_s * relu_s, axis=-1, keepdims=True) + 1e-06)
    unit_t = relu_t * lax.rsqrt(jnp.mean(relu_t * relu_t, axis=-1, keepdims=True) + 1e-06)
    gap = unit_s - unit_t
    return jnp.sum(lin_weight * gap * gap, axis=-1)


def teacher_kernel(
    noise_ref,
    w_ref,
    gains_ref,
    delta_ref,
    out_ref,
    held,
    sent,
    inbox,
    start_x,
    first_x,
    inbox_recv,
    sent_send,
    first_send,
    first_recv,
    out_send,
    out_recv,
):
    mbs, rows, width = noise_ref.shape
    xl = lax.axis_index("dp_x")
    sec = lax.axis_index("section")
    barrier = pltpu.get_barrier_semaphore()
    for dx in range(2):
        for ds in range(8):
            if dx + ds > 0:
                pl.semaphore_signal(
                    barrier,
                    inc=1,
                    device_id={"dp_x": (xl + dx) % 2, "section": (sec + ds) % 8},
                    device_id_type=MESH,
                )
    pl.semaphore_wait(barrier, 15)

    def pass_on(t, slot, target):
        return pltpu.make_async_remote_copy(
            src_ref=sent.at[t],
            dst_ref=inbox.at[slot],
            send_sem=sent_send.at[t],
            recv_sem=inbox_recv.at[slot],
            device_id={"dp_x": 1 - xl, "section": target},
            device_id_type=MESH,
        )

    def share_first(j):
        return pltpu.make_async_remote_copy(
            src_ref=start_x.at[j],
            dst_ref=first_x,
            send_sem=first_send.at[j],
            recv_sem=first_recv,
            device_id={"section": j},
            device_id_type=MESH,
        )

    def share_out(slot, target):
        return pltpu.make_async_remote_copy(
            src_ref=out_ref.at[slot],
            dst_ref=out_ref.at[slot],
            send_sem=out_send.at[target],
            recv_sem=out_recv.at[slot],
            device_id={"section": target},
            device_id_type=MESH,
        )

    def run_pass(p):
        def step(j, carry):
            t = p * mbs + j
            if p == 0:

                @pl.when(sec == 0)
                def _():
                    held[...] = noise_ref[j]

            @pl.when((sec > 0) | (p > 0))
            def _():
                pass_on(t, t, 0).wait_recv()
                held[...] = inbox[t]

            if p > 0:

                @pl.when(sec == 0)
                def _():
                    moved = (
                        noise_ref[j].astype(jnp.float32)
                        + delta_ref[j // 2][:, :1] * held[...].astype(jnp.float32)
                    ).astype(jnp.bfloat16)
                    held[...] = moved
                    start_x[j] = moved

                    @pl.when(j == 0)
                    def _():
                        first_x[...] = moved

                    @pl.when(j > 0)
                    def _():
                        share_first(j).start()

            hidden = held[...].astype(jnp.float32)
            mean_sq = jnp.mean(hidden * hidden, axis=-1, keepdims=True)
            row = p * 4 + j // 2
            inputs = (
                hidden * lax.rsqrt(mean_sq + 1e-06) * gains_ref[0, row] + gains_ref[1, row]
            ).astype(jnp.bfloat16)
            chunk = 512
            for c in range(width // chunk):
                cols = pl.ds(c * chunk, chunk)
                mixed = jnp.dot(inputs, w_ref[:, cols], preferred_element_type=jnp.float32)
                sent[t, :, cols] = (
                    held[:, cols].astype(jnp.float32)
                    + gains_ref[2, row, :, cols] * jax.nn.gelu(mixed)
                ).astype(jnp.bfloat16)

            @pl.when(sec < 7)
            def _():
                pass_on(t, t, sec + 1).start()

            @pl.when(sec == 7)
            def _():
                if p == 0:
                    pass_on(t, t + mbs, 0).start()
                else:
                    pass_on(t, 2 * mbs, j).start()

            return carry

        lax.fori_loop(0, mbs, step, 0)

    run_pass(0)
    run_pass(1)
    pass_on(0, 2 * mbs, 0).wait_recv()

    @pl.when(sec > 0)
    def _():
        share_first(0).wait_recv()

    out_ref[sec] = (
        first_x[...].astype(jnp.float32)
        + delta_ref[4 + sec // 2][:, :1] * inbox[2 * mbs].astype(jnp.float32)
    ).astype(jnp.bfloat16)
    for ds in range(1, 8):
        share_out(sec, (sec + ds) % 8).start()

    def drain(t, carry):
        pass_on(t, t, 0).wait_send()
        return carry

    lax.fori_loop(0, 2 * mbs, drain, 0)

    @pl.when(sec == 0)
    def _():
        for j in range(1, 8):
            share_first(j).wait_send()

    for ds in range(1, 8):
        share_out((sec + ds) % 8, (sec + ds) % 8).wait_recv()
        share_out(sec, (sec + ds) % 8).wait_send()


def run_teacher(noise, weights, gains, delta):
    mbs, rows, width = noise.shape
    vmem = pl.BlockSpec(memory_space=pltpu.VMEM)
    return pl.pallas_call(
        teacher_kernel,
        out_shape=jax.ShapeDtypeStruct((mbs, rows, width), jnp.bfloat16),
        in_specs=[vmem] * 4,
        out_specs=vmem,
        scratch_shapes=[
            pltpu.VMEM((rows, width), jnp.bfloat16),
            pltpu.VMEM((2 * mbs, rows, width), jnp.bfloat16),
            pltpu.VMEM((2 * mbs + 1, rows, width), jnp.bfloat16),
            pltpu.VMEM((mbs, rows, width), jnp.bfloat16),
            pltpu.VMEM((rows, width), jnp.bfloat16),
            pltpu.SemaphoreType.DMA((2 * mbs + 1,)),
            pltpu.SemaphoreType.DMA((2 * mbs,)),
            pltpu.SemaphoreType.DMA((mbs,)),
            pltpu.SemaphoreType.DMA,
            pltpu.SemaphoreType.DMA((mbs,)),
            pltpu.SemaphoreType.DMA((mbs,)),
        ],
        compiler_params=pltpu.CompilerParams(
            collective_id=0, has_side_effects=True, vmem_limit_bytes=40 * 1024 * 1024
        ),
    )(noise, weights, gains, delta)


def local(
    noise,
    sched_index,
    text_ids,
    text_table,
    time_weight,
    block_weight,
    block_mod,
    student_weight,
    student_mod,
    feature_weight,
    lin_weight,
    token_weight,
):
    batches, tokens, model_width = noise.shape
    steps = sched_index.shape[1] - 1
    sections = lax.axis_size("section")
    own_section = lax.axis_index("section")
    vocab_rows = text_table.shape[0]
    offset = lax.axis_index(DP) * vocab_rows
    text_len = text_ids.shape[1]
    local_ids = text_ids - offset
    vocab_ids = jnp.arange(vocab_rows, dtype=jnp.int32)

    def add_group(group_id, counts):
        id_block = lax.dynamic_slice_in_dim(local_ids, group_id * 7, 7, 1)
        return counts + jnp.sum((id_block[:, :, None] == vocab_ids).astype(jnp.float32), axis=1)

    counts = lax.fori_loop(
        0,
        text_len // 7,
        add_group,
        jnp.zeros((batches * lax.axis_size(DP), vocab_rows), jnp.float32),
    )
    pooled = summed_on_arrival(
        jnp.dot(counts.astype(jnp.bfloat16), text_table, preferred_element_type=jnp.float32)
        / text_len,
        DP,
        0,
    )
    weights = lax.all_gather(block_weight, DP, axis=1, tiled=True)[0]
    section_mod = block_mod[0]
    indices_f = sched_index.astype(jnp.float32)
    half_freq = time_weight.shape[0] // 2
    frequency = jnp.exp(-math.log(10000.0) * jnp.arange(half_freq, dtype=jnp.float32) / half_freq)

    def conditions_of(pooled_in, indices_in):
        angles = indices_in[:, :, None] * frequency
        embedding = jnp.concatenate([jnp.cos(angles), jnp.sin(angles)], axis=-1)
        time_embed = jnp.dot(
            embedding.astype(jnp.bfloat16).reshape(-1, 2 * half_freq),
            time_weight,
            preferred_element_type=jnp.float32,
        )
        return jax.nn.silu(
            time_embed.reshape(batches, steps + 1, model_width) + pooled_in[:, None, :]
        )

    conditions = conditions_of(pooled, indices_f)
    deltas = (indices_f[:, 1:] - indices_f[:, :-1]) / LEVELS
    packed = jnp.concatenate(
        [pooled, jnp.pad(indices_f, ((0, 0), (0, 128 - steps - 1)))], axis=1
    )
    other = lax.ppermute(packed, "dp_x", [(0, 1), (1, 0)])
    odd = own_section % 2 == 1
    packed = jnp.where(odd, other, packed)
    pipe_cond = conditions_of(
        packed[:, :model_width], packed[:, model_width : model_width + steps + 1]
    )
    pipe_cond = jnp.moveaxis(pipe_cond[:, :steps], 1, 0).reshape(1, steps * batches, 1, model_width)
    ones = jnp.array([1.0, 0.0, 1.0], jnp.float32)[:, None, None, None]
    gains = ones + pipe_cond * section_mod[:, None, None, :]
    delta_lanes = jnp.broadcast_to(
        jnp.moveaxis(deltas, 1, 0).reshape(steps * batches, 1, 1), (steps * batches, 1, 128)
    )
    teacher = run_teacher(
        noise.reshape(sections, batches * tokens // sections, model_width),
        weights,
        gains,
        delta_lanes,
    ).reshape(noise.shape)
    col_count = student_weight.shape[1]
    first_col = own_section * col_count
    row_count = batches * tokens
    noise_f = noise.astype(jnp.float32)
    cond_zero = conditions[:, 0][:, None, :]
    time_zero = (indices_f[:, 0] / LEVELS)[:, None, None]
    inputs = (
        modulated(noise_f, cond_zero, student_mod)
        .astype(jnp.bfloat16)
        .reshape(row_count, model_width)
    )
    mixed = jnp.dot(inputs, collect(student_weight, DP, 0), preferred_element_type=jnp.float32)
    z_cols = lax.dynamic_slice_in_dim(noise_f, first_col, col_count, 2).reshape(
        row_count, col_count
    )
    gate_full = 1.0 + cond_zero * student_mod[2]
    gate_rows = jnp.broadcast_to(
        lax.dynamic_slice_in_dim(gate_full, first_col, col_count, 2), (batches, tokens, col_count)
    ).reshape(row_count, col_count)
    t_rows = jnp.broadcast_to(time_zero, (batches, tokens, 1)).reshape(row_count, 1)

    def advance(mixed_in):
        return z_cols - t_rows * (z_cols + gate_rows * jax.nn.gelu(mixed_in))

    moved, pull_back = jax.vjp(advance, mixed)
    feat_student = jnp.dot(
        moved.astype(jnp.bfloat16), feature_weight, preferred_element_type=jnp.float32
    )
    target_cols = lax.dynamic_slice_in_dim(teacher, first_col, col_count, 2).reshape(
        row_count, col_count
    )
    feat_teacher = jnp.dot(target_cols, feature_weight, preferred_element_type=jnp.float32)
    share_rows = row_count // sections
    part_student, part_teacher = side_by_side(
        (feat_student.astype(jnp.bfloat16), feat_teacher.astype(jnp.bfloat16)), "section", 0, 1
    )
    weight_share = lax.dynamic_slice_in_dim(token_weight, own_section * share_rows, share_rows, 0)

    def objective(feat_in):
        token_dist = distance(feat_in, part_teacher, lin_weight)
        return (jnp.sum(weight_share * token_dist), token_dist)

    total, pull_feat, token_distance = jax.vjp(objective, part_student, has_aux=True)
    grad_share = pull_feat(jnp.ones_like(total))[0].astype(jnp.bfloat16)
    grad_feat = collect(grad_share, "section", 0)
    out_grad = lax.dot_general(
        grad_feat, feature_weight, (((1,), (1,)), ((), ())), preferred_element_type=jnp.float32
    )
    mixed_grad = pull_back(out_grad)[0].astype(jnp.bfloat16)
    partial_grad = lax.dot_general(
        inputs, mixed_grad, (((0,), (0,)), ((), ())), preferred_element_type=jnp.float32
    )
    student_grad = sum_by_parts(partial_grad.astype(jnp.bfloat16), (("dp_x", "dp_z"), "dp_c"))
    return (teacher, student_grad, token_distance)


def solution(mesh):
    torus = Mesh(
        mesh.devices.reshape(2, 8, 2, mesh.shape["section"]), ("dp_x", "dp_z", "dp_c", "section")
    )
    in_specs = (
        P(DP, None, None),
        P(DP, None),
        P(),
        P(DP, None),
        P(),
        P("section", DP, None),
        P("section", None, None),
        P(DP, "section"),
        P(),
        P("section", None),
        P(),
        P(DP),
    )
    out_specs = (P(DP, None, None), P(None, "section"), P(DP_SECTION))
    return jax.shard_map(local, mesh=torus, in_specs=in_specs, out_specs=out_specs, check_vma=False)
```

```python
import math

import jax
import jax.numpy as jnp
from jax import lax
from jax.experimental import pallas as pl
from jax.experimental.pallas import tpu as pltpu
from jax.sharding import Mesh
from jax.sharding import PartitionSpec as P

LEVELS = 1000
DP = ("dp_x", "dp_z", "dp_c")
DP_SECTION = ("dp_x", "dp_z", "dp_c", "section")
MESH = pl.DeviceIdType.MESH


def in_blocks(x, dim, count):
    shape = x.shape
    blocks = x.reshape(*shape[:dim], count, shape[dim] // count, *shape[dim + 1 :])
    return jnp.moveaxis(blocks, dim, 0)


def summed_on_arrival(x, axis, dim):
    blocks = in_blocks(x, dim, lax.axis_size(axis))
    arrived = lax.all_to_all(blocks, axis, split_axis=0, concat_axis=0, tiled=True)
    return arrived.sum(axis=0)


def in_order(blocks, dim):
    blocks = jnp.moveaxis(blocks, 0, dim)
    shape = blocks.shape
    return blocks.reshape(*shape[:dim], shape[dim] * shape[dim + 1], *shape[dim + 2 :])


def from_everyone(x, axis):
    copies = jnp.broadcast_to(x, (lax.axis_size(axis), *x.shape))
    return lax.all_to_all(copies, axis, split_axis=0, concat_axis=0, tiled=True)


def collect(x, axis, dim):
    return in_order(from_everyone(x, axis), dim)


def modulated(hidden_f, cond_vec, gains):
    mean_sq = jnp.mean(hidden_f * hidden_f, axis=-1, keepdims=True)
    normed = hidden_f * lax.rsqrt(mean_sq + 1e-06)
    return normed * (1.0 + cond_vec * gains[0]) + cond_vec * gains[1]


def teacher_block(hidden, weight, gains, cond_vec):
    hidden_f = hidden.astype(jnp.float32)
    inputs = modulated(hidden_f, cond_vec, gains).astype(jnp.bfloat16)
    mixed = jnp.dot(inputs, weight, preferred_element_type=jnp.float32)
    return (hidden_f + (1.0 + cond_vec * gains[2]) * jax.nn.gelu(mixed)).astype(jnp.bfloat16)


def teacher_kernel(
    noise_ref,
    w_ref,
    gains_ref,
    delta_ref,
    out_ref,
    held,
    sent,
    inbox,
    start_x,
    first_x,
    inbox_recv,
    sent_send,
    first_send,
    first_recv,
    out_send,
    out_recv,
):
    mbs, rows, width = noise_ref.shape
    xl = lax.axis_index("dp_x")
    sec = lax.axis_index("section")
    barrier = pltpu.get_barrier_semaphore()
    for dx in range(2):
        for ds in range(8):
            if dx + ds > 0:
                pl.semaphore_signal(
                    barrier,
                    inc=1,
                    device_id={"dp_x": (xl + dx) % 2, "section": (sec + ds) % 8},
                    device_id_type=MESH,
                )
    pl.semaphore_wait(barrier, 15)

    def pass_on(t, slot, target):
        return pltpu.make_async_remote_copy(
            src_ref=sent.at[t],
            dst_ref=inbox.at[slot],
            send_sem=sent_send.at[t],
            recv_sem=inbox_recv.at[slot],
            device_id={"dp_x": 1 - xl, "section": target},
            device_id_type=MESH,
        )

    def share_first(j):
        return pltpu.make_async_remote_copy(
            src_ref=start_x.at[j],
            dst_ref=first_x,
            send_sem=first_send.at[j],
            recv_sem=first_recv,
            device_id={"section": j},
            device_id_type=MESH,
        )

    def share_out(slot, target):
        return pltpu.make_async_remote_copy(
            src_ref=out_ref.at[slot],
            dst_ref=out_ref.at[slot],
            send_sem=out_send.at[target],
            recv_sem=out_recv.at[slot],
            device_id={"section": target},
            device_id_type=MESH,
        )

    def run_pass(p):
        def step(j, carry):
            t = p * mbs + j
            if p == 0:

                @pl.when(sec == 0)
                def _():
                    held[...] = noise_ref[j]

            @pl.when((sec > 0) | (p > 0))
            def _():
                pass_on(t, t, 0).wait_recv()
                held[...] = inbox[t]

            if p > 0:

                @pl.when(sec == 0)
                def _():
                    moved = (
                        noise_ref[j].astype(jnp.float32)
                        + delta_ref[j // 2][:, :1] * held[...].astype(jnp.float32)
                    ).astype(jnp.bfloat16)
                    held[...] = moved
                    start_x[j] = moved

                    @pl.when(j == 0)
                    def _():
                        first_x[...] = moved

                    @pl.when(j > 0)
                    def _():
                        share_first(j).start()

            hidden = held[...].astype(jnp.float32)
            mean_sq = jnp.mean(hidden * hidden, axis=-1, keepdims=True)
            row = p * 4 + j // 2
            inputs = (
                hidden * lax.rsqrt(mean_sq + 1e-06) * gains_ref[0, row] + gains_ref[1, row]
            ).astype(jnp.bfloat16)
            chunk = 512
            for c in range(width // chunk):
                cols = pl.ds(c * chunk, chunk)
                mixed = jnp.dot(inputs, w_ref[:, cols], preferred_element_type=jnp.float32)
                sent[t, :, cols] = (
                    held[:, cols].astype(jnp.float32)
                    + gains_ref[2, row, :, cols] * jax.nn.gelu(mixed)
                ).astype(jnp.bfloat16)

            @pl.when(sec < 7)
            def _():
                pass_on(t, t, sec + 1).start()

            @pl.when(sec == 7)
            def _():
                if p == 0:
                    pass_on(t, t + mbs, 0).start()
                else:
                    pass_on(t, 2 * mbs, j).start()

            return carry

        lax.fori_loop(0, mbs, step, 0)

    run_pass(0)
    run_pass(1)
    pass_on(0, 2 * mbs, 0).wait_recv()

    @pl.when(sec > 0)
    def _():
        share_first(0).wait_recv()

    out_ref[sec] = (
        first_x[...].astype(jnp.float32)
        + delta_ref[4 + sec // 2][:, :1] * inbox[2 * mbs].astype(jnp.float32)
    ).astype(jnp.bfloat16)
    for ds in range(1, 8):
        share_out(sec, (sec + ds) % 8).start()

    def drain(t, carry):
        pass_on(t, t, 0).wait_send()
        return carry

    lax.fori_loop(0, 2 * mbs, drain, 0)

    @pl.when(sec == 0)
    def _():
        for j in range(1, 8):
            share_first(j).wait_send()

    for ds in range(1, 8):
        share_out((sec + ds) % 8, (sec + ds) % 8).wait_recv()
        share_out(sec, (sec + ds) % 8).wait_send()


def run_teacher(noise, weights, gains, delta):
    mbs, rows, width = noise.shape
    vmem = pl.BlockSpec(memory_space=pltpu.VMEM)
    return pl.pallas_call(
        teacher_kernel,
        out_shape=jax.ShapeDtypeStruct((mbs, rows, width), jnp.bfloat16),
        in_specs=[vmem] * 4,
        out_specs=vmem,
        scratch_shapes=[
            pltpu.VMEM((rows, width), jnp.bfloat16),
            pltpu.VMEM((2 * mbs, rows, width), jnp.bfloat16),
            pltpu.VMEM((2 * mbs + 1, rows, width), jnp.bfloat16),
            pltpu.VMEM((mbs, rows, width), jnp.bfloat16),
            pltpu.VMEM((rows, width), jnp.bfloat16),
            pltpu.SemaphoreType.DMA((2 * mbs + 1,)),
            pltpu.SemaphoreType.DMA((2 * mbs,)),
            pltpu.SemaphoreType.DMA((mbs,)),
            pltpu.SemaphoreType.DMA,
            pltpu.SemaphoreType.DMA((mbs,)),
            pltpu.SemaphoreType.DMA((mbs,)),
        ],
        compiler_params=pltpu.CompilerParams(
            collective_id=0, has_side_effects=True, vmem_limit_bytes=40 * 1024 * 1024
        ),
    )(noise, weights, gains, delta)


def loss_kernel(
    teacher_ref,
    feature_ref,
    own_feature_ref,
    student_part_ref,
    lin_ref,
    token_ref,
    inputs_ref,
    slope_ref,
    dist_ref,
    grad_ref,
    feats,
    grads,
    partial,
    half_out,
    half_in,
    summed,
    pieces,
    final,
    feat_send,
    feat_recv,
    grad_send,
    grad_recv,
    half_send,
    half_recv,
    piece_send,
    piece_recv,
    final_send,
    final_recv,
    twin_send,
    twin_recv,
):
    sections, rows, feat = student_part_ref.shape
    chips = summed.shape[0]
    piece = summed.shape[1]
    width = inputs_ref.shape[1]
    xl = lax.axis_index("dp_x")
    zz = lax.axis_index("dp_z")
    core = lax.axis_index("dp_c")
    sec = lax.axis_index("section")
    chip = xl * 8 + zz

    def at_section(k):
        return {"section": k}

    def at_chip(q):
        return {"dp_x": q // 8, "dp_z": q % 8}

    def at_twin():
        return {"dp_c": 1 - core}

    barrier = pltpu.get_barrier_semaphore()

    def greet(where):
        pl.semaphore_signal(barrier, inc=1, device_id=where, device_id_type=MESH)

    for k in range(1, sections):
        greet(at_section((sec + k) % sections))
    for k in range(1, chips):
        greet(at_chip((chip + k) % chips))
    greet(at_twin())
    pl.semaphore_wait(barrier, sections + chips - 1)

    def copy(src, dst, send, recv, where):
        return pltpu.make_async_remote_copy(
            src_ref=src,
            dst_ref=dst,
            send_sem=send,
            recv_sem=recv,
            device_id=where,
            device_id_type=MESH,
        )

    def send_feat(k, slot):
        return copy(
            student_part_ref.at[k], feats.at[slot], feat_send.at[k], feat_recv.at[slot], at_section(k)
        )

    def send_grad(k, slot):
        return copy(grads.at[slot], grads.at[slot], grad_send.at[k], grad_recv.at[slot], at_section(k))

    def send_piece(q, slot):
        return copy(summed.at[q], pieces.at[slot], piece_send.at[q], piece_recv.at[slot], at_chip(q))

    def send_final(q, slot):
        block = final.at[core, slot]
        return copy(block, block, final_send.at[q], final_recv.at[slot], at_chip(q))

    def send_twin(half, slot):
        block = final.at[half, slot]
        return copy(block, block, twin_send.at[slot], twin_recv.at[slot], at_twin())

    send_half = copy(half_out, half_in, half_send, half_recv, at_twin())

    for k in range(1, sections):
        send_feat((sec + k) % sections, sec).start()

    feat_teacher = jnp.dot(
        teacher_ref[sec], feature_ref[...], preferred_element_type=jnp.float32
    )
    feat_student = student_part_ref[sec].astype(jnp.float32)
    for k in range(1, sections):
        other = (sec + k) % sections
        send_feat(other, other).wait_recv()
        feat_student = feat_student + feats[other].astype(jnp.float32)

    def unit(f):
        positive = jnp.maximum(f, 0.0)
        scale = lax.rsqrt(jnp.mean(positive * positive, axis=-1, keepdims=True) + 1e-06)
        return positive * scale, scale

    unit_s, scale_s = unit(feat_student)
    unit_t, _ = unit(feat_teacher)
    gap = unit_s - unit_t
    lin = lin_ref[...]
    dist_ref[...] = jnp.sum(lin * gap * gap, axis=-1, keepdims=True)
    unit_grad = 2.0 * token_ref[...] * lin * gap
    mean_dot = jnp.mean(unit_grad * unit_s, axis=-1, keepdims=True)
    feat_grad = scale_s * (unit_grad - unit_s * mean_dot)
    grads[sec] = jnp.where(feat_student > 0.0, feat_grad, 0.0).astype(jnp.bfloat16)
    for k in range(1, sections):
        send_grad((sec + k) % sections, sec).start()
    for k in range(1, sections):
        other = (sec + k) % sections
        send_grad(other, other).wait_recv()

    out_grad = lax.dot_general(
        grads[...].reshape(sections * rows, feat),
        own_feature_ref[...],
        (((1,), (1,)), ((), ())),
        preferred_element_type=jnp.float32,
    )
    mixed_grad = (out_grad * slope_ref[...]).astype(jnp.bfloat16)
    half_rows = width // 2
    for half in range(2):
        partial[half] = lax.dot_general(
            inputs_ref[:, half * half_rows : (half + 1) * half_rows],
            mixed_grad,
            (((0,), (0,)), ((), ())),
            preferred_element_type=jnp.float32,
        ).reshape(chips, piece, -1)
    half_out[...] = partial[1 - core].astype(jnp.bfloat16)
    send_half.start()
    send_half.wait_recv()
    summed[...] = (partial[core] + half_in[...].astype(jnp.float32)).astype(jnp.bfloat16)
    for k in range(1, chips):
        send_piece((chip + k) % chips, chip).start()
    total = summed[chip].astype(jnp.float32)
    for k in range(1, chips):
        other = (chip + chips - k) % chips
        send_piece(other, other).wait_recv()
        total = total + pieces[other].astype(jnp.float32)
    final[core, chip] = total.astype(jnp.bfloat16)
    for k in range(1, chips):
        send_final((chip + k) % chips, chip).start()
    send_twin(core, chip).start()
    grad_ref[core, chip] = final[core, chip].astype(jnp.float32)
    for k in range(1, chips):
        other = (chip + chips - k) % chips
        send_final(other, other).wait_recv()
        send_twin(core, other).start()
        grad_ref[core, other] = final[core, other].astype(jnp.float32)
    for k in range(chips):
        other = (chip + chips - k) % chips
        send_twin(1 - core, other).wait_recv()
        grad_ref[1 - core, other] = final[1 - core, other].astype(jnp.float32)

    send_half.wait_send()
    for k in range(1, sections):
        send_feat((sec + k) % sections, sec).wait_send()
        send_grad((sec + k) % sections, sec).wait_send()
    for k in range(1, chips):
        send_piece((chip + k) % chips, chip).wait_send()
        send_final((chip + k) % chips, chip).wait_send()
    for k in range(chips):
        send_twin(core, k).wait_send()


def run_loss(teacher, feature, own_feature, student_part, lin, token, inputs, slope):
    sections, rows, feat = student_part.shape
    width = inputs.shape[1]
    cols = slope.shape[1]
    chips = 16
    piece = width // (2 * chips)
    vmem = pl.BlockSpec(memory_space=pltpu.VMEM)
    dma = pltpu.SemaphoreType.DMA
    bf16 = jnp.bfloat16
    dist, grad = pl.pallas_call(
        loss_kernel,
        out_shape=(
            jax.ShapeDtypeStruct((rows, 1), jnp.float32),
            jax.ShapeDtypeStruct((2, chips, piece, cols), jnp.float32),
        ),
        in_specs=[vmem] * 8,
        out_specs=(vmem, vmem),
        scratch_shapes=[
            pltpu.VMEM((sections, rows, feat), bf16),
            pltpu.VMEM((sections, rows, feat), bf16),
            pltpu.VMEM((2, chips, piece, cols), jnp.float32),
            pltpu.VMEM((chips, piece, cols), bf16),
            pltpu.VMEM((chips, piece, cols), bf16),
            pltpu.VMEM((chips, piece, cols), bf16),
            pltpu.VMEM((chips, piece, cols), bf16),
            pltpu.VMEM((2, chips, piece, cols), bf16),
            dma((sections,)),
            dma((sections,)),
            dma((sections,)),
            dma((sections,)),
            dma,
            dma,
            dma((chips,)),
            dma((chips,)),
            dma((chips,)),
            dma((chips,)),
            dma((chips,)),
            dma((chips,)),
        ],
        compiler_params=pltpu.CompilerParams(
            collective_id=1, has_side_effects=True, vmem_limit_bytes=40 * 1024 * 1024
        ),
    )(teacher, feature, own_feature, student_part, lin, token, inputs, slope)
    return dist.reshape(rows), grad.reshape(width, cols)


def local(
    noise,
    sched_index,
    text_ids,
    text_table,
    time_weight,
    block_weight,
    block_mod,
    student_weight,
    student_mod,
    feature_weight,
    lin_weight,
    token_weight,
):
    batches, tokens, model_width = noise.shape
    steps = sched_index.shape[1] - 1
    sections = lax.axis_size("section")
    own_section = lax.axis_index("section")
    vocab_rows = text_table.shape[0]
    offset = lax.axis_index(DP) * vocab_rows
    text_len = text_ids.shape[1]
    local_ids = text_ids - offset
    vocab_ids = jnp.arange(vocab_rows, dtype=jnp.int32)

    def add_group(group_id, counts):
        id_block = lax.dynamic_slice_in_dim(local_ids, group_id * 7, 7, 1)
        return counts + jnp.sum((id_block[:, :, None] == vocab_ids).astype(jnp.float32), axis=1)

    counts = lax.fori_loop(
        0,
        text_len // 7,
        add_group,
        jnp.zeros((batches * lax.axis_size(DP), vocab_rows), jnp.float32),
    )
    pooled = summed_on_arrival(
        jnp.dot(counts.astype(jnp.bfloat16), text_table, preferred_element_type=jnp.float32)
        / text_len,
        DP,
        0,
    )
    weights = lax.all_gather(block_weight, DP, axis=1, tiled=True)[0]
    section_mod = block_mod[0]
    indices_f = sched_index.astype(jnp.float32)
    half_freq = time_weight.shape[0] // 2
    frequency = jnp.exp(-math.log(10000.0) * jnp.arange(half_freq, dtype=jnp.float32) / half_freq)

    def conditions_of(pooled_in, indices_in):
        angles = indices_in[:, :, None] * frequency
        embedding = jnp.concatenate([jnp.cos(angles), jnp.sin(angles)], axis=-1)
        time_embed = jnp.dot(
            embedding.astype(jnp.bfloat16).reshape(-1, 2 * half_freq),
            time_weight,
            preferred_element_type=jnp.float32,
        )
        return jax.nn.silu(
            time_embed.reshape(batches, steps + 1, model_width) + pooled_in[:, None, :]
        )

    conditions = conditions_of(pooled, indices_f)
    deltas = (indices_f[:, 1:] - indices_f[:, :-1]) / LEVELS
    packed = jnp.concatenate(
        [pooled, jnp.pad(indices_f, ((0, 0), (0, 128 - steps - 1)))], axis=1
    )
    other = lax.ppermute(packed, "dp_x", [(0, 1), (1, 0)])
    odd = own_section % 2 == 1
    packed = jnp.where(odd, other, packed)
    pipe_cond = conditions_of(
        packed[:, :model_width], packed[:, model_width : model_width + steps + 1]
    )
    pipe_cond = jnp.moveaxis(pipe_cond[:, :steps], 1, 0).reshape(1, steps * batches, 1, model_width)
    ones = jnp.array([1.0, 0.0, 1.0], jnp.float32)[:, None, None, None]
    gains = ones + pipe_cond * section_mod[:, None, None, :]
    delta_lanes = jnp.broadcast_to(
        jnp.moveaxis(deltas, 1, 0).reshape(steps * batches, 1, 1), (steps * batches, 1, 128)
    )
    teacher_parts = run_teacher(
        noise.reshape(sections, batches * tokens // sections, model_width),
        weights,
        gains,
        delta_lanes,
    )
    teacher = teacher_parts.reshape(noise.shape)
    col_count = student_weight.shape[1]
    first_col = own_section * col_count
    row_count = batches * tokens
    noise_f = noise.astype(jnp.float32)
    cond_zero = conditions[:, 0][:, None, :]
    time_zero = (indices_f[:, 0] / LEVELS)[:, None, None]
    inputs = (
        modulated(noise_f, cond_zero, student_mod)
        .astype(jnp.bfloat16)
        .reshape(row_count, model_width)
    )
    mixed = jnp.dot(inputs, collect(student_weight, DP, 0), preferred_element_type=jnp.float32)
    z_cols = lax.dynamic_slice_in_dim(noise_f, first_col, col_count, 2).reshape(
        row_count, col_count
    )
    gate_full = 1.0 + cond_zero * student_mod[2]
    gate_rows = jnp.broadcast_to(
        lax.dynamic_slice_in_dim(gate_full, first_col, col_count, 2), (batches, tokens, col_count)
    ).reshape(row_count, col_count)
    t_rows = jnp.broadcast_to(time_zero, (batches, tokens, 1)).reshape(row_count, 1)

    def advance(mixed_in):
        return z_cols - t_rows * (z_cols + gate_rows * jax.nn.gelu(mixed_in))

    moved, pull_back = jax.vjp(advance, mixed)
    slope = pull_back(jnp.ones_like(moved))[0]
    feat_student = jnp.dot(
        moved.astype(jnp.bfloat16), feature_weight, preferred_element_type=jnp.float32
    )
    share_rows = row_count // sections
    weight_share = lax.dynamic_slice_in_dim(token_weight, own_section * share_rows, share_rows, 0)
    feature_full = lax.all_gather(feature_weight, "section", axis=0, tiled=True)
    token_distance, student_grad = run_loss(
        teacher_parts,
        feature_full,
        feature_weight,
        feat_student.astype(jnp.bfloat16).reshape(sections, share_rows, -1),
        lin_weight[None, :],
        weight_share[:, None],
        inputs,
        slope,
    )
    return (teacher, student_grad, token_distance)


def solution(mesh):
    torus = Mesh(
        mesh.devices.reshape(2, 8, 2, mesh.shape["section"]), ("dp_x", "dp_z", "dp_c", "section")
    )
    in_specs = (
        P(DP, None, None),
        P(DP, None),
        P(),
        P(DP, None),
        P(),
        P("section", DP, None),
        P("section", None, None),
        P(DP, "section"),
        P(),
        P("section", None),
        P(),
        P(DP),
    )
    out_specs = (P(DP, None, None), P(None, "section"), P(DP_SECTION))
    return jax.shard_map(local, mesh=torus, in_specs=in_specs, out_specs=out_specs, check_vma=False)
```

```python
import math

import jax
import jax.numpy as jnp
from jax import lax
from jax.experimental import pallas as pl
from jax.experimental.pallas import tpu as pltpu
from jax.sharding import Mesh
from jax.sharding import PartitionSpec as P

LEVELS = 1000
DP = ("dp_x", "dp_z", "dp_c")
SECTION = ("sec_y", "sec_x")
MESH = pl.DeviceIdType.MESH


def modulated(hidden_f, cond_vec, gains):
    mean_sq = jnp.mean(hidden_f * hidden_f, axis=-1, keepdims=True)
    normed = hidden_f * lax.rsqrt(mean_sq + 1e-06)
    return normed * (1.0 + cond_vec * gains[0]) + cond_vec * gains[1]


def teacher_kernel(
    noise_ref,
    ids_ref,
    sched_ref,
    frequency_ref,
    time_weight_ref,
    block_ref,
    block_mod_ref,
    student_shard_ref,
    feature_shard_ref,
    table_ref,
    x2_ref,
    cond_ref,
    student_ref,
    feature_ref,
    table,
    weight,
    mods,
    rows_out,
    rows_in,
    pooled,
    sched,
    cond,
    held,
    sent,
    inbox,
    start_x,
    first_x,
    table_sem,
    weight_send,
    weight_recv,
    row_send,
    row_recv,
    pooled_send,
    pooled_recv,
    sched_send,
    sched_recv,
    noise_send,
    inbox_recv,
    sent_send,
    first_send,
    first_recv,
    student_send,
    student_recv,
    feature_send,
    feature_recv,
    mods_send,
    mods_recv,
):
    mbs, rows, width = noise_ref.shape
    xl = lax.axis_index("dp_x")
    zz = lax.axis_index("dp_z")
    core = lax.axis_index("dp_c")
    sy = lax.axis_index("sec_y")
    sx = lax.axis_index("sec_x")
    sec = sy * 2 + sx
    dev = xl * 16 + zz * 2 + core
    twin = {"dp_c": 1 - core}

    def at_section(k):
        return {"sec_y": k // 2, "sec_x": k % 2}

    def at_dp(k):
        return {"dp_x": k // 16, "dp_z": (k // 2) % 8, "dp_c": k % 2}

    load_table = pltpu.make_async_copy(table_ref, table, table_sem)
    load_table.start()

    barrier = pltpu.get_barrier_semaphore()

    def greet(where):
        pl.semaphore_signal(barrier, inc=1, device_id=where, device_id_type=MESH)

    for k in range(1, 8):
        for dc in range(2):
            greet({**at_section((sec + k) % 8), "dp_c": (core + dc) % 2})
    for k in range(1, 32):
        greet(at_dp((dev + k) % 32))
    greet({"sec_x": 1 - sx, "dp_x": 1 - xl})
    pl.semaphore_wait(barrier, 46)

    def copy(src, dst, send, recv, where):
        return pltpu.make_async_remote_copy(
            src_ref=src,
            dst_ref=dst,
            send_sem=send,
            recv_sem=recv,
            device_id=where,
            device_id_type=MESH,
        )

    started = []

    def start(what, when=None):
        started.append((what, when))
        if when is None:
            what.start()
        else:
            pl.when(when)(what.start)

    source = sx == core
    relay = sx != core

    def piece_a(a, z):
        return a * 16 + (z % 8) * 2 + core

    def piece_b(a, z):
        return a * 16 + (z % 8) * 2 + 1 - core

    z_up = {"dp_z": (zz + 1) % 8}
    z_down = {"dp_z": (zz + 7) % 8}
    x_mate = {"dp_x": 1 - xl}
    x_outer = {"dp_x": 1 - xl, "sec_x": 1 - sx}
    way = {0: z_up, 1: z_down, 2: x_mate, 3: x_outer}

    def go(p, towards, when=None):
        block = weight.at[p]
        start(
            copy(block, block, weight_send.at[p * 4 + towards], weight_recv.at[p], way[towards]),
            when,
        )

    def arrive(p):
        block = weight.at[p]
        copy(block, block, weight_send.at[p], weight_recv.at[p], twin).wait_recv()

    @pl.when(source)
    def _():
        weight[dev] = block_ref[...]
        mods[...] = block_mod_ref[...]

    lend_mods = copy(block_mod_ref, mods, mods_send, mods_recv, x_outer)
    start(lend_mods, source)

    start(copy(block_ref, weight.at[dev], weight_send.at[128], weight_recv.at[dev], twin), relay)
    go(piece_a(xl, zz), 2, source)
    go(piece_a(xl, zz), 3, source)

    sched[core] = sched_ref[...]
    start(copy(sched_ref, sched.at[core], sched_send, sched_recv, twin))
    first_chip = sy == 0
    first_stage = first_chip & (core == 0)
    lender = first_chip & (core == 1) & (sx == 1)

    for j in range(mbs):
        start(
            copy(noise_ref.at[j], inbox.at[j], noise_send.at[j], inbox_recv.at[j], twin), lender
        )

    @pl.when(first_stage & (sx == 0))
    def _():
        inbox[0:mbs] = noise_ref[...]

    for k in range(1, 4):
        start(
            copy(
                feature_shard_ref,
                feature_ref.at[sec],
                feature_send.at[k],
                feature_recv.at[sec],
                {"sec_y": (sy + k) % 4},
            )
        )
    feature_ref[sec] = feature_shard_ref[...]

    @pl.when(source)
    def _():
        arrive(piece_b(xl, zz))

    go(piece_b(xl, zz), 0, source)
    go(piece_b(xl, zz), 1, source)
    go(piece_b(xl, zz), 2, source)
    go(piece_b(xl, zz), 3, source)

    vocab = table.shape[0]
    local_ids = ids_ref[...]
    lanes = lax.broadcasted_iota(jnp.int32, (local_ids.shape[0], vocab), 1)
    counts = jnp.zeros(lanes.shape, jnp.float32)
    for t in range(local_ids.shape[1]):
        counts = counts + jnp.where(local_ids[:, t : t + 1] == lanes, 1.0, 0.0)
    load_table.wait()
    part = jnp.dot(
        counts.astype(jnp.bfloat16), table[...], preferred_element_type=jnp.float32
    ) / local_ids.shape[1]
    for g in range(16):
        rows_out[g] = part[g : g + 1]
    rows_in[dev] = rows_out[dev // 2]
    for k in range(1, 32):
        other = (dev + k) % 32
        start(
            copy(
                rows_out.at[other // 2],
                rows_in.at[dev],
                row_send.at[k],
                row_recv.at[dev],
                at_dp(other),
            )
        )

    arrive_a = piece_a(1 - xl, zz)
    arrive(arrive_a)
    go(arrive_a, 2, relay)

    @pl.when(relay)
    def _():
        arrive(piece_a(xl, zz))

    for a in range(2):
        go(piece_a(a, zz), 0)
        go(piece_a(a, zz), 1)

    def take_x(z):
        p = piece_b(1 - xl, z)
        arrive(p)
        odd = z % 2
        go(p, 3, source & (odd == 1))
        go(p, 2, relay & (odd == 0))

    def take_z_b(k, up):
        z = zz + 8 - k if up else zz + k
        p = piece_b(xl, z)
        last = k == 4
        here = source & (xl == (0 if up else 1)) if last else source

        @pl.when(here)
        def _():
            arrive(p)

        if k < 3:
            go(p, 0 if up else 1, here)
        elif k == 3:
            go(p, 0 if up else 1, source & (xl == (0 if up else 1)))
        go(p, 2, here)
        go(p, 3, here)

    def take_z_a(k, up):
        z = zz + 8 - k if up else zz + k
        for a in range(2):
            reach = (4 - a) if up else (3 + a)
            if k <= reach:
                p = piece_a(a, z)
                arrive(p)
                if k < reach:
                    go(p, 0 if up else 1)

    def ring_step(k):
        for up in (True, False):
            take_z_b(k, up)
        for up in (True, False):
            take_z_a(k, up)
        if k == 1:
            take_x(zz)
        else:
            take_x(zz + 9 - k)
            take_x(zz + k - 1)

    ring_step(1)

    total = rows_in[dev]
    for k in range(1, 32):
        other = (dev + 32 - k) % 32
        copy(
            rows_out.at[0], rows_in.at[other], row_send.at[k], row_recv.at[other], at_dp(other)
        ).wait_recv()
        total = total + rows_in[other]
    pooled[sec] = total
    for k in range(1, 8):
        start(
            copy(
                pooled.at[sec],
                pooled.at[sec],
                pooled_send.at[k],
                pooled_recv.at[sec],
                at_section((sec + k) % 8),
            )
        )
    ring_step(2)
    copy(sched_ref, sched.at[1 - core], sched_send, sched_recv, twin).wait_recv()
    for k in range(1, 8):
        other = (sec + k) % 8
        copy(
            pooled.at[other],
            pooled.at[other],
            pooled_send.at[k],
            pooled_recv.at[other],
            at_section(other),
        ).wait_recv()
    for c in range(2):
        angles = sched[c, 0] * frequency_ref[...]
        embedding = jnp.concatenate([jnp.cos(angles), jnp.sin(angles)], axis=-1)
        embed = jnp.dot(
            embedding.astype(jnp.bfloat16), time_weight_ref[...], preferred_element_type=jnp.float32
        )
        for r in range(8):
            cond[c, r] = jax.nn.silu(embed[r : r + 1] + pooled[c * 4 + r % 4])
    cond_ref[...] = cond[core]
    ring_step(3)
    ring_step(4)
    take_x(zz + 4)

    @pl.when(relay)
    def _():
        for z in range(8):
            arrive(piece_b(xl, z))

    student_ref[dev] = student_shard_ref[...]
    for k in range(1, 16):
        start(
            copy(
                student_shard_ref,
                student_ref.at[dev],
                student_send.at[k],
                student_recv.at[dev],
                at_dp((dev + 2 * k) % 32),
            )
        )
    for k in range(4):
        slot = ((sy + k) % 4) * 2 + sx
        block = feature_ref.at[slot]
        across = copy(
            block, block, feature_send.at[4 + k], feature_recv.at[slot], {"sec_x": 1 - sx}
        )
        if k > 0:
            across.wait_recv()
        start(across)

    pl.when(relay)(lend_mods.wait_recv)

    def pass_on(t, slot, where):
        return copy(sent.at[t], inbox.at[slot], sent_send.at[t], inbox_recv.at[slot], where)

    def share_first(j):
        return copy(
            start_x.at[j], first_x, first_send.at[j], first_recv, {**at_section(j), "dp_c": sx}
        )

    def run_pass(p):
        def step(j, carry):
            t = p * mbs + j
            arrived = pass_on(t, t, twin)
            if p == 0:

                @pl.when(jnp.logical_not(first_stage & (sx == 0)))
                def _():
                    arrived.wait_recv()

            else:
                arrived.wait_recv()
            held[...] = inbox[t]

            if p > 0:

                @pl.when(first_stage)
                def _():
                    moved = (
                        inbox[j].astype(jnp.float32)
                        + sched[sx, 1, pl.ds(j // 2, 1), :1] * held[...].astype(jnp.float32)
                    ).astype(jnp.bfloat16)
                    held[...] = moved
                    start_x[j] = moved

                    @pl.when((j == 0) & (sx == 0))
                    def _():
                        first_x[...] = moved

                    @pl.when((j > 0) | (sx > 0))
                    def _():
                        share_first(j).start()

            hidden = held[...].astype(jnp.float32)
            mean_sq = jnp.mean(hidden * hidden, axis=-1, keepdims=True)
            cond_row = cond[sx, p * 4 + j // 2]
            inputs = (
                hidden * lax.rsqrt(mean_sq + 1e-06) * (1.0 + cond_row * mods[0:1])
                + cond_row * mods[1:2]
            ).astype(jnp.bfloat16)
            gate = 1.0 + cond_row * mods[2:3]
            chunk = 512
            for c in range(width // chunk):
                cols = slice(c * chunk, (c + 1) * chunk)
                mixed = jnp.dot(
                    inputs,
                    weight[:, :, cols].reshape(width, chunk),
                    preferred_element_type=jnp.float32,
                )
                sent[t, :, cols] = (
                    hidden[:, cols] + gate[:, cols] * jax.nn.gelu(mixed)
                ).astype(jnp.bfloat16)

            @pl.when(core == 0)
            def _():
                pass_on(t, t, twin).start()

            @pl.when((core == 1) & (sy < 3))
            def _():
                pass_on(t, t, {"dp_c": 0, "sec_y": (sy + 1) % 4}).start()

            @pl.when((core == 1) & (sy == 3))
            def _():
                if p == 0:
                    pass_on(t, t + mbs, {"dp_c": 0, "sec_y": 0}).start()
                else:

                    @pl.when((sx == 1) & (j == mbs - 1))
                    def _():
                        inbox[2 * mbs] = sent[t]

                    @pl.when((sx == 0) | (j < mbs - 1))
                    def _():
                        pass_on(t, 2 * mbs, {**at_section(j), "dp_c": sx}).start()

            return carry

        lax.fori_loop(0, mbs, step, 0)

    run_pass(0)
    for k in range(16):
        slot = (dev + 2 * k) % 32
        block = student_ref.at[slot]
        to_twin = copy(block, block, student_send.at[16 + k], student_recv.at[slot], twin)
        if k > 0:
            to_twin.wait_recv()
        start(to_twin)
    run_pass(1)

    last_self = (core == 1) & (sec == 7)
    first_self = (core == 0) & (sec == 0)

    @pl.when(jnp.logical_not(last_self))
    def _():
        pass_on(0, 2 * mbs, twin).wait_recv()

    @pl.when(jnp.logical_not(first_self))
    def _():
        share_first(0).wait_recv()

    x2_ref[...] = (
        first_x[...].astype(jnp.float32)
        + sched[core, 1, pl.ds(4 + sec // 2, 1), :1] * inbox[2 * mbs].astype(jnp.float32)
    ).astype(jnp.bfloat16)

    def drain(t, carry):
        pass_on(t, t, twin).wait_send()
        return carry

    lax.fori_loop(0, 2 * mbs - 1, drain, 0)

    @pl.when(jnp.logical_not(last_self))
    def _():
        pass_on(2 * mbs - 1, 0, twin).wait_send()

    @pl.when(first_stage)
    def _():
        for j in range(1, mbs):
            share_first(j).wait_send()

        @pl.when(sx > 0)
        def _():
            share_first(0).wait_send()

    for k in range(16):
        slot = (dev + 2 * k) % 32 + 1 - 2 * core
        block = student_ref.at[slot]
        copy(block, block, student_send.at[0], student_recv.at[slot], twin).wait_recv()
    for k in range(4):
        slot = ((sy + k) % 4) * 2 + 1 - sx
        block = feature_ref.at[slot]
        copy(block, block, feature_send.at[0], feature_recv.at[slot], twin).wait_recv()
    for what, when in started:
        if when is None:
            what.wait_send()
        else:
            pl.when(when)(what.wait_send)


def run_teacher(
    noise, ids, sched, frequency, time_weight, block, block_mod, student_shard, feature_shard, table
):
    mbs, rows, width = noise.shape
    vocab = table.shape[0]
    piece = block.shape[0]
    cols = student_shard.shape[1]
    feat_rows, feat = feature_shard.shape
    vmem = pl.BlockSpec(memory_space=pltpu.VMEM)
    dma = pltpu.SemaphoreType.DMA
    bf16 = jnp.bfloat16
    f32 = jnp.float32
    return pl.pallas_call(
        teacher_kernel,
        out_shape=(
            jax.ShapeDtypeStruct((rows, width), bf16),
            jax.ShapeDtypeStruct((8, 1, width), f32),
            jax.ShapeDtypeStruct((32, piece, cols), bf16),
            jax.ShapeDtypeStruct((8, feat_rows, feat), bf16),
        ),
        in_specs=[vmem] * 9 + [pl.BlockSpec(memory_space=pl.ANY)],
        out_specs=(vmem,) * 4,
        scratch_shapes=[
            pltpu.VMEM((vocab, width), bf16),
            pltpu.VMEM((32, piece, width), bf16),
            pltpu.VMEM((3, width), f32),
            pltpu.VMEM((16, 1, width), f32),
            pltpu.VMEM((32, 1, width), f32),
            pltpu.VMEM((8, 1, width), f32),
            pltpu.VMEM((2, 2, 8, 128), f32),
            pltpu.VMEM((2, 8, 1, width), f32),
            pltpu.VMEM((rows, width), bf16),
            pltpu.VMEM((2 * mbs, rows, width), bf16),
            pltpu.VMEM((2 * mbs + 1, rows, width), bf16),
            pltpu.VMEM((mbs, rows, width), bf16),
            pltpu.VMEM((rows, width), bf16),
            dma,
            dma((129,)),
            dma((32,)),
            dma((32,)),
            dma((32,)),
            dma((8,)),
            dma((8,)),
            dma,
            dma,
            dma((mbs,)),
            dma((2 * mbs + 1,)),
            dma((2 * mbs,)),
            dma((mbs,)),
            dma,
            dma((32,)),
            dma((32,)),
            dma((8,)),
            dma((8,)),
            dma,
            dma,
        ],
        compiler_params=pltpu.CompilerParams(
            collective_id=0, has_side_effects=True, vmem_limit_bytes=48 * 1024 * 1024
        ),
    )(noise, ids, sched, frequency, time_weight, block, block_mod, student_shard, feature_shard, table)


def loss_kernel(
    x2_ref,
    feature_ref,
    student_part_ref,
    lin_ref,
    token_ref,
    inputs_ref,
    slope_ref,
    teacher_ref,
    dist_ref,
    grad_ref,
    feats,
    grads,
    partial,
    half_out,
    half_in,
    summed,
    pieces,
    final,
    feat_send,
    feat_recv,
    grad_send,
    grad_recv,
    half_send,
    half_recv,
    piece_send,
    piece_recv,
    final_send,
    final_recv,
    twin_send,
    twin_recv,
    out_send,
    out_recv,
):
    sections, rows, feat = student_part_ref.shape
    chips = summed.shape[0]
    piece = summed.shape[1]
    width = inputs_ref.shape[1]
    xl = lax.axis_index("dp_x")
    zz = lax.axis_index("dp_z")
    core = lax.axis_index("dp_c")
    sec = lax.axis_index(SECTION)
    chip = xl * 8 + zz

    def at_section(k):
        return {"sec_y": k // 2, "sec_x": k % 2}

    def at_chip(q):
        return {"dp_x": q // 8, "dp_z": q % 8}

    def at_twin():
        return {"dp_c": 1 - core}

    barrier = pltpu.get_barrier_semaphore()

    def greet(where):
        pl.semaphore_signal(barrier, inc=1, device_id=where, device_id_type=MESH)

    for k in range(1, sections):
        greet(at_section((sec + k) % sections))
    for k in range(1, chips):
        greet(at_chip((chip + k) % chips))
    greet(at_twin())
    pl.semaphore_wait(barrier, sections + chips - 1)

    def copy(src, dst, send, recv, where):
        return pltpu.make_async_remote_copy(
            src_ref=src,
            dst_ref=dst,
            send_sem=send,
            recv_sem=recv,
            device_id=where,
            device_id_type=MESH,
        )

    def send_feat(k, slot):
        return copy(
            student_part_ref.at[k], feats.at[slot], feat_send.at[k], feat_recv.at[slot], at_section(k)
        )

    def send_grad(k, slot):
        return copy(grads.at[slot], grads.at[slot], grad_send.at[k], grad_recv.at[slot], at_section(k))

    def send_piece(q, slot):
        return copy(summed.at[q], pieces.at[slot], piece_send.at[q], piece_recv.at[slot], at_chip(q))

    def send_final(q, slot):
        block = final.at[core, slot]
        return copy(block, block, final_send.at[q], final_recv.at[slot], at_chip(q))

    def send_twin(half, slot):
        block = final.at[half, slot]
        return copy(block, block, twin_send.at[slot], twin_recv.at[slot], at_twin())

    send_half = copy(half_out, half_in, half_send, half_recv, at_twin())

    def send_out(k, slot):
        return copy(x2_ref, teacher_ref.at[slot], out_send.at[k], out_recv.at[slot], at_section(k))

    for k in range(1, sections):
        send_feat((sec + k) % sections, sec).start()
    for k in range(1, sections):
        send_out((sec + k) % sections, sec).start()
    teacher_ref[sec] = x2_ref[...]

    feat_teacher = jnp.dot(
        x2_ref[...], feature_ref[...].reshape(width, feat), preferred_element_type=jnp.float32
    )
    feat_student = student_part_ref[sec].astype(jnp.float32)
    for k in range(1, sections):
        other = (sec + k) % sections
        send_feat(other, other).wait_recv()
        feat_student = feat_student + feats[other].astype(jnp.float32)

    def unit(f):
        positive = jnp.maximum(f, 0.0)
        scale = lax.rsqrt(jnp.mean(positive * positive, axis=-1, keepdims=True) + 1e-06)
        return positive * scale, scale

    unit_s, scale_s = unit(feat_student)
    unit_t, _ = unit(feat_teacher)
    gap = unit_s - unit_t
    lin = lin_ref[...]
    dist_ref[...] = jnp.sum(lin * gap * gap, axis=-1, keepdims=True)
    unit_grad = 2.0 * token_ref[...] * lin * gap
    mean_dot = jnp.mean(unit_grad * unit_s, axis=-1, keepdims=True)
    feat_grad = scale_s * (unit_grad - unit_s * mean_dot)
    grads[sec] = jnp.where(feat_student > 0.0, feat_grad, 0.0).astype(jnp.bfloat16)
    for k in range(1, sections):
        send_grad((sec + k) % sections, sec).start()
    for k in range(1, sections):
        other = (sec + k) % sections
        send_grad(other, other).wait_recv()

    out_grad = lax.dot_general(
        grads[...].reshape(sections * rows, feat),
        feature_ref[sec],
        (((1,), (1,)), ((), ())),
        preferred_element_type=jnp.float32,
    )
    mixed_grad = (out_grad * slope_ref[...]).astype(jnp.bfloat16)
    half_rows = width // 2
    for half in range(2):
        partial[half] = lax.dot_general(
            inputs_ref[:, half * half_rows : (half + 1) * half_rows],
            mixed_grad,
            (((0,), (0,)), ((), ())),
            preferred_element_type=jnp.float32,
        ).reshape(chips, piece, -1)
    half_out[...] = partial[1 - core].astype(jnp.bfloat16)
    send_half.start()
    send_half.wait_recv()
    summed[...] = (partial[core] + half_in[...].astype(jnp.float32)).astype(jnp.bfloat16)
    for k in range(1, chips):
        send_piece((chip + k) % chips, chip).start()
    total = summed[chip].astype(jnp.float32)
    for k in range(1, chips):
        other = (chip + chips - k) % chips
        send_piece(other, other).wait_recv()
        total = total + pieces[other].astype(jnp.float32)
    final[core, chip] = total.astype(jnp.bfloat16)
    for k in range(1, chips):
        send_final((chip + k) % chips, chip).start()
    send_twin(core, chip).start()
    grad_ref[core, chip] = final[core, chip].astype(jnp.float32)
    for k in range(1, chips):
        other = (chip + chips - k) % chips
        send_final(other, other).wait_recv()
        send_twin(core, other).start()
        grad_ref[core, other] = final[core, other].astype(jnp.float32)
    for k in range(chips):
        other = (chip + chips - k) % chips
        send_twin(1 - core, other).wait_recv()
        grad_ref[1 - core, other] = final[1 - core, other].astype(jnp.float32)

    for k in range(1, sections):
        other = (sec + k) % sections
        send_out(other, other).wait_recv()
        send_out(other, sec).wait_send()
    send_half.wait_send()
    for k in range(1, sections):
        send_feat((sec + k) % sections, sec).wait_send()
        send_grad((sec + k) % sections, sec).wait_send()
    for k in range(1, chips):
        send_piece((chip + k) % chips, chip).wait_send()
        send_final((chip + k) % chips, chip).wait_send()
    for k in range(chips):
        send_twin(core, k).wait_send()


def run_loss(x2, feature, student_part, lin, token, inputs, slope):
    sections, rows, feat = student_part.shape
    width = inputs.shape[1]
    cols = slope.shape[1]
    chips = 16
    piece = width // (2 * chips)
    vmem = pl.BlockSpec(memory_space=pltpu.VMEM)
    dma = pltpu.SemaphoreType.DMA
    bf16 = jnp.bfloat16
    teacher, dist, grad = pl.pallas_call(
        loss_kernel,
        out_shape=(
            jax.ShapeDtypeStruct((sections, rows, width), bf16),
            jax.ShapeDtypeStruct((rows, 1), jnp.float32),
            jax.ShapeDtypeStruct((2, chips, piece, cols), jnp.float32),
        ),
        in_specs=[vmem] * 7,
        out_specs=(vmem, vmem, vmem),
        scratch_shapes=[
            pltpu.VMEM((sections, rows, feat), bf16),
            pltpu.VMEM((sections, rows, feat), bf16),
            pltpu.VMEM((2, chips, piece, cols), jnp.float32),
            pltpu.VMEM((chips, piece, cols), bf16),
            pltpu.VMEM((chips, piece, cols), bf16),
            pltpu.VMEM((chips, piece, cols), bf16),
            pltpu.VMEM((chips, piece, cols), bf16),
            pltpu.VMEM((2, chips, piece, cols), bf16),
            dma((sections,)),
            dma((sections,)),
            dma((sections,)),
            dma((sections,)),
            dma,
            dma,
            dma((chips,)),
            dma((chips,)),
            dma((chips,)),
            dma((chips,)),
            dma((chips,)),
            dma((chips,)),
            dma((sections,)),
            dma((sections,)),
        ],
        compiler_params=pltpu.CompilerParams(
            collective_id=1, has_side_effects=True, vmem_limit_bytes=40 * 1024 * 1024
        ),
    )(x2, feature, student_part, lin, token, inputs, slope)
    return teacher, dist.reshape(rows), grad.reshape(width, cols)


def local(
    noise,
    sched_index,
    text_ids,
    text_table,
    time_weight,
    block_weight,
    block_mod,
    student_weight,
    student_mod,
    feature_weight,
    lin_weight,
    token_weight,
):
    batches, tokens, model_width = noise.shape
    sections = lax.axis_size(SECTION)
    own_section = lax.axis_index(SECTION)
    row_count = batches * tokens
    share_rows = row_count // sections
    vocab_rows = text_table.shape[0]
    offset = lax.axis_index(DP) * vocab_rows
    ids = lax.dynamic_index_in_dim(
        text_ids.reshape(16, 8, -1), own_section, 1, keepdims=False
    ) - offset
    indices_f = sched_index.astype(jnp.float32)
    half_freq = time_weight.shape[0] // 2
    frequency = jnp.exp(-math.log(10000.0) * jnp.arange(half_freq, dtype=jnp.float32) / half_freq)
    deltas = (indices_f[:, 1:] - indices_f[:, :-1]) / LEVELS
    sched = jnp.broadcast_to(
        jnp.stack([indices_f[:, :2].T.reshape(8), deltas.T.reshape(8)])[:, :, None], (2, 8, 128)
    )
    x2, cond, student_full, feature_full = run_teacher(
        noise.reshape(sections, share_rows, model_width),
        ids,
        sched,
        frequency[None, :],
        time_weight,
        block_weight[0],
        block_mod[0],
        student_weight,
        feature_weight,
        text_table,
    )
    col_count = student_weight.shape[1]
    first_col = own_section * col_count
    noise_f = noise.astype(jnp.float32)
    cond_zero = cond[:batches]
    time_zero = (indices_f[:, 0] / LEVELS)[:, None, None]
    inputs = (
        modulated(noise_f, cond_zero, student_mod)
        .astype(jnp.bfloat16)
        .reshape(row_count, model_width)
    )
    mixed = jnp.dot(
        inputs, student_full.reshape(model_width, col_count), preferred_element_type=jnp.float32
    )
    z_cols = lax.dynamic_slice_in_dim(noise_f, first_col, col_count, 2).reshape(
        row_count, col_count
    )
    gate_full = 1.0 + cond_zero * student_mod[2]
    gate_rows = jnp.broadcast_to(
        lax.dynamic_slice_in_dim(gate_full, first_col, col_count, 2), (batches, tokens, col_count)
    ).reshape(row_count, col_count)
    t_rows = jnp.broadcast_to(time_zero, (batches, tokens, 1)).reshape(row_count, 1)

    def advance(mixed_in):
        return z_cols - t_rows * (z_cols + gate_rows * jax.nn.gelu(mixed_in))

    moved, pull_back = jax.vjp(advance, mixed)
    slope = pull_back(jnp.ones_like(moved))[0]
    feat_student = jnp.dot(
        moved.astype(jnp.bfloat16), feature_weight, preferred_element_type=jnp.float32
    )
    weight_share = lax.dynamic_slice_in_dim(token_weight, own_section * share_rows, share_rows, 0)
    teacher, token_distance, student_grad = run_loss(
        x2,
        feature_full,
        feat_student.astype(jnp.bfloat16).reshape(sections, share_rows, -1),
        lin_weight[None, :],
        weight_share[:, None],
        inputs,
        slope,
    )
    return (teacher.reshape(noise.shape), student_grad, token_distance)


def solution(mesh):
    torus = Mesh(mesh.devices.reshape(2, 8, 2, 4, 2), DP + SECTION)
    in_specs = (
        P(DP, None, None),
        P(DP, None),
        P(),
        P(DP, None),
        P(),
        P(SECTION, DP, None),
        P(SECTION, None, None),
        P(DP, SECTION),
        P(),
        P(SECTION, None),
        P(),
        P(DP),
    )
    out_specs = (P(DP, None, None), P(None, SECTION), P(DP + SECTION))
    return jax.shard_map(local, mesh=torus, in_specs=in_specs, out_specs=out_specs, check_vma=False)
```

```python
import math

import jax
import jax.numpy as jnp
from jax import lax
from jax.experimental import pallas as pl
from jax.experimental.pallas import tpu as pltpu
from jax.sharding import Mesh
from jax.sharding import PartitionSpec as P

LEVELS = 1000
DP = ("dp_x", "dp_z", "dp_c")
SECTION = ("sec_y", "sec_x")
MESH = pl.DeviceIdType.MESH


def train_kernel(
    noise_ref,
    ids_ref,
    sched_ref,
    frequency_ref,
    time_weight_ref,
    block_ref,
    block_mod_ref,
    student_shard_ref,
    feature_shard_ref,
    student_mod_ref,
    lin_ref,
    token_ref,
    table_ref,
    teacher_ref,
    dist_ref,
    grad_ref,
    table,
    weight,
    mods,
    rows_out,
    rows_in,
    pooled,
    sched,
    cond,
    held,
    sent,
    inbox,
    start_x,
    first_x,
    student_ref,
    feature_ref,
    student_t,
    slope,
    feat_part,
    feats,
    grads,
    partial,
    half_out,
    half_in,
    summed,
    pieces,
    final,
    table_sem,
    weight_send,
    weight_recv,
    row_send,
    row_recv,
    pooled_send,
    pooled_recv,
    sched_send,
    sched_recv,
    noise_send,
    inbox_recv,
    sent_send,
    first_send,
    first_recv,
    student_send,
    student_recv,
    feature_send,
    feature_recv,
    mods_send,
    mods_recv,
    feat_send,
    feat_recv,
    grad_send,
    grad_recv,
    half_send,
    half_recv,
    piece_send,
    piece_recv,
    final_send,
    final_recv,
    twin_send,
    twin_recv,
    out_send,
    out_recv,
):
    mbs, rows, width = noise_ref.shape
    chunk = 512
    chunks = width // chunk
    xl = lax.axis_index("dp_x")
    zz = lax.axis_index("dp_z")
    core = lax.axis_index("dp_c")
    sy = lax.axis_index("sec_y")
    sx = lax.axis_index("sec_x")
    sec = sy * 2 + sx
    dev = xl * 16 + zz * 2 + core
    twin = {"dp_c": 1 - core}

    def at_section(k):
        return {"sec_y": k // 2, "sec_x": k % 2}

    def at_dp(k):
        return {"dp_x": k // 16, "dp_z": (k // 2) % 8, "dp_c": k % 2}

    load_table = pltpu.make_async_copy(table_ref, table, table_sem)
    load_table.start()

    barrier = pltpu.get_barrier_semaphore()

    def greet(where):
        pl.semaphore_signal(barrier, inc=1, device_id=where, device_id_type=MESH)

    for k in range(1, 8):
        for dc in range(2):
            greet({**at_section((sec + k) % 8), "dp_c": (core + dc) % 2})
    for k in range(1, 32):
        greet(at_dp((dev + k) % 32))
    greet({"sec_x": 1 - sx, "dp_x": 1 - xl})
    pl.semaphore_wait(barrier, 46)

    def copy(src, dst, send, recv, where):
        return pltpu.make_async_remote_copy(
            src_ref=src,
            dst_ref=dst,
            send_sem=send,
            recv_sem=recv,
            device_id=where,
            device_id_type=MESH,
        )

    started = []

    def start(what, when=None):
        started.append((what, when))
        if when is None:
            what.start()
        else:
            pl.when(when)(what.start)

    source = sx == core
    relay = sx != core

    def piece_a(a, z):
        return a * 16 + (z % 8) * 2 + core

    def piece_b(a, z):
        return a * 16 + (z % 8) * 2 + 1 - core

    z_up = {"dp_z": (zz + 1) % 8}
    z_down = {"dp_z": (zz + 7) % 8}
    x_mate = {"dp_x": 1 - xl}
    x_outer = {"dp_x": 1 - xl, "sec_x": 1 - sx}
    way = {0: z_up, 1: z_down, 2: x_mate, 3: x_outer}

    def go(p, towards, when=None):
        block = weight.at[p]
        start(
            copy(block, block, weight_send.at[p * 4 + towards], weight_recv.at[p], way[towards]),
            when,
        )

    def arrive(p):
        block = weight.at[p]
        copy(block, block, weight_send.at[p], weight_recv.at[p], twin).wait_recv()

    @pl.when(source)
    def _():
        weight[dev] = block_ref[...]
        mods[...] = block_mod_ref[...]

    lend_mods = copy(block_mod_ref, mods, mods_send, mods_recv, x_outer)
    start(lend_mods, source)

    start(copy(block_ref, weight.at[dev], weight_send.at[dev * 4], weight_recv.at[dev], twin), relay)
    go(piece_a(xl, zz), 2, source)
    go(piece_a(xl, zz), 3, source)

    sched[core] = sched_ref[...]
    start(copy(sched_ref, sched.at[core], sched_send, sched_recv, twin))
    first_chip = sy == 0
    first_stage = first_chip & (core == 0)
    lender = first_chip & (core == 1) & (sx == 1)

    for j in range(mbs):
        for c in range(chunks):
            cols = slice(c * chunk, (c + 1) * chunk)
            start(
                copy(
                    noise_ref.at[j, :, cols],
                    inbox.at[j, :, cols],
                    noise_send.at[j * chunks + c],
                    inbox_recv.at[j * chunks + c],
                    twin,
                ),
                lender,
            )

    @pl.when(first_stage & (sx == 0))
    def _():
        inbox[0:mbs] = noise_ref[...]

    for k in range(1, 4):
        start(
            copy(
                feature_shard_ref,
                feature_ref.at[sec],
                feature_send.at[k],
                feature_recv.at[sec],
                {"sec_y": (sy + k) % 4},
            )
        )
    feature_ref[sec] = feature_shard_ref[...]

    @pl.when(source)
    def _():
        arrive(piece_b(xl, zz))

    go(piece_b(xl, zz), 0, source)
    go(piece_b(xl, zz), 1, source)
    go(piece_b(xl, zz), 2, source)
    go(piece_b(xl, zz), 3, source)

    vocab = table.shape[0]
    local_ids = ids_ref[...]
    lanes = lax.broadcasted_iota(jnp.int32, (local_ids.shape[0], vocab), 1)
    counts = jnp.zeros(lanes.shape, jnp.float32)
    for t in range(local_ids.shape[1]):
        counts = counts + jnp.where(local_ids[:, t : t + 1] == lanes, 1.0, 0.0)
    load_table.wait()
    part = jnp.dot(
        counts.astype(jnp.bfloat16), table[...], preferred_element_type=jnp.float32
    ) / local_ids.shape[1]
    for g in range(16):
        rows_out[g] = part[g : g + 1]
    rows_in[dev] = rows_out[dev // 2]
    for k in range(1, 32):
        other = (dev + k) % 32
        start(
            copy(
                rows_out.at[other // 2],
                rows_in.at[dev],
                row_send.at[k],
                row_recv.at[dev],
                at_dp(other),
            )
        )

    arrive_a = piece_a(1 - xl, zz)
    arrive(arrive_a)
    go(arrive_a, 2, relay)

    @pl.when(relay)
    def _():
        arrive(piece_a(xl, zz))

    for a in range(2):
        go(piece_a(a, zz), 0)
        go(piece_a(a, zz), 1)

    def take_x(z):
        p = piece_b(1 - xl, z)
        arrive(p)
        odd = z % 2
        go(p, 3, source & (odd == 1))
        go(p, 2, relay & (odd == 0))

    def take_z_b(k, up):
        z = zz + 8 - k if up else zz + k
        p = piece_b(xl, z)
        last = k == 4
        here = source & (xl == (0 if up else 1)) if last else source

        @pl.when(here)
        def _():
            arrive(p)

        if k < 3:
            go(p, 0 if up else 1, here)
        elif k == 3:
            go(p, 0 if up else 1, source & (xl == (0 if up else 1)))
        go(p, 2, here)
        go(p, 3, here)

    def take_z_a(k, up):
        z = zz + 8 - k if up else zz + k
        for a in range(2):
            reach = (4 - a) if up else (3 + a)
            if k <= reach:
                p = piece_a(a, z)
                arrive(p)
                if k < reach:
                    go(p, 0 if up else 1)

    def ring_step(k):
        for up in (True, False):
            take_z_b(k, up)
        for up in (True, False):
            take_z_a(k, up)
        if k == 1:
            take_x(zz)
        else:
            take_x(zz + 9 - k)
            take_x(zz + k - 1)

    ring_step(1)

    total = rows_in[dev]
    for k in range(1, 32):
        other = (dev + 32 - k) % 32
        copy(
            rows_out.at[0], rows_in.at[other], row_send.at[k], row_recv.at[other], at_dp(other)
        ).wait_recv()
        total = total + rows_in[other]
    pooled[sec] = total
    for k in range(1, 8):
        start(
            copy(
                pooled.at[sec],
                pooled.at[sec],
                pooled_send.at[k],
                pooled_recv.at[sec],
                at_section((sec + k) % 8),
            )
        )
    ring_step(2)
    copy(sched_ref, sched.at[1 - core], sched_send, sched_recv, twin).wait_recv()
    for k in range(1, 8):
        other = (sec + k) % 8
        copy(
            pooled.at[other],
            pooled.at[other],
            pooled_send.at[k],
            pooled_recv.at[other],
            at_section(other),
        ).wait_recv()
    for c in range(2):
        angles = sched[c, 0] * frequency_ref[...]
        embedding = jnp.concatenate([jnp.cos(angles), jnp.sin(angles)], axis=-1)
        embed = jnp.dot(
            embedding.astype(jnp.bfloat16), time_weight_ref[...], preferred_element_type=jnp.float32
        )
        for r in range(8):
            cond[c, r] = jax.nn.silu(embed[r : r + 1] + pooled[c * 4 + r % 4])
    ring_step(3)
    ring_step(4)
    take_x(zz + 4)

    @pl.when(relay)
    def _():
        for z in range(8):
            arrive(piece_b(xl, z))

    student_ref[dev] = student_shard_ref[...]
    for k in range(1, 16):
        start(
            copy(
                student_shard_ref,
                student_ref.at[dev],
                student_send.at[k],
                student_recv.at[dev],
                at_dp((dev + 2 * k) % 32),
            )
        )
    pl.when(relay)(lend_mods.wait_recv)

    def pass_on(t, slot, c, where):
        cols = pl.ds(c * chunk, chunk)
        return copy(
            sent.at[t, :, cols],
            inbox.at[slot, :, cols],
            sent_send.at[t * chunks + c],
            inbox_recv.at[slot * chunks + c],
            where,
        )

    def hop(t, p, j, c):
        @pl.when(core == 0)
        def _():
            pass_on(t, t, c, twin).start()

        @pl.when((core == 1) & (sy < 3))
        def _():
            pass_on(t, t, c, {"dp_c": 0, "sec_y": (sy + 1) % 4}).start()

        @pl.when((core == 1) & (sy == 3))
        def _():
            if p == 0:
                pass_on(t, t + mbs, c, {"dp_c": 0, "sec_y": 0}).start()
            else:

                @pl.when((sx == 1) & (j == mbs - 1))
                def _():
                    cols = slice(c * chunk, (c + 1) * chunk)
                    inbox[2 * mbs, :, cols] = sent[t, :, cols]

                @pl.when((sx == 0) | (j < mbs - 1))
                def _():
                    pass_on(t, 2 * mbs, c, {**at_section(j), "dp_c": sx}).start()

    def share_first(j):
        return copy(
            start_x.at[j], first_x, first_send.at[j], first_recv, {**at_section(j), "dp_c": sx}
        )

    def run_pass(p):
        def step(j, carry):
            t = p * mbs + j
            waited = jnp.logical_not(first_stage & (sx == 0)) if p == 0 else None
            for c in range(chunks):
                arrived = pass_on(t, t, c, twin)
                if p == 0:
                    pl.when(waited)(arrived.wait_recv)
                else:
                    arrived.wait_recv()
            held[...] = inbox[t]

            if p > 0:

                @pl.when(first_stage)
                def _():
                    moved = (
                        inbox[j].astype(jnp.float32)
                        + sched[sx, 1, pl.ds(j // 2, 1), :1] * held[...].astype(jnp.float32)
                    ).astype(jnp.bfloat16)
                    held[...] = moved
                    start_x[j] = moved

                    @pl.when((j == 0) & (sx == 0))
                    def _():
                        first_x[...] = moved

                    @pl.when((j > 0) | (sx > 0))
                    def _():
                        share_first(j).start()

            hidden = held[...].astype(jnp.float32)
            mean_sq = jnp.mean(hidden * hidden, axis=-1, keepdims=True)
            cond_row = cond[sx, p * 4 + j // 2]
            inputs = (
                hidden * lax.rsqrt(mean_sq + 1e-06) * (1.0 + cond_row * mods[0:1])
                + cond_row * mods[1:2]
            ).astype(jnp.bfloat16)
            gate = 1.0 + cond_row * mods[2:3]
            for c in range(chunks):
                cols = slice(c * chunk, (c + 1) * chunk)
                mixed = jnp.dot(
                    inputs,
                    weight[:, :, cols].reshape(width, chunk),
                    preferred_element_type=jnp.float32,
                )
                sent[t, :, cols] = (
                    hidden[:, cols] + gate[:, cols] * jax.nn.gelu(mixed)
                ).astype(jnp.bfloat16)
                hop(t, p, j, c)

            return carry

        lax.fori_loop(0, mbs, step, 0)

    run_pass(0)
    for k in range(16):
        slot = (dev + 2 * k) % 32
        block = student_ref.at[slot]
        to_twin = copy(block, block, student_send.at[16 + k], student_recv.at[slot], twin)
        if k > 0:
            to_twin.wait_recv()
        start(to_twin)
    for k in range(16):
        slot = (dev + 2 * k) % 32 + 1 - 2 * core
        block = student_ref.at[slot]
        copy(block, block, student_send.at[0], student_recv.at[slot], twin).wait_recv()

    def own_cols(x):
        n = student_ref.shape[2]
        picked = x[:, 0:n]
        for k in range(1, 8):
            picked = jnp.where(sec == k, x[:, k * n : (k + 1) * n], picked)
        return picked

    root = math.sqrt(2.0 / math.pi)
    for n in range(4):
        latents = noise_ref[2 * n : 2 * n + 2].reshape(2 * rows, width).astype(jnp.float32)
        mean_sq = jnp.mean(latents * latents, axis=-1, keepdims=True)
        cond_row = cond[core, n]
        student_in = (
            latents * lax.rsqrt(mean_sq + 1e-06) * (1.0 + cond_row * student_mod_ref[0:1])
            + cond_row * student_mod_ref[1:2]
        ).astype(jnp.bfloat16)
        mixed = jnp.dot(
            student_in,
            student_ref[...].reshape(width, student_ref.shape[2]),
            preferred_element_type=jnp.float32,
        )
        bent = jnp.tanh(root * (mixed + 0.044715 * mixed * mixed * mixed))
        half = 0.5 * (1.0 + bent)
        bend = half + 0.5 * mixed * (1.0 - bent * bent) * root * (
            1.0 + 3.0 * 0.044715 * mixed * mixed
        )
        gate = own_cols(1.0 + cond_row * student_mod_ref[2:3])
        level = sched[core, 0, n : n + 1, :1] / LEVELS
        z = own_cols(latents)
        moved = z - level * (z + gate * (mixed * half))
        slope[2 * n * rows : 2 * (n + 1) * rows] = -level * gate * bend
        student_t[:, 2 * n * rows : 2 * (n + 1) * rows] = student_in.T
        feat_part[2 * n : 2 * n + 2] = (
            jnp.dot(
                moved.astype(jnp.bfloat16),
                feature_shard_ref[...],
                preferred_element_type=jnp.float32,
            )
            .astype(jnp.bfloat16)
            .reshape(2, rows, -1)
        )

    def send_feat(k, slot):
        return copy(
            feat_part.at[k], feats.at[slot], feat_send.at[k], feat_recv.at[slot], at_section(k)
        )

    for k in range(1, 8):
        start(send_feat((sec + k) % 8, sec))
    for k in range(4):
        slot = ((sy + k) % 4) * 2 + sx
        block = feature_ref.at[slot]
        across = copy(
            block, block, feature_send.at[4 + k], feature_recv.at[slot], x_outer
        )
        if k > 0:
            across.wait_recv()
        start(across)

    run_pass(1)

    last_self = (core == 1) & (sec == 7)
    first_self = (core == 0) & (sec == 0)

    for c in range(chunks):
        pl.when(jnp.logical_not(last_self))(pass_on(0, 2 * mbs, c, twin).wait_recv)

    @pl.when(jnp.logical_not(first_self))
    def _():
        share_first(0).wait_recv()

    x2 = (
        first_x[...].astype(jnp.float32)
        + sched[core, 1, pl.ds(4 + sec // 2, 1), :1] * inbox[2 * mbs].astype(jnp.float32)
    ).astype(jnp.bfloat16)
    teacher_ref[sec] = x2
    for k in range(4):
        slot = ((sy + k) % 4) * 2 + 1 - sx
        block = feature_ref.at[slot]
        copy(block, block, feature_send.at[0], feature_recv.at[slot], twin).wait_recv()

    sections = 8
    chips = summed.shape[0]
    piece = summed.shape[1]
    feat = feats.shape[2]
    chip = xl * 8 + zz

    def at_chip(q):
        return {"dp_x": q // 8, "dp_z": q % 8}

    def send_grad(k, slot):
        return copy(grads.at[slot], grads.at[slot], grad_send.at[k], grad_recv.at[slot], at_section(k))

    def send_piece(q, slot):
        return copy(summed.at[q], pieces.at[slot], piece_send.at[q], piece_recv.at[slot], at_chip(q))

    def send_final(q, slot):
        block = final.at[core, slot]
        return copy(block, block, final_send.at[q], final_recv.at[slot], at_chip(q))

    def send_twin(half, slot):
        block = final.at[half, slot]
        return copy(block, block, twin_send.at[slot], twin_recv.at[slot], twin)

    send_half = copy(half_out, half_in, half_send, half_recv, twin)

    def send_out(k, slot):
        return copy(teacher_ref.at[slot], teacher_ref.at[slot], out_send.at[k], out_recv.at[slot], at_section(k))

    feat_teacher = jnp.dot(
        x2, feature_ref[...].reshape(width, feat), preferred_element_type=jnp.float32
    )
    feat_student = feat_part[sec].astype(jnp.float32)
    for k in range(1, sections):
        other = (sec + k) % sections
        send_feat(other, other).wait_recv()
        feat_student = feat_student + feats[other].astype(jnp.float32)

    def unit(f):
        positive = jnp.maximum(f, 0.0)
        scale = lax.rsqrt(jnp.mean(positive * positive, axis=-1, keepdims=True) + 1e-06)
        return positive * scale, scale

    unit_s, scale_s = unit(feat_student)
    unit_t, _ = unit(feat_teacher)
    gap = unit_s - unit_t
    lin = lin_ref[...]
    dist_ref[...] = lax.dot_general(
        lin,
        gap * gap,
        (((1,), (1,)), ((), ())),
        preferred_element_type=jnp.float32,
        precision=lax.Precision.HIGHEST,
    )
    unit_grad = 2.0 * token_ref[...] * lin * gap
    mean_dot = jnp.mean(unit_grad * unit_s, axis=-1, keepdims=True)
    feat_grad = scale_s * (unit_grad - unit_s * mean_dot)
    grads[sec] = jnp.where(feat_student > 0.0, feat_grad, 0.0).astype(jnp.bfloat16)
    for k in range(1, sections):
        send_grad((sec + k) % sections, sec).start()
    for k in range(1, sections):
        other = (sec + k) % sections
        send_grad(other, other).wait_recv()

    out_grad = lax.dot_general(
        grads[...].reshape(sections * rows, feat),
        feature_ref[sec],
        (((1,), (1,)), ((), ())),
        preferred_element_type=jnp.float32,
    )
    mixed_grad = (out_grad * slope[...]).astype(jnp.bfloat16)
    half_rows = width // 2
    for half in range(2):
        partial[half] = lax.dot_general(
            student_t[half * half_rows : (half + 1) * half_rows],
            mixed_grad,
            (((1,), (0,)), ((), ())),
            preferred_element_type=jnp.float32,
        ).reshape(chips, piece, -1)
    half_out[...] = partial[1 - core].astype(jnp.bfloat16)
    send_half.start()
    for k in range(1, sections):
        send_out((sec + k) % sections, sec).start()
    send_half.wait_recv()
    summed[...] = (partial[core] + half_in[...].astype(jnp.float32)).astype(jnp.bfloat16)
    for k in range(1, chips):
        send_piece((chip + k) % chips, chip).start()
    total = summed[chip].astype(jnp.float32)
    for k in range(1, chips):
        other = (chip + chips - k) % chips
        send_piece(other, other).wait_recv()
        total = total + pieces[other].astype(jnp.float32)
    final[core, chip] = total.astype(jnp.bfloat16)
    for k in range(1, chips):
        send_final((chip + k) % chips, chip).start()
    send_twin(core, chip).start()
    grad_ref[core, chip] = final[core, chip].astype(jnp.float32)
    for k in range(1, chips):
        other = (chip + chips - k) % chips
        send_final(other, other).wait_recv()
        send_twin(core, other).start()
        grad_ref[core, other] = final[core, other].astype(jnp.float32)
    for k in range(chips):
        other = (chip + chips - k) % chips
        send_twin(1 - core, other).wait_recv()
        grad_ref[1 - core, other] = final[1 - core, other].astype(jnp.float32)

    for k in range(1, sections):
        other = (sec + k) % sections
        send_out(other, other).wait_recv()
        send_out(other, sec).wait_send()
    send_half.wait_send()
    for k in range(1, sections):
        send_grad((sec + k) % sections, sec).wait_send()
    for k in range(1, chips):
        send_piece((chip + k) % chips, chip).wait_send()
        send_final((chip + k) % chips, chip).wait_send()
    for k in range(chips):
        send_twin(core, k).wait_send()

    def drain(t, carry):
        for c in range(chunks):
            pass_on(t, t, c, twin).wait_send()
        return carry

    lax.fori_loop(0, 2 * mbs - 1, drain, 0)

    for c in range(chunks):
        pl.when(jnp.logical_not(last_self))(pass_on(2 * mbs - 1, 0, c, twin).wait_send)

    @pl.when(first_stage)
    def _():
        for j in range(1, mbs):
            share_first(j).wait_send()

        @pl.when(sx > 0)
        def _():
            share_first(0).wait_send()

    for what, when in started:
        if when is None:
            what.wait_send()
        else:
            pl.when(when)(what.wait_send)


def run_train(
    noise,
    ids,
    sched,
    frequency,
    time_weight,
    block,
    block_mod,
    student_shard,
    feature_shard,
    student_mod,
    lin,
    token,
    table,
):
    mbs, rows, width = noise.shape
    vocab = table.shape[0]
    piece = block.shape[0]
    cols = student_shard.shape[1]
    feat_rows, feat = feature_shard.shape
    vmem = pl.BlockSpec(memory_space=pltpu.VMEM)
    dma = pltpu.SemaphoreType.DMA
    bf16 = jnp.bfloat16
    f32 = jnp.float32
    return pl.pallas_call(
        train_kernel,
        out_shape=(
            jax.ShapeDtypeStruct((mbs, rows, width), bf16),
            jax.ShapeDtypeStruct((1, rows), f32),
            jax.ShapeDtypeStruct((2, 16, piece, cols), f32),
        ),
        in_specs=[vmem] * 12 + [pl.BlockSpec(memory_space=pl.ANY)],
        out_specs=(vmem,) * 3,
        scratch_shapes=[
            pltpu.VMEM((vocab, width), bf16),
            pltpu.VMEM((32, piece, width), bf16),
            pltpu.VMEM((3, width), f32),
            pltpu.VMEM((16, 1, width), f32),
            pltpu.VMEM((32, 1, width), f32),
            pltpu.VMEM((8, 1, width), f32),
            pltpu.VMEM((2, 2, 8, 128), f32),
            pltpu.VMEM((2, 8, 1, width), f32),
            pltpu.VMEM((rows, width), bf16),
            pltpu.VMEM((2 * mbs, rows, width), bf16),
            pltpu.VMEM((2 * mbs + 1, rows, width), bf16),
            pltpu.VMEM((mbs, rows, width), bf16),
            pltpu.VMEM((rows, width), bf16),
            pltpu.VMEM((32, piece, cols), bf16),
            pltpu.VMEM((8, feat_rows, feat), bf16),
            pltpu.VMEM((width, mbs * rows), bf16),
            pltpu.VMEM((mbs * rows, cols), f32),
            pltpu.VMEM((8, rows, feat), bf16),
            pltpu.VMEM((8, rows, feat), bf16),
            pltpu.VMEM((8, rows, feat), bf16),
            pltpu.VMEM((2, 16, piece, cols), f32),
            pltpu.VMEM((16, piece, cols), bf16),
            pltpu.VMEM((16, piece, cols), bf16),
            pltpu.VMEM((16, piece, cols), bf16),
            pltpu.VMEM((16, piece, cols), bf16),
            pltpu.VMEM((2, 16, piece, cols), bf16),
            dma,
            dma((129,)),
            dma((32,)),
            dma((32,)),
            dma((32,)),
            dma((8,)),
            dma((8,)),
            dma,
            dma,
            dma((mbs * 3,)),
            dma(((2 * mbs + 1) * 3,)),
            dma((2 * mbs * 3,)),
            dma((mbs,)),
            dma,
            dma((32,)),
            dma((32,)),
            dma((8,)),
            dma((8,)),
            dma,
            dma,
            dma((8,)),
            dma((8,)),
            dma((8,)),
            dma((8,)),
            dma,
            dma,
            dma((16,)),
            dma((16,)),
            dma((16,)),
            dma((16,)),
            dma((16,)),
            dma((16,)),
            dma((8,)),
            dma((8,)),
        ],
        compiler_params=pltpu.CompilerParams(
            collective_id=0, has_side_effects=True, vmem_limit_bytes=56 * 1024 * 1024
        ),
    )(
        noise,
        ids,
        sched,
        frequency,
        time_weight,
        block,
        block_mod,
        student_shard,
        feature_shard,
        student_mod,
        lin,
        token,
        table,
    )


def local(
    noise,
    sched_index,
    text_ids,
    text_table,
    time_weight,
    block_weight,
    block_mod,
    student_weight,
    student_mod,
    feature_weight,
    lin_weight,
    token_weight,
):
    batches, tokens, model_width = noise.shape
    sections = lax.axis_size(SECTION)
    own_section = lax.axis_index(SECTION)
    row_count = batches * tokens
    share_rows = row_count // sections
    vocab_rows = text_table.shape[0]
    offset = lax.axis_index(DP) * vocab_rows
    ids = lax.dynamic_index_in_dim(
        text_ids.reshape(16, 8, -1), own_section, 1, keepdims=False
    ) - offset
    indices_f = sched_index.astype(jnp.float32)
    half_freq = time_weight.shape[0] // 2
    frequency = jnp.exp(-math.log(10000.0) * jnp.arange(half_freq, dtype=jnp.float32) / half_freq)
    deltas = (indices_f[:, 1:] - indices_f[:, :-1]) / LEVELS
    sched = jnp.broadcast_to(
        jnp.stack([indices_f[:, :2].T.reshape(8), deltas.T.reshape(8)])[:, :, None], (2, 8, 128)
    )
    weight_share = lax.dynamic_slice_in_dim(token_weight, own_section * share_rows, share_rows, 0)
    teacher, token_distance, student_grad = run_train(
        noise.reshape(sections, share_rows, model_width),
        ids,
        sched,
        frequency[None, :],
        time_weight,
        block_weight[0],
        block_mod[0],
        student_weight,
        feature_weight,
        student_mod,
        lin_weight[None, :],
        weight_share[:, None],
        text_table,
    )
    return (
        teacher.reshape(noise.shape),
        student_grad.reshape(model_width, -1),
        token_distance.reshape(share_rows),
    )


def solution(mesh):
    torus = Mesh(mesh.devices.reshape(2, 8, 2, 4, 2), DP + SECTION)
    in_specs = (
        P(DP, None, None),
        P(DP, None),
        P(),
        P(DP, None),
        P(),
        P(SECTION, DP, None),
        P(SECTION, None, None),
        P(DP, SECTION),
        P(),
        P(SECTION, None),
        P(),
        P(DP),
    )
    out_specs = (P(DP, None, None), P(None, SECTION), P(DP + SECTION))
    return jax.shard_map(local, mesh=torus, in_specs=in_specs, out_specs=out_specs, check_vma=False)
```

```python
import math

import jax
import jax.numpy as jnp
import numpy as np
from jax import lax
from jax.experimental import pallas as pl
from jax.experimental.pallas import tpu as pltpu
from jax.sharding import Mesh
from jax.sharding import PartitionSpec as P

LEVELS = 1000
DP = ("dp_x", "dp_z", "dp_c")
SECTION = ("sec_y", "sec_x")
MESH = pl.DeviceIdType.MESH


def train_kernel(
    noise_ref,
    ids_ref,
    sched_ref,
    frequency_ref,
    time_weight_ref,
    block_ref,
    block_mod_ref,
    student_shard_ref,
    feature_shard_ref,
    student_mod_ref,
    lin_ref,
    token_ref,
    table_ref,
    teacher_ref,
    dist_ref,
    grad_ref,
    ids,
    table,
    weight,
    mods,
    rows_out,
    rows_in,
    pooled,
    sched,
    cond,
    held,
    sent,
    inbox,
    start_x,
    first_x,
    student_ref,
    feature_ref,
    student_rows,
    slope,
    slope_t,
    feat_part,
    feats,
    grads,
    partial,
    half_out,
    half_in,
    summed,
    pieces,
    final,
    table_sem,
    weight_send,
    weight_recv,
    row_send,
    row_recv,
    pooled_send,
    pooled_recv,
    sched_send,
    sched_recv,
    noise_send,
    inbox_recv,
    sent_send,
    first_send,
    first_recv,
    student_send,
    student_recv,
    feature_send,
    feature_recv,
    mods_send,
    mods_recv,
    feat_send,
    feat_recv,
    grad_send,
    grad_recv,
    half_send,
    half_recv,
    piece_send,
    piece_recv,
    final_send,
    final_recv,
    twin_send,
    twin_recv,
    out_send,
    out_recv,
):
    mbs, rows, width = noise_ref.shape
    chunk = 512
    chunks = width // chunk
    xl = lax.axis_index("dp_x")
    zz = lax.axis_index("dp_z")
    core = lax.axis_index("dp_c")
    sy = lax.axis_index("sec_y")
    sx = lax.axis_index("sec_x")
    sec = sy * 2 + sx
    dev = xl * 16 + zz * 2 + core
    twin = {"dp_c": 1 - core}

    def at_section(k):
        return {"sec_y": k // 2, "sec_x": k % 2}

    def at_dp(k):
        return {"dp_x": k // 16, "dp_z": (k // 2) % 8, "dp_c": k % 2}

    load_table = pltpu.make_async_copy(table_ref, table, table_sem)
    load_table.start()

    barrier = pltpu.get_barrier_semaphore()

    def greet(where):
        pl.semaphore_signal(barrier, inc=1, device_id=where, device_id_type=MESH)

    for k in range(1, 8):
        for dc in range(2):
            greet({**at_section((sec + k) % 8), "dp_c": (core + dc) % 2})
    for k in range(1, 32):
        greet(at_dp((dev + k) % 32))
    greet({"sec_x": 1 - sx, "dp_x": 1 - xl})
    pl.semaphore_wait(barrier, 46)

    def copy(src, dst, send, recv, where):
        return pltpu.make_async_remote_copy(
            src_ref=src,
            dst_ref=dst,
            send_sem=send,
            recv_sem=recv,
            device_id=where,
            device_id_type=MESH,
        )

    started = []

    def start(what, when=None):
        started.append((what, when))
        if when is None:
            what.start()
        else:
            pl.when(when)(what.start)

    source = sx == core
    relay = sx != core

    def piece_a(a, z):
        return a * 16 + (z % 8) * 2 + core

    def piece_b(a, z):
        return a * 16 + (z % 8) * 2 + 1 - core

    z_up = {"dp_z": (zz + 1) % 8}
    z_down = {"dp_z": (zz + 7) % 8}
    x_mate = {"dp_x": 1 - xl}
    x_outer = {"dp_x": 1 - xl, "sec_x": 1 - sx}
    way = {0: z_up, 1: z_down, 2: x_mate, 3: x_outer}

    def go(p, towards, when=None):
        block = weight.at[p]
        start(
            copy(block, block, weight_send.at[p * 4 + towards], weight_recv.at[p], way[towards]),
            when,
        )

    def arrive(p):
        block = weight.at[p]
        copy(block, block, weight_send.at[p], weight_recv.at[p], twin).wait_recv()

    @pl.when(source)
    def _():
        weight[dev] = block_ref[...]
        mods[...] = block_mod_ref[...]

    lend_mods = copy(block_mod_ref, mods, mods_send, mods_recv, x_outer)
    start(lend_mods, source)

    start(copy(block_ref, weight.at[dev], weight_send.at[dev * 4], weight_recv.at[dev], twin), relay)
    for towards in (2, 3, 0, 1):
        go(piece_a(xl, zz), towards, source)

    levels = [
        jnp.broadcast_to(sched_ref[:, r : r + 1].astype(jnp.float32), (4, 128)) for r in range(3)
    ]
    for r in range(2):
        sched[core, 0, 4 * r : 4 * r + 4] = levels[r]
        sched[core, 1, 4 * r : 4 * r + 4] = (levels[r + 1] - levels[r]) / LEVELS
    start(copy(sched.at[core], sched.at[core], sched_send, sched_recv, twin))
    first_chip = sy == 0
    first_stage = first_chip & (core == 0)
    lender = first_chip & (core == 1) & (sx == 1)

    for j in range(mbs):
        for c in range(chunks):
            cols = slice(c * chunk, (c + 1) * chunk)
            start(
                copy(
                    noise_ref.at[j, :, cols],
                    inbox.at[j, :, cols],
                    noise_send.at[j * chunks + c],
                    inbox_recv.at[j * chunks + c],
                    twin,
                ),
                lender,
            )

    @pl.when(first_stage & (sx == 0))
    def _():
        inbox[0:mbs] = noise_ref[...]

    for k in range(1, 4):
        start(
            copy(
                feature_shard_ref,
                feature_ref.at[sec],
                feature_send.at[k],
                feature_recv.at[sec],
                {"sec_y": (sy + k) % 4},
            )
        )
    feature_ref[sec] = feature_shard_ref[...]

    @pl.when(source)
    def _():
        arrive(piece_b(xl, zz))

    go(piece_b(xl, zz), 0, source)
    go(piece_b(xl, zz), 1, source)
    go(piece_b(xl, zz), 2, source)
    go(piece_b(xl, zz), 3, source)

    arrive_a = piece_a(1 - xl, zz)
    arrive(arrive_a)
    go(arrive_a, 2, relay)

    go(arrive_a, 0)
    go(arrive_a, 1)

    @pl.when(relay)
    def _():
        arrive(piece_a(xl, zz))

    go(piece_a(xl, zz), 0, relay)
    go(piece_a(xl, zz), 1, relay)

    vocab = table.shape[0]
    text_len, samples = ids_ref.shape
    ids[...] = jnp.zeros_like(ids)
    ids[0:text_len] = ids_ref[...].astype(jnp.float32)
    by_sample = ids[...].T.reshape(samples // 8, 8, -1)
    place = lax.broadcasted_iota(jnp.int32, by_sample.shape, 1)
    own_ids = jnp.sum(jnp.where(place == sec, by_sample, 0.0), axis=1)
    local_ids = own_ids.astype(jnp.int32) - dev * vocab
    lanes = lax.broadcasted_iota(jnp.int32, (samples // 8, vocab), 1)
    counts = jnp.zeros(lanes.shape, jnp.float32)
    for t in range(text_len):
        counts = counts + jnp.where(local_ids[:, t : t + 1] == lanes, 1.0, 0.0)
    load_table.wait()
    part = jnp.dot(
        counts.astype(jnp.bfloat16), table[...], preferred_element_type=jnp.float32
    ) / text_len
    for g in range(16):
        rows_out[g] = part[g : g + 1]
    rows_in[dev] = rows_out[dev // 2]
    for k in range(1, 32):
        other = (dev + k) % 32
        start(
            copy(
                rows_out.at[other // 2],
                rows_in.at[dev],
                row_send.at[k],
                row_recv.at[dev],
                at_dp(other),
            )
        )

    def take_x(z):
        p = piece_b(1 - xl, z)
        arrive(p)
        odd = z % 2
        go(p, 3, source & (odd == 1))
        go(p, 2, relay & (odd == 0))

    def take_z_b(k, up):
        z = zz + 8 - k if up else zz + k
        p = piece_b(xl, z)
        last = k == 4
        here = source & (xl == (0 if up else 1)) if last else source

        @pl.when(here)
        def _():
            arrive(p)

        if k < 3:
            go(p, 0 if up else 1, here)
        elif k == 3:
            go(p, 0 if up else 1, source & (xl == (0 if up else 1)))
        go(p, 2, here)
        go(p, 3, here)

    def take_z_a(k, up):
        z = zz + 8 - k if up else zz + k
        for a in range(2):
            reach = (4 - a) if up else (3 + a)
            if k <= reach:
                p = piece_a(a, z)
                arrive(p)
                if k < reach:
                    go(p, 0 if up else 1)

    def ring_step(k):
        for up in (True, False):
            take_z_b(k, up)
        for up in (True, False):
            take_z_a(k, up)
        if k == 1:
            take_x(zz)
        else:
            take_x(zz + 9 - k)
            take_x(zz + k - 1)

    ring_step(1)

    total = rows_in[dev]
    for k in range(1, 32):
        other = (dev + 32 - k) % 32
        copy(
            rows_out.at[0], rows_in.at[other], row_send.at[k], row_recv.at[other], at_dp(other)
        ).wait_recv()
        total = total + rows_in[other]
    pooled[sec] = total
    for k in range(1, 8):
        start(
            copy(
                pooled.at[sec],
                pooled.at[sec],
                pooled_send.at[k],
                pooled_recv.at[sec],
                at_section((sec + k) % 8),
            )
        )
    ring_step(2)
    copy(sched.at[core], sched.at[1 - core], sched_send, sched_recv, twin).wait_recv()
    for k in range(1, 8):
        other = (sec + k) % 8
        copy(
            pooled.at[other],
            pooled.at[other],
            pooled_send.at[k],
            pooled_recv.at[other],
            at_section(other),
        ).wait_recv()
    for c in range(2):
        angles = sched[c, 0] * frequency_ref[...]
        embedding = jnp.concatenate([jnp.cos(angles), jnp.sin(angles)], axis=-1)
        embed = jnp.dot(
            embedding.astype(jnp.bfloat16), time_weight_ref[...], preferred_element_type=jnp.float32
        )
        for r in range(8):
            cond[c, r] = jax.nn.silu(embed[r : r + 1] + pooled[c * 4 + r % 4])
    ring_step(3)
    ring_step(4)
    take_x(zz + 4)

    @pl.when(relay)
    def _():
        for z in range(8):
            arrive(piece_b(xl, z))

    student_ref[dev] = student_shard_ref[...]
    for k in range(1, 16):
        start(
            copy(
                student_shard_ref,
                student_ref.at[dev],
                student_send.at[k],
                student_recv.at[dev],
                at_dp((dev + 2 * k) % 32),
            )
        )
    pl.when(relay)(lend_mods.wait_recv)

    def pass_on(t, slot, c, where):
        cols = pl.ds(c * chunk, chunk)
        return copy(
            sent.at[t, :, cols],
            inbox.at[slot, :, cols],
            sent_send.at[t * chunks + c],
            inbox_recv.at[slot * chunks + c],
            where,
        )

    def hop(t, p, j, c):
        @pl.when(core == 0)
        def _():
            pass_on(t, t, c, twin).start()

        @pl.when((core == 1) & (sy < 3))
        def _():
            pass_on(t, t, c, {"dp_c": 0, "sec_y": (sy + 1) % 4}).start()

        @pl.when((core == 1) & (sy == 3))
        def _():
            if p == 0:
                pass_on(t, t + mbs, c, {"dp_c": 0, "sec_y": 0}).start()
            else:

                @pl.when((sx == 1) & (j == mbs - 1))
                def _():
                    cols = slice(c * chunk, (c + 1) * chunk)
                    inbox[2 * mbs, :, cols] = sent[t, :, cols]

                @pl.when((sx == 0) | (j < mbs - 1))
                def _():
                    pass_on(t, 2 * mbs, c, {**at_section(j), "dp_c": sx}).start()

    def share_first(j):
        return copy(
            start_x.at[j], first_x, first_send.at[j], first_recv, {**at_section(j), "dp_c": sx}
        )

    def run_pass(p):
        def step(j, carry):
            t = p * mbs + j
            waited = jnp.logical_not(first_stage & (sx == 0)) if p == 0 else None
            for c in range(chunks):
                arrived = pass_on(t, t, c, twin)
                if p == 0:
                    pl.when(waited)(arrived.wait_recv)
                else:
                    arrived.wait_recv()
            held[...] = inbox[t]

            if p > 0:

                @pl.when(first_stage)
                def _():
                    moved = (
                        inbox[j].astype(jnp.float32)
                        + sched[sx, 1, pl.ds(j // 2, 1), :1] * held[...].astype(jnp.float32)
                    ).astype(jnp.bfloat16)
                    held[...] = moved
                    start_x[j] = moved

                    @pl.when((j == 0) & (sx == 0))
                    def _():
                        first_x[...] = moved

                    @pl.when((j > 0) | (sx > 0))
                    def _():
                        share_first(j).start()

            hidden = held[...].astype(jnp.float32)
            mean_sq = jnp.mean(hidden * hidden, axis=-1, keepdims=True)
            cond_row = cond[sx, p * 4 + j // 2]
            inputs = (
                hidden * lax.rsqrt(mean_sq + 1e-06) * (1.0 + cond_row * mods[0])
                + cond_row * mods[1]
            ).astype(jnp.bfloat16)
            gate = 1.0 + cond_row * mods[2]
            for c in range(chunks):
                cols = slice(c * chunk, (c + 1) * chunk)
                mixed = jnp.dot(
                    inputs,
                    weight[:, :, cols].reshape(width, chunk),
                    preferred_element_type=jnp.float32,
                )
                sent[t, :, cols] = (
                    hidden[:, cols] + gate[:, cols] * jax.nn.gelu(mixed)
                ).astype(jnp.bfloat16)
                hop(t, p, j, c)

            return carry

        lax.fori_loop(0, mbs, step, 0)

    run_pass(0)
    for k in range(16):
        slot = (dev + 2 * k) % 32
        block = student_ref.at[slot]
        to_twin = copy(block, block, student_send.at[16 + k], student_recv.at[slot], twin)
        if k > 0:
            to_twin.wait_recv()
        start(to_twin)
    for k in range(16):
        slot = (dev + 2 * k) % 32 + 1 - 2 * core
        block = student_ref.at[slot]
        copy(block, block, student_send.at[0], student_recv.at[slot], twin).wait_recv()

    def own_cols(x):
        n = student_ref.shape[2]
        picked = x[:, 0:n]
        for k in range(1, 8):
            picked = jnp.where(sec == k, x[:, k * n : (k + 1) * n], picked)
        return picked

    root = math.sqrt(2.0 / math.pi)
    for n in range(4):
        latents = noise_ref[2 * n : 2 * n + 2].reshape(2 * rows, width).astype(jnp.float32)
        mean_sq = jnp.mean(latents * latents, axis=-1, keepdims=True)
        cond_row = cond[core, n]
        student_in = (
            latents * lax.rsqrt(mean_sq + 1e-06) * (1.0 + cond_row * student_mod_ref[0:1])
            + cond_row * student_mod_ref[1:2]
        ).astype(jnp.bfloat16)
        mixed = jnp.dot(
            student_in,
            student_ref[...].reshape(width, student_ref.shape[2]),
            preferred_element_type=jnp.float32,
        )
        bent = jnp.tanh(root * (mixed + 0.044715 * mixed * mixed * mixed))
        half = 0.5 * (1.0 + bent)
        bend = half + 0.5 * mixed * (1.0 - bent * bent) * root * (
            1.0 + 3.0 * 0.044715 * mixed * mixed
        )
        gate = own_cols(1.0 + cond_row * student_mod_ref[2:3])
        level = sched[core, 0, n : n + 1, :1] / LEVELS
        z = own_cols(latents)
        moved = z - level * (z + gate * (mixed * half))
        slope[2 * n * rows : 2 * (n + 1) * rows] = -level * gate * bend
        student_rows[2 * n * rows : 2 * (n + 1) * rows] = student_in
        feat_part[2 * n : 2 * n + 2] = (
            jnp.dot(
                moved.astype(jnp.bfloat16),
                feature_shard_ref[...],
                preferred_element_type=jnp.float32,
            )
            .astype(jnp.bfloat16)
            .reshape(2, rows, -1)
        )

    slope_t[...] = slope[...].T

    def send_feat(k, slot):
        return copy(
            feat_part.at[k], feats.at[slot], feat_send.at[k], feat_recv.at[slot], at_section(k)
        )

    for k in range(1, 8):
        start(send_feat((sec + k) % 8, sec))
    for k in range(4):
        slot = ((sy + k) % 4) * 2 + sx
        block = feature_ref.at[slot]
        across = copy(
            block, block, feature_send.at[4 + k], feature_recv.at[slot], x_outer
        )
        if k > 0:
            across.wait_recv()
        start(across)

    run_pass(1)

    last_self = (core == 1) & (sec == 7)
    first_self = (core == 0) & (sec == 0)

    for c in range(chunks):
        pl.when(jnp.logical_not(last_self))(pass_on(0, 2 * mbs, c, twin).wait_recv)

    @pl.when(jnp.logical_not(first_self))
    def _():
        share_first(0).wait_recv()

    x2 = (
        first_x[...].astype(jnp.float32)
        + sched[core, 1, pl.ds(4 + sec // 2, 1), :1] * inbox[2 * mbs].astype(jnp.float32)
    ).astype(jnp.bfloat16)
    teacher_ref[sec] = x2
    for k in range(4):
        slot = ((sy + k) % 4) * 2 + 1 - sx
        block = feature_ref.at[slot]
        copy(block, block, feature_send.at[0], feature_recv.at[slot], twin).wait_recv()

    sections = 8
    chips = summed.shape[0]
    piece = summed.shape[1]
    feat = feats.shape[2]
    chip = xl * 8 + zz

    def at_chip(q):
        return {"dp_x": q // 8, "dp_z": q % 8}

    def send_grad(k, slot):
        return copy(grads.at[slot], grads.at[slot], grad_send.at[k], grad_recv.at[slot], at_section(k))

    def send_piece(q, slot):
        return copy(summed.at[q], pieces.at[slot], piece_send.at[q], piece_recv.at[slot], at_chip(q))

    def send_final(q, slot):
        block = final.at[core, slot]
        return copy(block, block, final_send.at[q], final_recv.at[slot], at_chip(q))

    def send_twin(half, slot):
        block = final.at[half, slot]
        return copy(block, block, twin_send.at[slot], twin_recv.at[slot], twin)

    send_half = copy(half_out, half_in, half_send, half_recv, twin)

    def send_out(k, slot):
        return copy(teacher_ref.at[slot], teacher_ref.at[slot], out_send.at[k], out_recv.at[slot], at_section(k))

    feat_teacher = jnp.dot(
        x2, feature_ref[...].reshape(width, feat), preferred_element_type=jnp.float32
    )
    feat_student = feat_part[sec].astype(jnp.float32)
    for k in range(1, sections):
        other = (sec + k) % sections
        send_feat(other, other).wait_recv()
        feat_student = feat_student + feats[other].astype(jnp.float32)

    def unit(f):
        positive = jnp.maximum(f, 0.0)
        scale = lax.rsqrt(jnp.mean(positive * positive, axis=-1, keepdims=True) + 1e-06)
        return positive * scale, scale

    unit_s, scale_s = unit(feat_student)
    unit_t, _ = unit(feat_teacher)
    gap = unit_s - unit_t
    lin = lin_ref[...]
    dist_ref[...] = lax.dot_general(
        lin,
        gap * gap,
        (((1,), (1,)), ((), ())),
        preferred_element_type=jnp.float32,
        precision=lax.Precision.HIGHEST,
    )
    tokens = token_ref.shape[1]
    own_token = lax.broadcasted_iota(jnp.int32, (rows, tokens), 0) + sec * rows
    token_col = jnp.sum(
        jnp.where(
            lax.broadcasted_iota(jnp.int32, (rows, tokens), 1) == own_token, token_ref[...], 0.0
        ),
        axis=1,
        keepdims=True,
    )
    unit_grad = 2.0 * token_col * lin * gap
    mean_dot = jnp.mean(unit_grad * unit_s, axis=-1, keepdims=True)
    feat_grad = scale_s * (unit_grad - unit_s * mean_dot)
    grads[sec] = jnp.where(feat_student > 0.0, feat_grad, 0.0).astype(jnp.bfloat16)
    for k in range(1, sections):
        send_grad((sec + k) % sections, sec).start()
    for k in range(1, sections):
        other = (sec + k) % sections
        send_grad(other, other).wait_recv()

    out_grad = lax.dot_general(
        feature_ref[sec],
        grads[...].reshape(sections * rows, feat),
        (((1,), (1,)), ((), ())),
        preferred_element_type=jnp.float32,
    )
    mixed_grad = (out_grad * slope_t[...]).astype(jnp.bfloat16)
    product = jnp.dot(mixed_grad, student_rows[...], preferred_element_type=jnp.float32)
    lanes = 128
    blocks = width // lanes
    half_cols = product.shape[0] // 2
    for half in range(2):
        kept = product[half * half_cols : (half + 1) * half_cols]
        partial[half] = jnp.concatenate(
            [kept[:, b * lanes : (b + 1) * lanes] for b in range(blocks)], axis=0
        ).reshape(chips, piece, lanes)
    half_out[...] = partial[1 - core].astype(jnp.bfloat16)
    send_half.start()
    for k in range(1, sections):
        send_out((sec + k) % sections, sec).start()
    send_half.wait_recv()
    summed[...] = (partial[core] + half_in[...].astype(jnp.float32)).astype(jnp.bfloat16)
    for k in range(1, chips):
        send_piece((chip + k) % chips, chip).start()
    total = summed[chip].astype(jnp.float32)
    for k in range(1, chips):
        other = (chip + chips - k) % chips
        send_piece(other, other).wait_recv()
        total = total + pieces[other].astype(jnp.float32)
    final[core, chip] = total.astype(jnp.bfloat16)
    for k in range(1, chips):
        send_final((chip + k) % chips, chip).start()
    send_twin(core, chip).start()
    for k in range(1, chips):
        other = (chip + chips - k) % chips
        send_final(other, other).wait_recv()
        send_twin(core, other).start()
    for k in range(chips):
        other = (chip + chips - k) % chips
        send_twin(1 - core, other).wait_recv()
    for half in range(2):
        kept = final[half].astype(jnp.float32).reshape(blocks * half_cols, lanes)
        for b in range(blocks):
            grad_ref[half * half_cols : (half + 1) * half_cols, b * lanes : (b + 1) * lanes] = kept[
                b * half_cols : (b + 1) * half_cols
            ]

    for k in range(1, sections):
        other = (sec + k) % sections
        send_out(other, other).wait_recv()
        send_out(other, sec).wait_send()
    send_half.wait_send()
    for k in range(1, sections):
        send_grad((sec + k) % sections, sec).wait_send()
    for k in range(1, chips):
        send_piece((chip + k) % chips, chip).wait_send()
        send_final((chip + k) % chips, chip).wait_send()
    for k in range(chips):
        send_twin(core, k).wait_send()

    def drain(t, carry):
        for c in range(chunks):
            pass_on(t, t, c, twin).wait_send()
        return carry

    lax.fori_loop(0, 2 * mbs - 1, drain, 0)

    for c in range(chunks):
        pl.when(jnp.logical_not(last_self))(pass_on(2 * mbs - 1, 0, c, twin).wait_send)

    @pl.when(first_stage)
    def _():
        for j in range(1, mbs):
            share_first(j).wait_send()

        @pl.when(sx > 0)
        def _():
            share_first(0).wait_send()

    for what, when in started:
        if when is None:
            what.wait_send()
        else:
            pl.when(when)(what.wait_send)


def run_train(
    noise,
    ids,
    sched,
    frequency,
    time_weight,
    block,
    block_mod,
    student_shard,
    feature_shard,
    student_mod,
    lin,
    token,
    table,
):
    mbs, rows, width = noise.shape
    vocab = table.shape[0]
    piece = block.shape[0]
    cols = student_shard.shape[1]
    feat_rows, feat = feature_shard.shape
    part = cols * width // (32 * 128)
    vmem = pl.BlockSpec(memory_space=pltpu.VMEM)
    dma = pltpu.SemaphoreType.DMA
    bf16 = jnp.bfloat16
    f32 = jnp.float32
    return pl.pallas_call(
        train_kernel,
        out_shape=(
            jax.ShapeDtypeStruct((mbs, rows, width), bf16),
            jax.ShapeDtypeStruct((1, rows), f32),
            jax.ShapeDtypeStruct((cols, width), f32),
        ),
        in_specs=[vmem] * 12 + [pl.BlockSpec(memory_space=pl.ANY)],
        out_specs=(vmem,) * 3,
        scratch_shapes=[
            pltpu.VMEM((128, ids.shape[1]), f32),
            pltpu.VMEM((vocab, width), bf16),
            pltpu.VMEM((32, piece, width), bf16),
            pltpu.VMEM((3, 1, width), f32),
            pltpu.VMEM((16, 1, width), f32),
            pltpu.VMEM((32, 1, width), f32),
            pltpu.VMEM((8, 1, width), f32),
            pltpu.VMEM((2, 2, 8, 128), f32),
            pltpu.VMEM((2, 8, 1, width), f32),
            pltpu.VMEM((rows, width), bf16),
            pltpu.VMEM((2 * mbs, rows, width), bf16),
            pltpu.VMEM((2 * mbs + 1, rows, width), bf16),
            pltpu.VMEM((mbs, rows, width), bf16),
            pltpu.VMEM((rows, width), bf16),
            pltpu.VMEM((32, piece, cols), bf16),
            pltpu.VMEM((8, feat_rows, feat), bf16),
            pltpu.VMEM((mbs * rows, width), bf16),
            pltpu.VMEM((mbs * rows, cols), f32),
            pltpu.VMEM((cols, mbs * rows), f32),
            pltpu.VMEM((8, rows, feat), bf16),
            pltpu.VMEM((8, rows, feat), bf16),
            pltpu.VMEM((8, rows, feat), bf16),
            pltpu.VMEM((2, 16, part, 128), f32),
            pltpu.VMEM((16, part, 128), bf16),
            pltpu.VMEM((16, part, 128), bf16),
            pltpu.VMEM((16, part, 128), bf16),
            pltpu.VMEM((16, part, 128), bf16),
            pltpu.VMEM((2, 16, part, 128), bf16),
            dma,
            dma((129,)),
            dma((32,)),
            dma((32,)),
            dma((32,)),
            dma((8,)),
            dma((8,)),
            dma,
            dma,
            dma((mbs * 3,)),
            dma(((2 * mbs + 1) * 3,)),
            dma((2 * mbs * 3,)),
            dma((mbs,)),
            dma,
            dma((32,)),
            dma((32,)),
            dma((8,)),
            dma((8,)),
            dma,
            dma,
            dma((8,)),
            dma((8,)),
            dma((8,)),
            dma((8,)),
            dma,
            dma,
            dma((16,)),
            dma((16,)),
            dma((16,)),
            dma((16,)),
            dma((16,)),
            dma((16,)),
            dma((8,)),
            dma((8,)),
        ],
        compiler_params=pltpu.CompilerParams(
            collective_id=0, has_side_effects=True, vmem_limit_bytes=56 * 1024 * 1024
        ),
    )(
        noise,
        ids,
        sched,
        frequency,
        time_weight,
        block,
        block_mod,
        student_shard,
        feature_shard,
        student_mod,
        lin,
        token,
        table,
    )


def local(
    noise,
    sched_index,
    text_ids,
    text_table,
    time_weight,
    block_weight,
    block_mod,
    student_weight,
    student_mod,
    feature_weight,
    lin_weight,
    token_weight,
):
    batches, tokens, model_width = noise.shape
    sections = lax.axis_size(SECTION)
    row_count = batches * tokens
    share_rows = row_count // sections
    half_freq = time_weight.shape[0] // 2
    frequency = np.exp(-math.log(10000.0) * np.arange(half_freq, dtype=np.float32) / half_freq)
    teacher, token_distance, student_grad = run_train(
        noise.reshape(sections, share_rows, model_width),
        text_ids.T,
        sched_index,
        jnp.asarray(frequency[None, :], jnp.float32),
        time_weight,
        block_weight[0],
        jnp.moveaxis(block_mod, 0, 1),
        student_weight,
        feature_weight,
        student_mod,
        lin_weight[None, :],
        token_weight[None, :],
        text_table,
    )
    return (
        teacher.reshape(noise.shape),
        student_grad.T,
        token_distance.reshape(share_rows),
    )


def solution(mesh):
    torus = Mesh(mesh.devices.reshape(2, 8, 2, 4, 2), DP + SECTION)
    in_specs = (
        P(DP, None, None),
        P(DP, None),
        P(),
        P(DP, None),
        P(),
        P(SECTION, DP, None),
        P(SECTION, None, None),
        P(DP, SECTION),
        P(),
        P(SECTION, None),
        P(),
        P(DP),
    )
    out_specs = (P(DP, None, None), P(None, SECTION), P(DP + SECTION))
    return jax.shard_map(local, mesh=torus, in_specs=in_specs, out_specs=out_specs, check_vma=False)
```

```python
import math

import jax
import jax.numpy as jnp
import numpy as np
from jax import lax
from jax.experimental import pallas as pl
from jax.experimental.pallas import tpu as pltpu
from jax.sharding import Mesh
from jax.sharding import PartitionSpec as P

LEVELS = 1000
DP = ("dp_x", "dp_z", "dp_c")
SECTION = ("sec_y", "sec_x")
MESH = pl.DeviceIdType.MESH


def train_kernel(
    noise_ref,
    ids_ref,
    sched_ref,
    frequency_ref,
    time_weight_ref,
    block_ref,
    block_mod_ref,
    student_shard_ref,
    feature_shard_ref,
    student_mod_ref,
    lin_ref,
    token_ref,
    table_ref,
    teacher_ref,
    dist_ref,
    grad_ref,
    ids,
    table,
    weight,
    mods,
    rows_out,
    rows_in,
    pooled,
    sched,
    cond,
    held,
    sent,
    inbox,
    start_x,
    first_x,
    student_ref,
    feature_ref,
    student_rows,
    slope,
    slope_t,
    feat_part,
    feats,
    grads,
    partial,
    half_out,
    half_in,
    summed,
    pieces,
    final,
    table_sem,
    weight_send,
    weight_recv,
    row_send,
    row_recv,
    pooled_send,
    pooled_recv,
    lend_send,
    lend_recv,
    inbox_recv,
    sent_send,
    first_send,
    first_recv,
    student_send,
    student_recv,
    feature_send,
    feature_recv,
    mods_send,
    mods_recv,
    feat_send,
    feat_recv,
    grad_send,
    grad_recv,
    half_send,
    half_recv,
    piece_send,
    piece_recv,
    final_send,
    final_recv,
    twin_send,
    twin_recv,
    out_send,
    out_recv,
):
    mbs, rows, width = noise_ref.shape
    chunk = 512
    chunks = width // chunk
    xl = lax.axis_index("dp_x")
    zz = lax.axis_index("dp_z")
    core = lax.axis_index("dp_c")
    sy = lax.axis_index("sec_y")
    sx = lax.axis_index("sec_x")
    sec = sy * 2 + sx
    dev = xl * 16 + zz * 2 + core
    twin = {"dp_c": 1 - core}

    def at_section(k):
        return {"sec_y": k // 2, "sec_x": k % 2}

    def at_dp(k):
        return {"dp_x": k // 16, "dp_z": (k // 2) % 8, "dp_c": k % 2}

    load_table = pltpu.make_async_copy(table_ref, table, table_sem)
    load_table.start()

    barrier = pltpu.get_barrier_semaphore()

    def greet(where):
        pl.semaphore_signal(barrier, inc=1, device_id=where, device_id_type=MESH)

    for k in range(1, 8):
        for dc in range(2):
            greet({**at_section((sec + k) % 8), "dp_c": (core + dc) % 2})
    for k in range(1, 32):
        greet(at_dp((dev + k) % 32))
    greet({"sec_x": 1 - sx, "dp_x": 1 - xl})
    pl.semaphore_wait(barrier, 46)

    def copy(src, dst, send, recv, where):
        return pltpu.make_async_remote_copy(
            src_ref=src,
            dst_ref=dst,
            send_sem=send,
            recv_sem=recv,
            device_id=where,
            device_id_type=MESH,
        )

    started = []

    def start(what, when=None):
        started.append((what, when))
        if when is None:
            what.start()
        else:
            pl.when(when)(what.start)

    source = sx == core
    relay = sx != core

    def piece_a(a, z):
        return a * 16 + (z % 8) * 2 + core

    def piece_b(a, z):
        return a * 16 + (z % 8) * 2 + 1 - core

    z_up = {"dp_z": (zz + 1) % 8}
    z_down = {"dp_z": (zz + 7) % 8}
    x_mate = {"dp_x": 1 - xl}
    x_outer = {"dp_x": 1 - xl, "sec_x": 1 - sx}
    way = {0: z_up, 1: z_down, 2: x_mate, 3: x_outer}

    def go(p, towards, when=None):
        block = weight.at[core, p]
        start(
            copy(block, block, weight_send.at[p * 4 + towards], weight_recv.at[p], way[towards]),
            when,
        )

    def lend(p, when=None):
        block = weight.at[core, p]
        start(copy(block, block, lend_send.at[p], lend_recv.at[p], twin), when)

    def arrive(p, when=None):
        block = weight.at[core, p]
        landed = copy(block, block, weight_send.at[p], weight_recv.at[p], twin)
        if when is None:
            landed.wait_recv()
        else:
            pl.when(when)(landed.wait_recv)
        lend(p, when)

    mods[sx] = block_mod_ref[...]
    lend_mods = copy(block_mod_ref, mods.at[sx], mods_send, mods_recv, x_outer)
    start(lend_mods)

    @pl.when(source)
    def _():
        weight[core, dev] = block_ref[...]

    own_shard = copy(
        block_ref, weight.at[1 - core, dev], weight_send.at[128], weight_recv.at[dev], twin
    )
    start(own_shard, relay)
    for towards in (2, 3, 0, 1):
        go(piece_a(xl, zz), towards, source)
    lend(piece_a(xl, zz), source)

    levels = [
        jnp.broadcast_to(sched_ref[:, r : r + 1].astype(jnp.float32), (4, 128)) for r in range(3)
    ]
    for r in range(2):
        sched[0, 4 * r : 4 * r + 4] = levels[r]
        sched[1, 4 * r : 4 * r + 4] = (levels[r + 1] - levels[r]) / LEVELS
    first_stage = sy == 0

    for k in range(1, 4):
        start(
            copy(
                feature_shard_ref,
                feature_ref.at[sec],
                feature_send.at[k],
                feature_recv.at[sec],
                {"sec_y": (sy + k) % 4},
            )
        )
    feature_ref[sec] = feature_shard_ref[...]

    arrive(piece_b(xl, zz), source)

    go(piece_b(xl, zz), 0, source)
    go(piece_b(xl, zz), 1, source)
    go(piece_b(xl, zz), 2, source)
    go(piece_b(xl, zz), 3, source)

    arrive_a = piece_a(1 - xl, zz)
    arrive(arrive_a)
    go(arrive_a, 2, relay)

    go(arrive_a, 0)
    go(arrive_a, 1)

    arrive(piece_a(xl, zz), relay)

    go(piece_a(xl, zz), 0, relay)
    go(piece_a(xl, zz), 1, relay)

    vocab = table.shape[0]
    text_len, samples = ids_ref.shape
    ids[...] = jnp.zeros_like(ids)
    ids[0:text_len] = ids_ref[...].astype(jnp.float32)
    by_sample = ids[...].T.reshape(samples // 8, 8, -1)
    place = lax.broadcasted_iota(jnp.int32, by_sample.shape, 1)
    own_ids = jnp.sum(jnp.where(place == sec, by_sample, 0.0), axis=1)
    local_ids = own_ids.astype(jnp.int32) - dev * vocab
    lanes = lax.broadcasted_iota(jnp.int32, (samples // 8, vocab), 1)
    counts = jnp.zeros(lanes.shape, jnp.float32)
    for t in range(text_len):
        counts = counts + jnp.where(local_ids[:, t : t + 1] == lanes, 1.0, 0.0)
    load_table.wait()
    part = jnp.dot(
        counts.astype(jnp.bfloat16), table[...], preferred_element_type=jnp.float32
    ) / text_len
    for g in range(16):
        rows_out[g] = part[g : g + 1]
    rows_in[dev] = rows_out[dev // 2]
    for k in range(1, 32):
        other = (dev + k) % 32
        start(
            copy(
                rows_out.at[other // 2],
                rows_in.at[dev],
                row_send.at[k],
                row_recv.at[dev],
                at_dp(other),
            )
        )

    def take_x(z):
        p = piece_b(1 - xl, z)
        arrive(p)
        odd = z % 2
        go(p, 3, source & (odd == 1))
        go(p, 2, relay & (odd == 0))

    def take_z_b(k, up):
        z = zz + 8 - k if up else zz + k
        p = piece_b(xl, z)
        last = k == 4
        here = source & (xl == (0 if up else 1)) if last else source

        arrive(p, here)

        if k < 3:
            go(p, 0 if up else 1, here)
        elif k == 3:
            go(p, 0 if up else 1, source & (xl == (0 if up else 1)))
        go(p, 2, here)
        go(p, 3, here)

    def take_z_a(k, up):
        z = zz + 8 - k if up else zz + k
        for a in range(2):
            reach = (4 - a) if up else (3 + a)
            if k <= reach:
                p = piece_a(a, z)
                arrive(p)
                if k < reach:
                    go(p, 0 if up else 1)

    def ring_step(k):
        for up in (True, False):
            take_z_b(k, up)
        for up in (True, False):
            take_z_a(k, up)
        if k == 1:
            take_x(zz)
        else:
            take_x(zz + 9 - k)
            take_x(zz + k - 1)

    ring_step(1)

    total = rows_in[dev]
    for k in range(1, 32):
        other = (dev + 32 - k) % 32
        copy(
            rows_out.at[0], rows_in.at[other], row_send.at[k], row_recv.at[other], at_dp(other)
        ).wait_recv()
        total = total + rows_in[other]
    pooled[sec] = total
    for k in range(1, 8):
        start(
            copy(
                pooled.at[sec],
                pooled.at[sec],
                pooled_send.at[k],
                pooled_recv.at[sec],
                at_section((sec + k) % 8),
            )
        )
    ring_step(2)
    for k in range(1, 8):
        other = (sec + k) % 8
        copy(
            pooled.at[other],
            pooled.at[other],
            pooled_send.at[k],
            pooled_recv.at[other],
            at_section(other),
        ).wait_recv()
    angles = sched[0] * frequency_ref[...]
    embedding = jnp.concatenate([jnp.cos(angles), jnp.sin(angles)], axis=-1)
    embed = jnp.dot(
        embedding.astype(jnp.bfloat16), time_weight_ref[...], preferred_element_type=jnp.float32
    )
    for r in range(8):
        cond[r] = jax.nn.silu(embed[r : r + 1] + pooled[core * 4 + r % 4])
    ring_step(3)
    ring_step(4)
    take_x(zz + 4)

    for z in range(8):
        arrive(piece_b(xl, z), relay)

    student_ref[dev] = student_shard_ref[...]
    for k in range(1, 16):
        start(
            copy(
                student_shard_ref,
                student_ref.at[dev],
                student_send.at[k],
                student_recv.at[dev],
                at_dp((dev + 2 * k) % 32),
            )
        )
    copy(block_mod_ref, mods.at[1 - sx], mods_send, mods_recv, x_outer).wait_recv()
    for p in range(32):
        block = weight.at[1 - core, p]
        copy(block, block, lend_send.at[p], lend_recv.at[p], twin).wait_recv()

    def pass_on(t, slot, c, where):
        cols = pl.ds(c * chunk, chunk)
        return copy(
            sent.at[t, :, cols],
            inbox.at[slot, :, cols],
            sent_send.at[t * chunks + c],
            inbox_recv.at[slot * chunks + c],
            where,
        )

    here = mbs // 2

    def hop(t, p, j, c):
        @pl.when(sy < 3)
        def _():
            pass_on(t, t, c, {"sec_y": (sy + 1) % 4}).start()

        @pl.when(sy == 3)
        def _():
            if p == 0:
                pass_on(t, t + here, c, {"sec_y": 0}).start()
            else:

                @pl.when((sx == 1) & (j == here - 1))
                def _():
                    cols = slice(c * chunk, (c + 1) * chunk)
                    inbox[2 * here, :, cols] = sent[t, :, cols]

                @pl.when((sx == 0) | (j < here - 1))
                def _():
                    pass_on(t, 2 * here, c, at_section(sx * here + j)).start()

    def share_first(j):
        return copy(
            start_x.at[j], first_x, first_send.at[j], first_recv, at_section(sx * here + j)
        )

    def run_pass(p):
        def step(j, carry):
            t = p * here + j
            sample = (sx * here + j) // 2
            for c in range(chunks):
                arrived = pass_on(t, t, c, twin)
                if p == 0:
                    pl.when(sy > 0)(arrived.wait_recv)
                else:
                    arrived.wait_recv()
            if p == 0:

                @pl.when(first_stage)
                def _():
                    held[...] = noise_ref[sx * here + j]

                @pl.when(sy > 0)
                def _():
                    held[...] = inbox[t]

            else:
                held[...] = inbox[t]

                @pl.when(first_stage)
                def _():
                    moved = (
                        noise_ref[sx * here + j].astype(jnp.float32)
                        + sched[1, pl.ds(sample, 1), :1] * held[...].astype(jnp.float32)
                    ).astype(jnp.bfloat16)
                    held[...] = moved
                    start_x[j] = moved

                    @pl.when((j == 0) & (sx == 0))
                    def _():
                        first_x[...] = moved

                    @pl.when((j > 0) | (sx > 0))
                    def _():
                        share_first(j).start()

            cond_row = cond[p * 4 + sample]
            for b in range(2):
                hidden = held[...].astype(jnp.float32)
                mean_sq = jnp.mean(hidden * hidden, axis=-1, keepdims=True)
                inputs = (
                    hidden * lax.rsqrt(mean_sq + 1e-06) * (1.0 + cond_row * mods[b, 0])
                    + cond_row * mods[b, 1]
                ).astype(jnp.bfloat16)
                gate = 1.0 + cond_row * mods[b, 2]
                for c in range(chunks):
                    cols = slice(c * chunk, (c + 1) * chunk)
                    mixed = jnp.dot(
                        inputs,
                        weight[b, :, :, cols].reshape(width, chunk),
                        preferred_element_type=jnp.float32,
                    )
                    result = (hidden[:, cols] + gate[:, cols] * jax.nn.gelu(mixed)).astype(
                        jnp.bfloat16
                    )
                    if b == 0:
                        held[:, cols] = result
                    else:
                        sent[t, :, cols] = result
                        hop(t, p, j, c)

            return carry

        lax.fori_loop(0, here, step, 0)

    run_pass(0)
    for k in range(16):
        slot = (dev + 2 * k) % 32
        block = student_ref.at[slot]
        to_twin = copy(block, block, student_send.at[16 + k], student_recv.at[slot], twin)
        if k > 0:
            to_twin.wait_recv()
        start(to_twin)
    for k in range(16):
        slot = (dev + 2 * k) % 32 + 1 - 2 * core
        block = student_ref.at[slot]
        copy(block, block, student_send.at[0], student_recv.at[slot], twin).wait_recv()

    def own_cols(x):
        n = student_ref.shape[2]
        picked = x[:, 0:n]
        for k in range(1, 8):
            picked = jnp.where(sec == k, x[:, k * n : (k + 1) * n], picked)
        return picked

    root = math.sqrt(2.0 / math.pi)
    for n in range(4):
        latents = noise_ref[2 * n : 2 * n + 2].reshape(2 * rows, width).astype(jnp.float32)
        mean_sq = jnp.mean(latents * latents, axis=-1, keepdims=True)
        cond_row = cond[n]
        student_in = (
            latents * lax.rsqrt(mean_sq + 1e-06) * (1.0 + cond_row * student_mod_ref[0:1])
            + cond_row * student_mod_ref[1:2]
        ).astype(jnp.bfloat16)
        mixed = jnp.dot(
            student_in,
            student_ref[...].reshape(width, student_ref.shape[2]),
            preferred_element_type=jnp.float32,
        )
        bent = jnp.tanh(root * (mixed + 0.044715 * mixed * mixed * mixed))
        half = 0.5 * (1.0 + bent)
        bend = half + 0.5 * mixed * (1.0 - bent * bent) * root * (
            1.0 + 3.0 * 0.044715 * mixed * mixed
        )
        gate = own_cols(1.0 + cond_row * student_mod_ref[2:3])
        level = sched[0, n : n + 1, :1] / LEVELS
        z = own_cols(latents)
        moved = z - level * (z + gate * (mixed * half))
        slope[2 * n * rows : 2 * (n + 1) * rows] = -level * gate * bend
        student_rows[2 * n * rows : 2 * (n + 1) * rows] = student_in
        feat_part[2 * n : 2 * n + 2] = (
            jnp.dot(
                moved.astype(jnp.bfloat16),
                feature_shard_ref[...],
                preferred_element_type=jnp.float32,
            )
            .astype(jnp.bfloat16)
            .reshape(2, rows, -1)
        )

    slope_t[...] = slope[...].T

    def send_feat(k, slot):
        return copy(
            feat_part.at[k], feats.at[slot], feat_send.at[k], feat_recv.at[slot], at_section(k)
        )

    for k in range(1, 8):
        start(send_feat((sec + k) % 8, sec))
    for k in range(4):
        slot = ((sy + k) % 4) * 2 + sx
        block = feature_ref.at[slot]
        across = copy(
            block, block, feature_send.at[4 + k], feature_recv.at[slot], x_outer
        )
        if k > 0:
            across.wait_recv()
        start(across)

    run_pass(1)

    last_self = sec == 7
    first_self = sec == 0

    for c in range(chunks):
        pl.when(jnp.logical_not(last_self))(pass_on(0, 2 * here, c, twin).wait_recv)

    @pl.when(jnp.logical_not(first_self))
    def _():
        share_first(0).wait_recv()

    x2 = (
        first_x[...].astype(jnp.float32)
        + sched[1, pl.ds(4 + sec // 2, 1), :1] * inbox[2 * here].astype(jnp.float32)
    ).astype(jnp.bfloat16)
    teacher_ref[sec] = x2
    for k in range(4):
        slot = ((sy + k) % 4) * 2 + 1 - sx
        block = feature_ref.at[slot]
        copy(block, block, feature_send.at[0], feature_recv.at[slot], twin).wait_recv()

    sections = 8
    chips = summed.shape[0]
    piece = summed.shape[1]
    feat = feats.shape[2]
    chip = xl * 8 + zz

    def at_chip(q):
        return {"dp_x": q // 8, "dp_z": q % 8}

    def send_grad(k, slot):
        return copy(grads.at[slot], grads.at[slot], grad_send.at[k], grad_recv.at[slot], at_section(k))

    def send_piece(q, slot):
        return copy(summed.at[q], pieces.at[slot], piece_send.at[q], piece_recv.at[slot], at_chip(q))

    def send_final(q, slot):
        block = final.at[core, slot]
        return copy(block, block, final_send.at[q], final_recv.at[slot], at_chip(q))

    def send_twin(half, slot):
        block = final.at[half, slot]
        return copy(block, block, twin_send.at[slot], twin_recv.at[slot], twin)

    send_half = copy(half_out, half_in, half_send, half_recv, twin)

    def send_out(k, slot):
        return copy(teacher_ref.at[slot], teacher_ref.at[slot], out_send.at[k], out_recv.at[slot], at_section(k))

    feat_teacher = jnp.dot(
        x2, feature_ref[...].reshape(width, feat), preferred_element_type=jnp.float32
    )
    feat_student = feat_part[sec].astype(jnp.float32)
    for k in range(1, sections):
        other = (sec + k) % sections
        send_feat(other, other).wait_recv()
        feat_student = feat_student + feats[other].astype(jnp.float32)

    def unit(f):
        positive = jnp.maximum(f, 0.0)
        scale = lax.rsqrt(jnp.mean(positive * positive, axis=-1, keepdims=True) + 1e-06)
        return positive * scale, scale

    unit_s, scale_s = unit(feat_student)
    unit_t, _ = unit(feat_teacher)
    gap = unit_s - unit_t
    lin = lin_ref[...]
    dist_ref[...] = lax.dot_general(
        lin,
        gap * gap,
        (((1,), (1,)), ((), ())),
        preferred_element_type=jnp.float32,
        precision=lax.Precision.HIGHEST,
    )
    tokens = token_ref.shape[1]
    own_token = lax.broadcasted_iota(jnp.int32, (rows, tokens), 0) + sec * rows
    token_col = jnp.sum(
        jnp.where(
            lax.broadcasted_iota(jnp.int32, (rows, tokens), 1) == own_token, token_ref[...], 0.0
        ),
        axis=1,
        keepdims=True,
    )
    unit_grad = 2.0 * token_col * lin * gap
    mean_dot = jnp.mean(unit_grad * unit_s, axis=-1, keepdims=True)
    feat_grad = scale_s * (unit_grad - unit_s * mean_dot)
    grads[sec] = jnp.where(feat_student > 0.0, feat_grad, 0.0).astype(jnp.bfloat16)
    for k in range(1, sections):
        send_grad((sec + k) % sections, sec).start()
    for k in range(1, sections):
        other = (sec + k) % sections
        send_grad(other, other).wait_recv()

    out_grad = lax.dot_general(
        feature_ref[sec],
        grads[...].reshape(sections * rows, feat),
        (((1,), (1,)), ((), ())),
        preferred_element_type=jnp.float32,
    )
    mixed_grad = (out_grad * slope_t[...]).astype(jnp.bfloat16)
    product = jnp.dot(mixed_grad, student_rows[...], preferred_element_type=jnp.float32)
    lanes = 128
    blocks = width // lanes
    half_cols = product.shape[0] // 2
    for half in range(2):
        kept = product[half * half_cols : (half + 1) * half_cols]
        partial[half] = jnp.concatenate(
            [kept[:, b * lanes : (b + 1) * lanes] for b in range(blocks)], axis=0
        ).reshape(chips, piece, lanes)
    half_out[...] = partial[1 - core].astype(jnp.bfloat16)
    send_half.start()
    for k in range(1, sections):
        send_out((sec + k) % sections, sec).start()
    send_half.wait_recv()
    summed[...] = (partial[core] + half_in[...].astype(jnp.float32)).astype(jnp.bfloat16)
    for k in range(1, chips):
        send_piece((chip + k) % chips, chip).start()
    total = summed[chip].astype(jnp.float32)
    for k in range(1, chips):
        other = (chip + chips - k) % chips
        send_piece(other, other).wait_recv()
        total = total + pieces[other].astype(jnp.float32)
    final[core, chip] = total.astype(jnp.bfloat16)
    for k in range(1, chips):
        send_final((chip + k) % chips, chip).start()
    send_twin(core, chip).start()
    for k in range(1, chips):
        other = (chip + chips - k) % chips
        send_final(other, other).wait_recv()
        send_twin(core, other).start()
    for k in range(chips):
        other = (chip + chips - k) % chips
        send_twin(1 - core, other).wait_recv()
    for half in range(2):
        kept = final[half].astype(jnp.float32).reshape(blocks * half_cols, lanes)
        for b in range(blocks):
            grad_ref[half * half_cols : (half + 1) * half_cols, b * lanes : (b + 1) * lanes] = kept[
                b * half_cols : (b + 1) * half_cols
            ]

    for k in range(1, sections):
        other = (sec + k) % sections
        send_out(other, other).wait_recv()
        send_out(other, sec).wait_send()
    send_half.wait_send()
    for k in range(1, sections):
        send_grad((sec + k) % sections, sec).wait_send()
    for k in range(1, chips):
        send_piece((chip + k) % chips, chip).wait_send()
        send_final((chip + k) % chips, chip).wait_send()
    for k in range(chips):
        send_twin(core, k).wait_send()

    def drain(t, carry):
        for c in range(chunks):
            pass_on(t, t, c, twin).wait_send()
        return carry

    lax.fori_loop(0, 2 * here - 1, drain, 0)

    for c in range(chunks):
        pl.when(jnp.logical_not(last_self))(pass_on(2 * here - 1, 0, c, twin).wait_send)

    @pl.when(first_stage)
    def _():
        for j in range(1, here):
            share_first(j).wait_send()

        @pl.when(sx > 0)
        def _():
            share_first(0).wait_send()

    for what, when in started:
        if when is None:
            what.wait_send()
        else:
            pl.when(when)(what.wait_send)


def run_train(
    noise,
    ids,
    sched,
    frequency,
    time_weight,
    block,
    block_mod,
    student_shard,
    feature_shard,
    student_mod,
    lin,
    token,
    table,
):
    mbs, rows, width = noise.shape
    vocab = table.shape[0]
    piece = block.shape[0]
    cols = student_shard.shape[1]
    feat_rows, feat = feature_shard.shape
    part = cols * width // (32 * 128)
    vmem = pl.BlockSpec(memory_space=pltpu.VMEM)
    dma = pltpu.SemaphoreType.DMA
    bf16 = jnp.bfloat16
    f32 = jnp.float32
    return pl.pallas_call(
        train_kernel,
        out_shape=(
            jax.ShapeDtypeStruct((mbs, rows, width), bf16),
            jax.ShapeDtypeStruct((1, rows), f32),
            jax.ShapeDtypeStruct((cols, width), f32),
        ),
        in_specs=[vmem] * 12 + [pl.BlockSpec(memory_space=pl.ANY)],
        out_specs=(vmem,) * 3,
        scratch_shapes=[
            pltpu.VMEM((128, ids.shape[1]), f32),
            pltpu.VMEM((vocab, width), bf16),
            pltpu.VMEM((2, 32, piece, width), bf16),
            pltpu.VMEM((2, 3, 1, width), f32),
            pltpu.VMEM((16, 1, width), f32),
            pltpu.VMEM((32, 1, width), f32),
            pltpu.VMEM((8, 1, width), f32),
            pltpu.VMEM((2, 8, 128), f32),
            pltpu.VMEM((8, 1, width), f32),
            pltpu.VMEM((rows, width), bf16),
            pltpu.VMEM((mbs, rows, width), bf16),
            pltpu.VMEM((mbs + 1, rows, width), bf16),
            pltpu.VMEM((mbs // 2, rows, width), bf16),
            pltpu.VMEM((rows, width), bf16),
            pltpu.VMEM((32, piece, cols), bf16),
            pltpu.VMEM((8, feat_rows, feat), bf16),
            pltpu.VMEM((mbs * rows, width), bf16),
            pltpu.VMEM((mbs * rows, cols), f32),
            pltpu.VMEM((cols, mbs * rows), f32),
            pltpu.VMEM((8, rows, feat), bf16),
            pltpu.VMEM((8, rows, feat), bf16),
            pltpu.VMEM((8, rows, feat), bf16),
            pltpu.VMEM((2, 16, part, 128), f32),
            pltpu.VMEM((16, part, 128), bf16),
            pltpu.VMEM((16, part, 128), bf16),
            pltpu.VMEM((16, part, 128), bf16),
            pltpu.VMEM((16, part, 128), bf16),
            pltpu.VMEM((2, 16, part, 128), bf16),
            dma,
            dma((129,)),
            dma((32,)),
            dma((32,)),
            dma((32,)),
            dma((8,)),
            dma((8,)),
            dma((32,)),
            dma((32,)),
            dma(((mbs + 1) * 3,)),
            dma((mbs * 3,)),
            dma((mbs // 2,)),
            dma,
            dma((32,)),
            dma((32,)),
            dma((8,)),
            dma((8,)),
            dma,
            dma,
            dma((8,)),
            dma((8,)),
            dma((8,)),
            dma((8,)),
            dma,
            dma,
            dma((16,)),
            dma((16,)),
            dma((16,)),
            dma((16,)),
            dma((16,)),
            dma((16,)),
            dma((8,)),
            dma((8,)),
        ],
        compiler_params=pltpu.CompilerParams(
            collective_id=0, has_side_effects=True, vmem_limit_bytes=56 * 1024 * 1024
        ),
    )(
        noise,
        ids,
        sched,
        frequency,
        time_weight,
        block,
        block_mod,
        student_shard,
        feature_shard,
        student_mod,
        lin,
        token,
        table,
    )


def local(
    noise,
    sched_index,
    text_ids,
    text_table,
    time_weight,
    block_weight,
    block_mod,
    student_weight,
    student_mod,
    feature_weight,
    lin_weight,
    token_weight,
):
    batches, tokens, model_width = noise.shape
    sections = lax.axis_size(SECTION)
    row_count = batches * tokens
    share_rows = row_count // sections
    half_freq = time_weight.shape[0] // 2
    frequency = np.exp(-math.log(10000.0) * np.arange(half_freq, dtype=np.float32) / half_freq)
    teacher, token_distance, student_grad = run_train(
        noise.reshape(sections, share_rows, model_width),
        text_ids.T,
        sched_index,
        jnp.asarray(frequency[None, :], jnp.float32),
        time_weight,
        block_weight[0],
        jnp.moveaxis(block_mod, 0, 1),
        student_weight,
        feature_weight,
        student_mod,
        lin_weight[None, :],
        token_weight[None, :],
        text_table,
    )
    return (
        teacher.reshape(noise.shape),
        student_grad.T,
        token_distance.reshape(share_rows),
    )


def solution(mesh):
    torus = Mesh(mesh.devices.reshape(2, 8, 2, 4, 2), DP + SECTION)
    in_specs = (
        P(DP, None, None),
        P(DP, None),
        P(),
        P(DP, None),
        P(),
        P(SECTION, DP, None),
        P(SECTION, None, None),
        P(DP, SECTION),
        P(),
        P(SECTION, None),
        P(),
        P(DP),
    )
    out_specs = (P(DP, None, None), P(None, SECTION), P(DP + SECTION))
    return jax.shard_map(local, mesh=torus, in_specs=in_specs, out_specs=out_specs, check_vma=False)
```

```python
import math

import jax
import jax.numpy as jnp
import numpy as np
from jax import lax
from jax.experimental import pallas as pl
from jax.experimental.pallas import tpu as pltpu
from jax.sharding import Mesh
from jax.sharding import PartitionSpec as P

LEVELS = 1000
DP = ("dp_x", "dp_z", "dp_c")
SECTION = ("sec_y", "sec_x")
MESH = pl.DeviceIdType.MESH


def train_kernel(
    noise_ref,
    ids_ref,
    sched_ref,
    frequency_ref,
    time_weight_ref,
    block_ref,
    block_mod_ref,
    student_shard_ref,
    feature_shard_ref,
    student_mod_ref,
    lin_ref,
    token_ref,
    table_ref,
    teacher_ref,
    dist_ref,
    grad_ref,
    ids,
    table,
    weight,
    mods,
    rows_out,
    rows_in,
    pooled,
    sched,
    cond,
    held,
    sent,
    inbox,
    start_x,
    first_x,
    student_ref,
    feature_ref,
    student_rows,
    slope,
    slope_t,
    feat_part,
    feats,
    grads,
    partial,
    half_out,
    half_in,
    summed,
    pieces,
    final,
    table_sem,
    weight_send,
    weight_recv,
    row_send,
    row_recv,
    pooled_send,
    pooled_recv,
    lend_send,
    lend_recv,
    inbox_recv,
    sent_send,
    first_send,
    first_recv,
    student_send,
    student_recv,
    feature_send,
    feature_recv,
    mods_send,
    mods_recv,
    feat_send,
    feat_recv,
    grad_send,
    grad_recv,
    half_send,
    half_recv,
    piece_send,
    piece_recv,
    final_send,
    final_recv,
    twin_send,
    twin_recv,
    out_send,
    out_recv,
):
    mbs, rows, width = noise_ref.shape
    chunk = 512
    chunks = width // chunk
    xl = lax.axis_index("dp_x")
    zz = lax.axis_index("dp_z")
    core = lax.axis_index("dp_c")
    sy = lax.axis_index("sec_y")
    sx = lax.axis_index("sec_x")
    sec = sy * 2 + sx
    dev = xl * 16 + zz * 2 + core
    twin = {"dp_c": 1 - core}

    def at_section(k):
        return {"sec_y": k // 2, "sec_x": k % 2}

    def at_dp(k):
        return {"dp_x": k // 16, "dp_z": (k // 2) % 8, "dp_c": k % 2}

    load_table = pltpu.make_async_copy(table_ref, table, table_sem)
    load_table.start()

    barrier = pltpu.get_barrier_semaphore()

    def greet(where):
        pl.semaphore_signal(barrier, inc=1, device_id=where, device_id_type=MESH)

    for k in range(1, 8):
        greet(at_section((sec + k) % 8))
    for k in range(1, 32):
        greet(at_dp((dev + k) % 32))
    greet({"sec_x": 1 - sx, "dp_x": 1 - xl})
    levels = [
        jnp.broadcast_to(sched_ref[:, r : r + 1].astype(jnp.float32), (4, 128)) for r in range(3)
    ]
    for r in range(2):
        sched[0, 4 * r : 4 * r + 4] = levels[r]
        sched[1, 4 * r : 4 * r + 4] = (levels[r + 1] - levels[r]) / LEVELS
    angles = sched[0] * frequency_ref[...]
    embedding = jnp.concatenate([jnp.cos(angles), jnp.sin(angles)], axis=-1)
    embed = jnp.dot(
        embedding.astype(jnp.bfloat16), time_weight_ref[...], preferred_element_type=jnp.float32
    )
    pl.semaphore_wait(barrier, 39)

    def copy(src, dst, send, recv, where):
        return pltpu.make_async_remote_copy(
            src_ref=src,
            dst_ref=dst,
            send_sem=send,
            recv_sem=recv,
            device_id=where,
            device_id_type=MESH,
        )

    started = []

    def start(what, when=None):
        started.append((what, when))
        if when is None:
            what.start()
        else:
            pl.when(when)(what.start)

    source = sx == core
    relay = sx != core

    def piece_a(a, z):
        return a * 16 + (z % 8) * 2 + core

    def piece_b(a, z):
        return a * 16 + (z % 8) * 2 + 1 - core

    z_up = {"dp_z": (zz + 1) % 8}
    z_down = {"dp_z": (zz + 7) % 8}
    x_mate = {"dp_x": 1 - xl}
    x_outer = {"dp_x": 1 - xl, "sec_x": 1 - sx}
    way = {0: z_up, 1: z_down, 2: x_mate, 3: x_outer}

    def go(p, towards, when=None):
        block = weight.at[core, p]
        start(
            copy(block, block, weight_send.at[p * 4 + towards], weight_recv.at[p], way[towards]),
            when,
        )

    def lend(p, when=None):
        block = weight.at[core, p]
        start(copy(block, block, lend_send.at[p], lend_recv.at[p], twin), when)

    def arrive(p, when=None):
        block = weight.at[core, p]
        landed = copy(block, block, weight_send.at[p], weight_recv.at[p], twin)
        if when is None:
            landed.wait_recv()
        else:
            pl.when(when)(landed.wait_recv)
        lend(p, when)

    mods[sx] = block_mod_ref[...]
    lend_mods = copy(block_mod_ref, mods.at[sx], mods_send, mods_recv, x_outer)
    start(lend_mods)

    @pl.when(source)
    def _():
        weight[core, dev] = block_ref[...]

    own_shard = copy(
        block_ref, weight.at[1 - core, dev], weight_send.at[128], weight_recv.at[dev], twin
    )
    start(own_shard, relay)
    for towards in (2, 3, 0, 1):
        go(piece_a(xl, zz), towards, source)
    lend(piece_a(xl, zz), source)

    first_stage = sy == 0

    for k in range(1, 4):
        start(
            copy(
                feature_shard_ref,
                feature_ref.at[sec],
                feature_send.at[k],
                feature_recv.at[sec],
                {"sec_y": (sy + k) % 4},
            )
        )
    feature_ref[sec] = feature_shard_ref[...]

    arrive(piece_b(xl, zz), source)

    go(piece_b(xl, zz), 0, source)
    go(piece_b(xl, zz), 1, source)
    go(piece_b(xl, zz), 2, source)
    go(piece_b(xl, zz), 3, source)

    arrive_a = piece_a(1 - xl, zz)
    arrive(arrive_a)
    go(arrive_a, 2, relay)

    go(arrive_a, 0)
    go(arrive_a, 1)

    arrive(piece_a(xl, zz), relay)

    go(piece_a(xl, zz), 0, relay)
    go(piece_a(xl, zz), 1, relay)

    vocab = table.shape[0]
    text_len, samples = ids_ref.shape
    ids[...] = jnp.zeros_like(ids)
    ids[0:text_len] = ids_ref[...].astype(jnp.float32)
    by_sample = ids[...].T.reshape(samples // 8, 8, -1)
    place = lax.broadcasted_iota(jnp.int32, by_sample.shape, 1)
    own_ids = jnp.sum(jnp.where(place == sec, by_sample, 0.0), axis=1)
    local_ids = own_ids.astype(jnp.int32) - dev * vocab
    lanes = lax.broadcasted_iota(jnp.int32, (samples // 8, vocab), 1)
    counts = jnp.zeros(lanes.shape, jnp.float32)
    for t in range(text_len):
        counts = counts + jnp.where(local_ids[:, t : t + 1] == lanes, 1.0, 0.0)
    load_table.wait()
    part = jnp.dot(
        counts.astype(jnp.bfloat16), table[...], preferred_element_type=jnp.float32
    ) / text_len
    for g in range(16):
        rows_out[g] = part[g : g + 1]
    rows_in[dev] = rows_out[dev // 2]
    for k in range(1, 32):
        other = (dev + k) % 32
        start(
            copy(
                rows_out.at[other // 2],
                rows_in.at[dev],
                row_send.at[k],
                row_recv.at[dev],
                at_dp(other),
            )
        )

    def take_x(z):
        p = piece_b(1 - xl, z)
        arrive(p)
        odd = z % 2
        go(p, 3, source & (odd == 1))
        go(p, 2, relay & (odd == 0))

    def take_z_b(k, up):
        z = zz + 8 - k if up else zz + k
        p = piece_b(xl, z)
        last = k == 4
        here = source & (xl == (0 if up else 1)) if last else source

        arrive(p, here)

        if k < 3:
            go(p, 0 if up else 1, here)
        elif k == 3:
            go(p, 0 if up else 1, source & (xl == (0 if up else 1)))
        go(p, 2, here)
        go(p, 3, here)

    def take_z_a(k, up):
        z = zz + 8 - k if up else zz + k
        for a in range(2):
            reach = (4 - a) if up else (3 + a)
            if k <= reach:
                p = piece_a(a, z)
                arrive(p)
                if k < reach:
                    go(p, 0 if up else 1)

    def ring_step(k):
        for up in (True, False):
            take_z_b(k, up)
        for up in (True, False):
            take_z_a(k, up)
        if k == 1:
            take_x(zz)
        else:
            take_x(zz + 9 - k)
            take_x(zz + k - 1)

    ring_step(1)

    ring_step(2)
    total = rows_in[dev]
    for k in range(1, 32):
        other = (dev + 32 - k) % 32
        copy(
            rows_out.at[0], rows_in.at[other], row_send.at[k], row_recv.at[other], at_dp(other)
        ).wait_recv()
        total = total + rows_in[other]
    pooled[sec] = total
    for k in range(1, 8):
        start(
            copy(
                pooled.at[sec],
                pooled.at[sec],
                pooled_send.at[k],
                pooled_recv.at[sec],
                at_section((sec + k) % 8),
            )
        )
    ring_step(3)
    ring_step(4)
    for k in range(1, 8):
        other = (sec + k) % 8
        copy(
            pooled.at[other],
            pooled.at[other],
            pooled_send.at[k],
            pooled_recv.at[other],
            at_section(other),
        ).wait_recv()
    for r in range(8):
        cond[r] = jax.nn.silu(embed[r : r + 1] + pooled[core * 4 + r % 4])
    take_x(zz + 4)

    for z in range(8):
        arrive(piece_b(xl, z), relay)

    student_ref[dev] = student_shard_ref[...]
    for k in range(1, 16):
        start(
            copy(
                student_shard_ref,
                student_ref.at[dev],
                student_send.at[k],
                student_recv.at[dev],
                at_dp((dev + 2 * k) % 32),
            )
        )
    copy(block_mod_ref, mods.at[1 - sx], mods_send, mods_recv, x_outer).wait_recv()
    for p in range(32):
        block = weight.at[1 - core, p]
        copy(block, block, lend_send.at[p], lend_recv.at[p], twin).wait_recv()

    def pass_on(t, slot, c, where):
        cols = pl.ds(c * chunk, chunk)
        return copy(
            sent.at[t, :, cols],
            inbox.at[slot, :, cols],
            sent_send.at[t * chunks + c],
            inbox_recv.at[slot * chunks + c],
            where,
        )

    here = mbs // 2

    def hop(t, p, j, c):
        @pl.when(sy < 3)
        def _():
            pass_on(t, t, c, {"sec_y": (sy + 1) % 4}).start()

        @pl.when(sy == 3)
        def _():
            if p == 0:
                pass_on(t, t + here, c, {"sec_y": 0}).start()
            else:

                @pl.when((sx == 1) & (j == here - 1))
                def _():
                    cols = slice(c * chunk, (c + 1) * chunk)
                    inbox[2 * here, :, cols] = sent[t, :, cols]

                @pl.when((sx == 0) | (j < here - 1))
                def _():
                    pass_on(t, 2 * here, c, at_section(sx * here + j)).start()

    def share_first(j):
        return copy(
            start_x.at[j], first_x, first_send.at[j], first_recv, at_section(sx * here + j)
        )

    def run_pass(p):
        def step(j, carry):
            t = p * here + j
            sample = (sx * here + j) // 2
            for c in range(chunks):
                arrived = pass_on(t, t, c, twin)
                if p == 0:
                    pl.when(sy > 0)(arrived.wait_recv)
                else:
                    arrived.wait_recv()
            if p == 0:

                @pl.when(first_stage)
                def _():
                    held[...] = noise_ref[sx * here + j]

                @pl.when(sy > 0)
                def _():
                    held[...] = inbox[t]

            else:
                held[...] = inbox[t]

                @pl.when(first_stage)
                def _():
                    moved = (
                        noise_ref[sx * here + j].astype(jnp.float32)
                        + sched[1, pl.ds(sample, 1), :1] * held[...].astype(jnp.float32)
                    ).astype(jnp.bfloat16)
                    held[...] = moved
                    start_x[j] = moved

                    @pl.when((j == 0) & (sx == 0))
                    def _():
                        first_x[...] = moved

                    @pl.when((j > 0) | (sx > 0))
                    def _():
                        share_first(j).start()

            cond_row = cond[p * 4 + sample]
            for b in range(2):
                hidden = held[...].astype(jnp.float32)
                mean_sq = jnp.mean(hidden * hidden, axis=-1, keepdims=True)
                inputs = (
                    hidden * lax.rsqrt(mean_sq + 1e-06) * (1.0 + cond_row * mods[b, 0])
                    + cond_row * mods[b, 1]
                ).astype(jnp.bfloat16)
                gate = 1.0 + cond_row * mods[b, 2]
                for c in range(chunks):
                    cols = slice(c * chunk, (c + 1) * chunk)
                    mixed = jnp.dot(
                        inputs,
                        weight[b, :, :, cols].reshape(width, chunk),
                        preferred_element_type=jnp.float32,
                    )
                    result = (hidden[:, cols] + gate[:, cols] * jax.nn.gelu(mixed)).astype(
                        jnp.bfloat16
                    )
                    if b == 0:
                        held[:, cols] = result
                    else:
                        sent[t, :, cols] = result
                        hop(t, p, j, c)

            return carry

        lax.fori_loop(0, here, step, 0)

    for k in range(4):
        slot = ((sy + k) % 4) * 2 + sx
        block = feature_ref.at[slot]
        across = copy(
            block, block, feature_send.at[4 + k], feature_recv.at[slot], x_outer
        )
        if k > 0:
            across.wait_recv()
        start(across)

    run_pass(0)
    for k in range(16):
        slot = (dev + 2 * k) % 32
        block = student_ref.at[slot]
        to_twin = copy(block, block, student_send.at[16 + k], student_recv.at[slot], twin)
        if k > 0:
            to_twin.wait_recv()
        start(to_twin)
    for k in range(16):
        slot = (dev + 2 * k) % 32 + 1 - 2 * core
        block = student_ref.at[slot]
        copy(block, block, student_send.at[0], student_recv.at[slot], twin).wait_recv()

    def own_cols(x):
        n = student_ref.shape[2]
        picked = x[:, 0:n]
        for k in range(1, 8):
            picked = jnp.where(sec == k, x[:, k * n : (k + 1) * n], picked)
        return picked

    root = math.sqrt(2.0 / math.pi)
    for n in range(4):
        latents = noise_ref[2 * n : 2 * n + 2].reshape(2 * rows, width).astype(jnp.float32)
        mean_sq = jnp.mean(latents * latents, axis=-1, keepdims=True)
        cond_row = cond[n]
        student_in = (
            latents * lax.rsqrt(mean_sq + 1e-06) * (1.0 + cond_row * student_mod_ref[0:1])
            + cond_row * student_mod_ref[1:2]
        ).astype(jnp.bfloat16)
        mixed = jnp.dot(
            student_in,
            student_ref[...].reshape(width, student_ref.shape[2]),
            preferred_element_type=jnp.float32,
        )
        bent = jnp.tanh(root * (mixed + 0.044715 * mixed * mixed * mixed))
        half = 0.5 * (1.0 + bent)
        bend = half + 0.5 * mixed * (1.0 - bent * bent) * root * (
            1.0 + 3.0 * 0.044715 * mixed * mixed
        )
        gate = own_cols(1.0 + cond_row * student_mod_ref[2:3])
        level = sched[0, n : n + 1, :1] / LEVELS
        z = own_cols(latents)
        moved = z - level * (z + gate * (mixed * half))
        slope[2 * n * rows : 2 * (n + 1) * rows] = -level * gate * bend
        student_rows[2 * n * rows : 2 * (n + 1) * rows] = student_in
        feat_part[2 * n : 2 * n + 2] = (
            jnp.dot(
                moved.astype(jnp.bfloat16),
                feature_shard_ref[...],
                preferred_element_type=jnp.float32,
            )
            .astype(jnp.bfloat16)
            .reshape(2, rows, -1)
        )

    slope_t[...] = slope[...].T

    def send_feat(k, slot):
        return copy(
            feat_part.at[k], feats.at[slot], feat_send.at[k], feat_recv.at[slot], at_section(k)
        )

    for k in range(1, 8):
        start(send_feat((sec + k) % 8, sec))
    run_pass(1)

    last_self = sec == 7
    first_self = sec == 0

    for c in range(chunks):
        pl.when(jnp.logical_not(last_self))(pass_on(0, 2 * here, c, twin).wait_recv)

    @pl.when(jnp.logical_not(first_self))
    def _():
        share_first(0).wait_recv()

    x2 = (
        first_x[...].astype(jnp.float32)
        + sched[1, pl.ds(4 + sec // 2, 1), :1] * inbox[2 * here].astype(jnp.float32)
    ).astype(jnp.bfloat16)
    teacher_ref[sec] = x2
    for k in range(4):
        slot = ((sy + k) % 4) * 2 + 1 - sx
        block = feature_ref.at[slot]
        copy(block, block, feature_send.at[0], feature_recv.at[slot], twin).wait_recv()

    sections = 8
    chips = summed.shape[0]
    piece = summed.shape[1]
    feat = feats.shape[2]
    chip = xl * 8 + zz

    def at_chip(q):
        return {"dp_x": q // 8, "dp_z": q % 8}

    def send_grad(k, slot):
        return copy(grads.at[slot], grads.at[slot], grad_send.at[k], grad_recv.at[slot], at_section(k))

    def send_piece(q, slot):
        return copy(summed.at[q], pieces.at[slot], piece_send.at[q], piece_recv.at[slot], at_chip(q))

    def send_final(q, slot):
        block = final.at[core, slot]
        return copy(block, block, final_send.at[q], final_recv.at[slot], at_chip(q))

    def send_twin(half, slot):
        block = final.at[half, slot]
        return copy(block, block, twin_send.at[slot], twin_recv.at[slot], twin)

    send_half = copy(half_out, half_in, half_send, half_recv, twin)

    def send_out(k, slot):
        return copy(teacher_ref.at[slot], teacher_ref.at[slot], out_send.at[k], out_recv.at[slot], at_section(k))

    feat_teacher = jnp.dot(
        x2, feature_ref[...].reshape(width, feat), preferred_element_type=jnp.float32
    )
    feat_student = feat_part[sec].astype(jnp.float32)
    for k in range(1, sections):
        other = (sec + k) % sections
        send_feat(other, other).wait_recv()
        feat_student = feat_student + feats[other].astype(jnp.float32)

    def unit(f):
        positive = jnp.maximum(f, 0.0)
        scale = lax.rsqrt(jnp.mean(positive * positive, axis=-1, keepdims=True) + 1e-06)
        return positive * scale, scale

    unit_s, scale_s = unit(feat_student)
    unit_t, _ = unit(feat_teacher)
    gap = unit_s - unit_t
    lin = lin_ref[...]
    dist_ref[...] = lax.dot_general(
        lin,
        gap * gap,
        (((1,), (1,)), ((), ())),
        preferred_element_type=jnp.float32,
        precision=lax.Precision.HIGHEST,
    )
    tokens = token_ref.shape[1]
    own_token = lax.broadcasted_iota(jnp.int32, (rows, tokens), 0) + sec * rows
    token_col = jnp.sum(
        jnp.where(
            lax.broadcasted_iota(jnp.int32, (rows, tokens), 1) == own_token, token_ref[...], 0.0
        ),
        axis=1,
        keepdims=True,
    )
    unit_grad = 2.0 * token_col * lin * gap
    mean_dot = jnp.mean(unit_grad * unit_s, axis=-1, keepdims=True)
    feat_grad = scale_s * (unit_grad - unit_s * mean_dot)
    grads[sec] = jnp.where(feat_student > 0.0, feat_grad, 0.0).astype(jnp.bfloat16)
    for k in range(1, sections):
        send_grad((sec + k) % sections, sec).start()
    for k in range(1, sections):
        other = (sec + k) % sections
        send_grad(other, other).wait_recv()

    out_grad = lax.dot_general(
        feature_ref[sec],
        grads[...].reshape(sections * rows, feat),
        (((1,), (1,)), ((), ())),
        preferred_element_type=jnp.float32,
    )
    mixed_grad = (out_grad * slope_t[...]).astype(jnp.bfloat16)
    product = jnp.dot(mixed_grad, student_rows[...], preferred_element_type=jnp.float32)
    lanes = 128
    blocks = width // lanes
    half_cols = product.shape[0] // 2
    for half in range(2):
        kept = product[half * half_cols : (half + 1) * half_cols]
        partial[half] = jnp.concatenate(
            [kept[:, b * lanes : (b + 1) * lanes] for b in range(blocks)], axis=0
        ).reshape(chips, piece, lanes)
    half_out[...] = partial[1 - core].astype(jnp.bfloat16)
    send_half.start()
    for k in range(1, sections):
        send_out((sec + k) % sections, sec).start()
    send_half.wait_recv()
    summed[...] = (partial[core] + half_in[...].astype(jnp.float32)).astype(jnp.bfloat16)
    for k in range(1, chips):
        send_piece((chip + k) % chips, chip).start()
    total = summed[chip].astype(jnp.float32)
    for k in range(1, chips):
        other = (chip + chips - k) % chips
        send_piece(other, other).wait_recv()
        total = total + pieces[other].astype(jnp.float32)
    final[core, chip] = total.astype(jnp.bfloat16)
    for k in range(1, chips):
        send_final((chip + k) % chips, chip).start()
    send_twin(core, chip).start()
    for k in range(1, chips):
        other = (chip + chips - k) % chips
        send_final(other, other).wait_recv()
        send_twin(core, other).start()
    for k in range(chips):
        other = (chip + chips - k) % chips
        send_twin(1 - core, other).wait_recv()
    for half in range(2):
        kept = final[half].astype(jnp.float32).reshape(blocks * half_cols, lanes)
        for b in range(blocks):
            grad_ref[half * half_cols : (half + 1) * half_cols, b * lanes : (b + 1) * lanes] = kept[
                b * half_cols : (b + 1) * half_cols
            ]

    for k in range(1, sections):
        other = (sec + k) % sections
        send_out(other, other).wait_recv()
        send_out(other, sec).wait_send()
    send_half.wait_send()
    for k in range(1, sections):
        send_grad((sec + k) % sections, sec).wait_send()
    for k in range(1, chips):
        send_piece((chip + k) % chips, chip).wait_send()
        send_final((chip + k) % chips, chip).wait_send()
    for k in range(chips):
        send_twin(core, k).wait_send()

    def drain(t, carry):
        for c in range(chunks):
            pass_on(t, t, c, twin).wait_send()
        return carry

    lax.fori_loop(0, 2 * here - 1, drain, 0)

    for c in range(chunks):
        pl.when(jnp.logical_not(last_self))(pass_on(2 * here - 1, 0, c, twin).wait_send)

    @pl.when(first_stage)
    def _():
        for j in range(1, here):
            share_first(j).wait_send()

        @pl.when(sx > 0)
        def _():
            share_first(0).wait_send()

    for what, when in started:
        if when is None:
            what.wait_send()
        else:
            pl.when(when)(what.wait_send)


def run_train(
    noise,
    ids,
    sched,
    frequency,
    time_weight,
    block,
    block_mod,
    student_shard,
    feature_shard,
    student_mod,
    lin,
    token,
    table,
):
    mbs, rows, width = noise.shape
    vocab = table.shape[0]
    piece = block.shape[0]
    cols = student_shard.shape[1]
    feat_rows, feat = feature_shard.shape
    part = cols * width // (32 * 128)
    vmem = pl.BlockSpec(memory_space=pltpu.VMEM)
    dma = pltpu.SemaphoreType.DMA
    bf16 = jnp.bfloat16
    f32 = jnp.float32
    return pl.pallas_call(
        train_kernel,
        out_shape=(
            jax.ShapeDtypeStruct((mbs, rows, width), bf16),
            jax.ShapeDtypeStruct((1, rows), f32),
            jax.ShapeDtypeStruct((cols, width), f32),
        ),
        in_specs=[vmem] * 12 + [pl.BlockSpec(memory_space=pl.ANY)],
        out_specs=(vmem,) * 3,
        scratch_shapes=[
            pltpu.VMEM((128, ids.shape[1]), f32),
            pltpu.VMEM((vocab, width), bf16),
            pltpu.VMEM((2, 32, piece, width), bf16),
            pltpu.VMEM((2, 3, 1, width), f32),
            pltpu.VMEM((16, 1, width), f32),
            pltpu.VMEM((32, 1, width), f32),
            pltpu.VMEM((8, 1, width), f32),
            pltpu.VMEM((2, 8, 128), f32),
            pltpu.VMEM((8, 1, width), f32),
            pltpu.VMEM((rows, width), bf16),
            pltpu.VMEM((mbs, rows, width), bf16),
            pltpu.VMEM((mbs + 1, rows, width), bf16),
            pltpu.VMEM((mbs // 2, rows, width), bf16),
            pltpu.VMEM((rows, width), bf16),
            pltpu.VMEM((32, piece, cols), bf16),
            pltpu.VMEM((8, feat_rows, feat), bf16),
            pltpu.VMEM((mbs * rows, width), bf16),
            pltpu.VMEM((mbs * rows, cols), f32),
            pltpu.VMEM((cols, mbs * rows), f32),
            pltpu.VMEM((8, rows, feat), bf16),
            pltpu.VMEM((8, rows, feat), bf16),
            pltpu.VMEM((8, rows, feat), bf16),
            pltpu.VMEM((2, 16, part, 128), f32),
            pltpu.VMEM((16, part, 128), bf16),
            pltpu.VMEM((16, part, 128), bf16),
            pltpu.VMEM((16, part, 128), bf16),
            pltpu.VMEM((16, part, 128), bf16),
            pltpu.VMEM((2, 16, part, 128), bf16),
            dma,
            dma((129,)),
            dma((32,)),
            dma((32,)),
            dma((32,)),
            dma((8,)),
            dma((8,)),
            dma((32,)),
            dma((32,)),
            dma(((mbs + 1) * 3,)),
            dma((mbs * 3,)),
            dma((mbs // 2,)),
            dma,
            dma((32,)),
            dma((32,)),
            dma((8,)),
            dma((8,)),
            dma,
            dma,
            dma((8,)),
            dma((8,)),
            dma((8,)),
            dma((8,)),
            dma,
            dma,
            dma((16,)),
            dma((16,)),
            dma((16,)),
            dma((16,)),
            dma((16,)),
            dma((16,)),
            dma((8,)),
            dma((8,)),
        ],
        compiler_params=pltpu.CompilerParams(
            collective_id=0, has_side_effects=True, vmem_limit_bytes=56 * 1024 * 1024
        ),
    )(
        noise,
        ids,
        sched,
        frequency,
        time_weight,
        block,
        block_mod,
        student_shard,
        feature_shard,
        student_mod,
        lin,
        token,
        table,
    )


def local(
    noise,
    sched_index,
    text_ids,
    text_table,
    time_weight,
    block_weight,
    block_mod,
    student_weight,
    student_mod,
    feature_weight,
    lin_weight,
    token_weight,
):
    batches, tokens, model_width = noise.shape
    sections = lax.axis_size(SECTION)
    row_count = batches * tokens
    share_rows = row_count // sections
    half_freq = time_weight.shape[0] // 2
    frequency = np.exp(-math.log(10000.0) * np.arange(half_freq, dtype=np.float32) / half_freq)
    teacher, token_distance, student_grad = run_train(
        noise.reshape(sections, share_rows, model_width),
        text_ids.T,
        sched_index,
        jnp.asarray(frequency[None, :], jnp.float32),
        time_weight,
        block_weight[0],
        jnp.moveaxis(block_mod, 0, 1),
        student_weight,
        feature_weight,
        student_mod,
        lin_weight[None, :],
        token_weight[None, :],
        text_table,
    )
    return (
        teacher.reshape(noise.shape),
        student_grad.T,
        token_distance.reshape(share_rows),
    )


def solution(mesh):
    torus = Mesh(mesh.devices.reshape(2, 8, 2, 4, 2), DP + SECTION)
    in_specs = (
        P(DP, None, None),
        P(DP, None),
        P(),
        P(DP, None),
        P(),
        P(SECTION, DP, None),
        P(SECTION, None, None),
        P(DP, SECTION),
        P(),
        P(SECTION, None),
        P(),
        P(DP),
    )
    out_specs = (P(DP, None, None), P(None, SECTION), P(DP + SECTION))
    return jax.shard_map(local, mesh=torus, in_specs=in_specs, out_specs=out_specs, check_vma=False)
```

```python
import math

import jax
import jax.numpy as jnp
import numpy as np
from jax import lax
from jax.experimental import pallas as pl
from jax.experimental.pallas import tpu as pltpu
from jax.sharding import Mesh
from jax.sharding import PartitionSpec as P

LEVELS = 1000
DP = ("dp_x", "dp_z", "dp_c")
SECTION = ("sec_y", "sec_x")
MESH = pl.DeviceIdType.MESH


def train_kernel(
    noise_ref,
    ids_ref,
    sched_ref,
    frequency_ref,
    time_weight_ref,
    block_ref,
    block_mod_ref,
    student_shard_ref,
    feature_shard_ref,
    student_mod_ref,
    lin_ref,
    token_ref,
    table_ref,
    teacher_ref,
    dist_ref,
    grad_ref,
    ids,
    table,
    weight,
    mods,
    rows_out,
    rows_in,
    pooled,
    sched,
    cond,
    held,
    sent,
    inbox,
    start_x,
    first_x,
    student_ref,
    feature_ref,
    student_rows,
    slope,
    slope_t,
    feat_part,
    feats,
    grads,
    partial,
    half_out,
    half_in,
    summed,
    pieces,
    final,
    table_sem,
    weight_send,
    weight_recv,
    row_send,
    row_recv,
    pooled_send,
    pooled_recv,
    lend_send,
    lend_recv,
    inbox_recv,
    sent_send,
    first_send,
    first_recv,
    student_send,
    student_recv,
    feature_send,
    feature_recv,
    mods_send,
    mods_recv,
    feat_send,
    feat_recv,
    grad_send,
    grad_recv,
    half_send,
    half_recv,
    piece_send,
    piece_recv,
    final_send,
    final_recv,
    twin_send,
    twin_recv,
    out_send,
    out_recv,
):
    mbs, rows, width = noise_ref.shape
    chunk = 256
    chunks = width // chunk
    xl = lax.axis_index("dp_x")
    zz = lax.axis_index("dp_z")
    core = lax.axis_index("dp_c")
    sy = lax.axis_index("sec_y")
    sx = lax.axis_index("sec_x")
    sec = sy * 2 + sx
    dev = xl * 16 + zz * 2 + core
    twin = {"dp_c": 1 - core}

    def at_section(k):
        return {"sec_y": k // 2, "sec_x": k % 2}

    def at_dp(k):
        return {"dp_x": k // 16, "dp_z": (k // 2) % 8, "dp_c": k % 2}

    load_table = pltpu.make_async_copy(table_ref, table, table_sem)
    load_table.start()

    barrier = pltpu.get_barrier_semaphore()

    def greet(where):
        pl.semaphore_signal(barrier, inc=1, device_id=where, device_id_type=MESH)

    for k in range(1, 8):
        greet(at_section((sec + k) % 8))
    for k in range(1, 32):
        greet(at_dp((dev + k) % 32))
    greet({"sec_x": 1 - sx, "dp_x": 1 - xl})
    levels = [
        jnp.broadcast_to(sched_ref[:, r : r + 1].astype(jnp.float32), (4, 128)) for r in range(3)
    ]
    for r in range(2):
        sched[0, 4 * r : 4 * r + 4] = levels[r]
        sched[1, 4 * r : 4 * r + 4] = (levels[r + 1] - levels[r]) / LEVELS
    angles = sched[0] * frequency_ref[...]
    embedding = jnp.concatenate([jnp.cos(angles), jnp.sin(angles)], axis=-1)
    embed = jnp.dot(
        embedding.astype(jnp.bfloat16), time_weight_ref[...], preferred_element_type=jnp.float32
    )
    pl.semaphore_wait(barrier, 39)

    def copy(src, dst, send, recv, where):
        return pltpu.make_async_remote_copy(
            src_ref=src,
            dst_ref=dst,
            send_sem=send,
            recv_sem=recv,
            device_id=where,
            device_id_type=MESH,
        )

    started = []

    def start(what, when=None):
        started.append((what, when))
        if when is None:
            what.start()
        else:
            pl.when(when)(what.start)

    source = sx == core
    relay = sx != core

    def piece_a(a, z):
        return a * 16 + (z % 8) * 2 + core

    def piece_b(a, z):
        return a * 16 + (z % 8) * 2 + 1 - core

    z_up = {"dp_z": (zz + 1) % 8}
    z_down = {"dp_z": (zz + 7) % 8}
    x_mate = {"dp_x": 1 - xl}
    x_outer = {"dp_x": 1 - xl, "sec_x": 1 - sx}
    way = {0: z_up, 1: z_down, 2: x_mate, 3: x_outer}

    def go(p, towards, when=None):
        block = weight.at[core, p]
        start(
            copy(block, block, weight_send.at[p * 4 + towards], weight_recv.at[p], way[towards]),
            when,
        )

    def lend(p, when=None):
        block = weight.at[core, p]
        start(copy(block, block, lend_send.at[p], lend_recv.at[p], twin), when)

    def arrive(p, when=None):
        block = weight.at[core, p]
        landed = copy(block, block, weight_send.at[p], weight_recv.at[p], twin)
        if when is None:
            landed.wait_recv()
        else:
            pl.when(when)(landed.wait_recv)
        lend(p, when)

    mods[sx] = block_mod_ref[...]
    lend_mods = copy(block_mod_ref, mods.at[sx], mods_send, mods_recv, x_outer)
    start(lend_mods)

    @pl.when(source)
    def _():
        weight[core, dev] = block_ref[...]

    own_shard = copy(
        block_ref, weight.at[1 - core, dev], weight_send.at[128], weight_recv.at[dev], twin
    )
    start(own_shard, relay)
    for towards in (2, 3, 0, 1):
        go(piece_a(xl, zz), towards, source)
    lend(piece_a(xl, zz), source)

    first_stage = sy == 0

    for k in range(1, 4):
        start(
            copy(
                feature_shard_ref,
                feature_ref.at[sec],
                feature_send.at[k],
                feature_recv.at[sec],
                {"sec_y": (sy + k) % 4},
            )
        )
    feature_ref[sec] = feature_shard_ref[...]

    arrive(piece_b(xl, zz), source)

    go(piece_b(xl, zz), 0, source)
    go(piece_b(xl, zz), 1, source)
    go(piece_b(xl, zz), 2, source)
    go(piece_b(xl, zz), 3, source)

    arrive_a = piece_a(1 - xl, zz)
    arrive(arrive_a)
    go(arrive_a, 2, relay)

    go(arrive_a, 0)
    go(arrive_a, 1)

    arrive(piece_a(xl, zz), relay)

    go(piece_a(xl, zz), 0, relay)
    go(piece_a(xl, zz), 1, relay)

    vocab = table.shape[0]
    text_len, samples = ids_ref.shape
    ids[...] = jnp.zeros_like(ids)
    ids[0:text_len] = ids_ref[...].astype(jnp.float32)
    by_sample = ids[...].T.reshape(samples // 8, 8, -1)
    place = lax.broadcasted_iota(jnp.int32, by_sample.shape, 1)
    own_ids = jnp.sum(jnp.where(place == sec, by_sample, 0.0), axis=1)
    local_ids = own_ids.astype(jnp.int32) - dev * vocab
    lanes = lax.broadcasted_iota(jnp.int32, (samples // 8, vocab), 1)
    counts = jnp.zeros(lanes.shape, jnp.float32)
    for t in range(text_len):
        counts = counts + jnp.where(local_ids[:, t : t + 1] == lanes, 1.0, 0.0)
    load_table.wait()
    part = jnp.dot(
        counts.astype(jnp.bfloat16), table[...], preferred_element_type=jnp.float32
    ) / text_len
    for g in range(16):
        rows_out[g] = part[g : g + 1]
    rows_in[dev] = rows_out[dev // 2]
    for k in range(1, 32):
        other = (dev + k) % 32
        start(
            copy(
                rows_out.at[other // 2],
                rows_in.at[dev],
                row_send.at[k],
                row_recv.at[dev],
                at_dp(other),
            )
        )

    def take_x(z):
        p = piece_b(1 - xl, z)
        arrive(p)
        odd = z % 2
        go(p, 3, source & (odd == 1))
        go(p, 2, relay & (odd == 0))

    def take_z_b(k, up):
        z = zz + 8 - k if up else zz + k
        p = piece_b(xl, z)
        last = k == 4
        here = source & (xl == (0 if up else 1)) if last else source

        arrive(p, here)

        if k < 3:
            go(p, 0 if up else 1, here)
        elif k == 3:
            go(p, 0 if up else 1, source & (xl == (0 if up else 1)))
        go(p, 2, here)
        go(p, 3, here)

    def take_z_a(k, up):
        z = zz + 8 - k if up else zz + k
        for a in range(2):
            reach = (4 - a) if up else (3 + a)
            if k <= reach:
                p = piece_a(a, z)
                arrive(p)
                if k < reach:
                    go(p, 0 if up else 1)

    def ring_step(k):
        for up in (True, False):
            take_z_b(k, up)
        for up in (True, False):
            take_z_a(k, up)
        if k == 1:
            take_x(zz)
        else:
            take_x(zz + 9 - k)
            take_x(zz + k - 1)

    ring_step(1)

    ring_step(2)
    total = rows_in[dev]
    for k in range(1, 32):
        other = (dev + 32 - k) % 32
        copy(
            rows_out.at[0], rows_in.at[other], row_send.at[k], row_recv.at[other], at_dp(other)
        ).wait_recv()
        total = total + rows_in[other]
    pooled[sec] = total
    for k in range(1, 8):
        start(
            copy(
                pooled.at[sec],
                pooled.at[sec],
                pooled_send.at[k],
                pooled_recv.at[sec],
                at_section((sec + k) % 8),
            )
        )
    ring_step(3)
    ring_step(4)
    for k in range(1, 8):
        other = (sec + k) % 8
        copy(
            pooled.at[other],
            pooled.at[other],
            pooled_send.at[k],
            pooled_recv.at[other],
            at_section(other),
        ).wait_recv()
    for r in range(8):
        cond[r] = jax.nn.silu(embed[r : r + 1] + pooled[core * 4 + r % 4])
    take_x(zz + 4)

    for z in range(8):
        arrive(piece_b(xl, z), relay)

    student_ref[dev] = student_shard_ref[...]
    for k in range(1, 16):
        start(
            copy(
                student_shard_ref,
                student_ref.at[dev],
                student_send.at[k],
                student_recv.at[dev],
                at_dp((dev + 2 * k) % 32),
            )
        )
    copy(block_mod_ref, mods.at[1 - sx], mods_send, mods_recv, x_outer).wait_recv()
    for p in range(32):
        block = weight.at[1 - core, p]
        copy(block, block, lend_send.at[p], lend_recv.at[p], twin).wait_recv()

    def pass_on(t, slot, c, where):
        cols = pl.ds(c * chunk, chunk)
        return copy(
            sent.at[t, :, cols],
            inbox.at[slot, :, cols],
            sent_send.at[t * chunks + c],
            inbox_recv.at[slot * chunks + c],
            where,
        )

    here = mbs // 2

    def hop(t, p, j, c):
        @pl.when(sy < 3)
        def _():
            pass_on(t, t, c, {"sec_y": (sy + 1) % 4}).start()

        @pl.when(sy == 3)
        def _():
            if p == 0:
                pass_on(t, t + here, c, {"sec_y": 0}).start()
            else:

                @pl.when((sx == 1) & (j == here - 1))
                def _():
                    cols = slice(c * chunk, (c + 1) * chunk)
                    inbox[2 * here, :, cols] = sent[t, :, cols]

                @pl.when((sx == 0) | (j < here - 1))
                def _():
                    pass_on(t, 2 * here, c, at_section(sx * here + j)).start()

    def share_first(j):
        return copy(
            start_x.at[j], first_x, first_send.at[j], first_recv, at_section(sx * here + j)
        )

    def run_pass(p):
        def step(j, carry):
            t = p * here + j
            sample = (sx * here + j) // 2
            for c in range(chunks):
                arrived = pass_on(t, t, c, twin)
                if p == 0:
                    pl.when(sy > 0)(arrived.wait_recv)
                else:
                    arrived.wait_recv()
            if p == 0:

                @pl.when(first_stage)
                def _():
                    held[...] = noise_ref[sx * here + j]

                @pl.when(sy > 0)
                def _():
                    held[...] = inbox[t]

            else:
                held[...] = inbox[t]

                @pl.when(first_stage)
                def _():
                    moved = (
                        noise_ref[sx * here + j].astype(jnp.float32)
                        + sched[1, pl.ds(sample, 1), :1] * held[...].astype(jnp.float32)
                    ).astype(jnp.bfloat16)
                    held[...] = moved
                    start_x[j] = moved

                    @pl.when((j == 0) & (sx == 0))
                    def _():
                        first_x[...] = moved

                    @pl.when((j > 0) | (sx > 0))
                    def _():
                        share_first(j).start()

            cond_row = cond[p * 4 + sample]
            for b in range(2):
                hidden = held[...].astype(jnp.float32)
                mean_sq = jnp.mean(hidden * hidden, axis=-1, keepdims=True)
                inputs = (
                    hidden * lax.rsqrt(mean_sq + 1e-06) * (1.0 + cond_row * mods[b, 0])
                    + cond_row * mods[b, 1]
                ).astype(jnp.bfloat16)
                gate = 1.0 + cond_row * mods[b, 2]
                for c in range(chunks):
                    cols = slice(c * chunk, (c + 1) * chunk)
                    mixed = jnp.dot(
                        inputs,
                        weight[b, :, :, cols].reshape(width, chunk),
                        preferred_element_type=jnp.float32,
                    )
                    result = (hidden[:, cols] + gate[:, cols] * jax.nn.gelu(mixed)).astype(
                        jnp.bfloat16
                    )
                    if b == 0:
                        held[:, cols] = result
                    else:
                        sent[t, :, cols] = result
                        hop(t, p, j, c)

            return carry

        lax.fori_loop(0, here, step, 0)

    for k in range(4):
        slot = ((sy + k) % 4) * 2 + sx
        block = feature_ref.at[slot]
        across = copy(
            block, block, feature_send.at[4 + k], feature_recv.at[slot], x_outer
        )
        if k > 0:
            across.wait_recv()
        start(across)

    run_pass(0)
    for k in range(16):
        slot = (dev + 2 * k) % 32
        block = student_ref.at[slot]
        to_twin = copy(block, block, student_send.at[16 + k], student_recv.at[slot], twin)
        if k > 0:
            to_twin.wait_recv()
        start(to_twin)
    for k in range(16):
        slot = (dev + 2 * k) % 32 + 1 - 2 * core
        block = student_ref.at[slot]
        copy(block, block, student_send.at[0], student_recv.at[slot], twin).wait_recv()

    def own_cols(x):
        n = student_ref.shape[2]
        picked = x[:, 0:n]
        for k in range(1, 8):
            picked = jnp.where(sec == k, x[:, k * n : (k + 1) * n], picked)
        return picked

    root = math.sqrt(2.0 / math.pi)
    for n in range(4):
        latents = noise_ref[2 * n : 2 * n + 2].reshape(2 * rows, width).astype(jnp.float32)
        mean_sq = jnp.mean(latents * latents, axis=-1, keepdims=True)
        cond_row = cond[n]
        student_in = (
            latents * lax.rsqrt(mean_sq + 1e-06) * (1.0 + cond_row * student_mod_ref[0:1])
            + cond_row * student_mod_ref[1:2]
        ).astype(jnp.bfloat16)
        mixed = jnp.dot(
            student_in,
            student_ref[...].reshape(width, student_ref.shape[2]),
            preferred_element_type=jnp.float32,
        )
        bent = jnp.tanh(root * (mixed + 0.044715 * mixed * mixed * mixed))
        half = 0.5 * (1.0 + bent)
        bend = half + 0.5 * mixed * (1.0 - bent * bent) * root * (
            1.0 + 3.0 * 0.044715 * mixed * mixed
        )
        gate = own_cols(1.0 + cond_row * student_mod_ref[2:3])
        level = sched[0, n : n + 1, :1] / LEVELS
        z = own_cols(latents)
        moved = z - level * (z + gate * (mixed * half))
        slope[2 * n * rows : 2 * (n + 1) * rows] = -level * gate * bend
        student_rows[2 * n * rows : 2 * (n + 1) * rows] = student_in
        feat_part[2 * n : 2 * n + 2] = (
            jnp.dot(
                moved.astype(jnp.bfloat16),
                feature_shard_ref[...],
                preferred_element_type=jnp.float32,
            )
            .astype(jnp.bfloat16)
            .reshape(2, rows, -1)
        )

    slope_t[...] = slope[...].T

    def send_feat(k, slot):
        return copy(
            feat_part.at[k], feats.at[slot], feat_send.at[k], feat_recv.at[slot], at_section(k)
        )

    for k in range(1, 8):
        start(send_feat((sec + k) % 8, sec))
    run_pass(1)

    last_self = sec == 7
    first_self = sec == 0

    for c in range(chunks):
        pl.when(jnp.logical_not(last_self))(pass_on(0, 2 * here, c, twin).wait_recv)

    @pl.when(jnp.logical_not(first_self))
    def _():
        share_first(0).wait_recv()

    x2 = (
        first_x[...].astype(jnp.float32)
        + sched[1, pl.ds(4 + sec // 2, 1), :1] * inbox[2 * here].astype(jnp.float32)
    ).astype(jnp.bfloat16)
    teacher_ref[sec] = x2
    for k in range(4):
        slot = ((sy + k) % 4) * 2 + 1 - sx
        block = feature_ref.at[slot]
        copy(block, block, feature_send.at[0], feature_recv.at[slot], twin).wait_recv()

    sections = 8
    chips = summed.shape[0]
    piece = summed.shape[1]
    feat = feats.shape[2]
    chip = xl * 8 + zz

    def at_chip(q):
        return {"dp_x": q // 8, "dp_z": q % 8}

    def send_grad(k, slot):
        return copy(grads.at[slot], grads.at[slot], grad_send.at[k], grad_recv.at[slot], at_section(k))

    def send_piece(q, slot):
        return copy(summed.at[q], pieces.at[slot], piece_send.at[q], piece_recv.at[slot], at_chip(q))

    def send_final(q, slot):
        block = final.at[core, slot]
        return copy(block, block, final_send.at[q], final_recv.at[slot], at_chip(q))

    def send_twin(half, slot):
        block = final.at[half, slot]
        return copy(block, block, twin_send.at[slot], twin_recv.at[slot], twin)

    send_half = copy(half_out, half_in, half_send, half_recv, twin)

    def send_out(k, slot):
        return copy(teacher_ref.at[slot], teacher_ref.at[slot], out_send.at[k], out_recv.at[slot], at_section(k))

    feat_teacher = jnp.dot(
        x2, feature_ref[...].reshape(width, feat), preferred_element_type=jnp.float32
    )
    feat_student = feat_part[sec].astype(jnp.float32)
    for k in range(1, sections):
        other = (sec + k) % sections
        send_feat(other, other).wait_recv()
        feat_student = feat_student + feats[other].astype(jnp.float32)

    def unit(f):
        positive = jnp.maximum(f, 0.0)
        scale = lax.rsqrt(jnp.mean(positive * positive, axis=-1, keepdims=True) + 1e-06)
        return positive * scale, scale

    unit_s, scale_s = unit(feat_student)
    unit_t, _ = unit(feat_teacher)
    gap = unit_s - unit_t
    lin = lin_ref[...]
    dist_ref[...] = lax.dot_general(
        lin,
        gap * gap,
        (((1,), (1,)), ((), ())),
        preferred_element_type=jnp.float32,
        precision=lax.Precision.HIGHEST,
    )
    tokens = token_ref.shape[1]
    own_token = lax.broadcasted_iota(jnp.int32, (rows, tokens), 0) + sec * rows
    token_col = jnp.sum(
        jnp.where(
            lax.broadcasted_iota(jnp.int32, (rows, tokens), 1) == own_token, token_ref[...], 0.0
        ),
        axis=1,
        keepdims=True,
    )
    unit_grad = 2.0 * token_col * lin * gap
    mean_dot = jnp.mean(unit_grad * unit_s, axis=-1, keepdims=True)
    feat_grad = scale_s * (unit_grad - unit_s * mean_dot)
    grads[sec] = jnp.where(feat_student > 0.0, feat_grad, 0.0).astype(jnp.bfloat16)
    for k in range(1, sections):
        send_grad((sec + k) % sections, sec).start()
    for k in range(1, sections):
        other = (sec + k) % sections
        send_grad(other, other).wait_recv()

    out_grad = lax.dot_general(
        feature_ref[sec],
        grads[...].reshape(sections * rows, feat),
        (((1,), (1,)), ((), ())),
        preferred_element_type=jnp.float32,
    )
    mixed_grad = (out_grad * slope_t[...]).astype(jnp.bfloat16)
    product = jnp.dot(mixed_grad, student_rows[...], preferred_element_type=jnp.float32)
    lanes = 128
    blocks = width // lanes
    half_cols = product.shape[0] // 2
    for half in range(2):
        kept = product[half * half_cols : (half + 1) * half_cols]
        partial[half] = jnp.concatenate(
            [kept[:, b * lanes : (b + 1) * lanes] for b in range(blocks)], axis=0
        ).reshape(chips, piece, lanes)
    half_out[...] = partial[1 - core].astype(jnp.bfloat16)
    send_half.start()
    send_half.wait_recv()
    summed[...] = (partial[core] + half_in[...].astype(jnp.float32)).astype(jnp.bfloat16)
    for k in range(1, chips):
        send_piece((chip + k) % chips, chip).start()
    for k in range(1, sections):
        send_out((sec + k) % sections, sec).start()
    total = summed[chip].astype(jnp.float32)
    for k in range(1, chips):
        other = (chip + chips - k) % chips
        send_piece(other, other).wait_recv()
        total = total + pieces[other].astype(jnp.float32)
    final[core, chip] = total.astype(jnp.bfloat16)
    for k in range(1, chips):
        send_final((chip + k) % chips, chip).start()
    send_twin(core, chip).start()
    for k in range(1, chips):
        other = (chip + chips - k) % chips
        send_final(other, other).wait_recv()
        send_twin(core, other).start()
    for k in range(chips):
        other = (chip + chips - k) % chips
        send_twin(1 - core, other).wait_recv()
    for half in range(2):
        kept = final[half].astype(jnp.float32).reshape(blocks * half_cols, lanes)
        for b in range(blocks):
            grad_ref[half * half_cols : (half + 1) * half_cols, b * lanes : (b + 1) * lanes] = kept[
                b * half_cols : (b + 1) * half_cols
            ]

    for k in range(1, sections):
        other = (sec + k) % sections
        send_out(other, other).wait_recv()
        send_out(other, sec).wait_send()
    send_half.wait_send()
    for k in range(1, sections):
        send_grad((sec + k) % sections, sec).wait_send()
    for k in range(1, chips):
        send_piece((chip + k) % chips, chip).wait_send()
        send_final((chip + k) % chips, chip).wait_send()
    for k in range(chips):
        send_twin(core, k).wait_send()

    def drain(t, carry):
        for c in range(chunks):
            pass_on(t, t, c, twin).wait_send()
        return carry

    lax.fori_loop(0, 2 * here - 1, drain, 0)

    for c in range(chunks):
        pl.when(jnp.logical_not(last_self))(pass_on(2 * here - 1, 0, c, twin).wait_send)

    @pl.when(first_stage)
    def _():
        for j in range(1, here):
            share_first(j).wait_send()

        @pl.when(sx > 0)
        def _():
            share_first(0).wait_send()

    for what, when in started:
        if when is None:
            what.wait_send()
        else:
            pl.when(when)(what.wait_send)


def run_train(
    noise,
    ids,
    sched,
    frequency,
    time_weight,
    block,
    block_mod,
    student_shard,
    feature_shard,
    student_mod,
    lin,
    token,
    table,
):
    mbs, rows, width = noise.shape
    vocab = table.shape[0]
    piece = block.shape[0]
    cols = student_shard.shape[1]
    feat_rows, feat = feature_shard.shape
    part = cols * width // (32 * 128)
    vmem = pl.BlockSpec(memory_space=pltpu.VMEM)
    dma = pltpu.SemaphoreType.DMA
    bf16 = jnp.bfloat16
    f32 = jnp.float32
    return pl.pallas_call(
        train_kernel,
        out_shape=(
            jax.ShapeDtypeStruct((mbs, rows, width), bf16),
            jax.ShapeDtypeStruct((1, rows), f32),
            jax.ShapeDtypeStruct((cols, width), f32),
        ),
        in_specs=[vmem] * 12 + [pl.BlockSpec(memory_space=pl.ANY)],
        out_specs=(vmem,) * 3,
        scratch_shapes=[
            pltpu.VMEM((128, ids.shape[1]), f32),
            pltpu.VMEM((vocab, width), bf16),
            pltpu.VMEM((2, 32, piece, width), bf16),
            pltpu.VMEM((2, 3, 1, width), f32),
            pltpu.VMEM((16, 1, width), f32),
            pltpu.VMEM((32, 1, width), f32),
            pltpu.VMEM((8, 1, width), f32),
            pltpu.VMEM((2, 8, 128), f32),
            pltpu.VMEM((8, 1, width), f32),
            pltpu.VMEM((rows, width), bf16),
            pltpu.VMEM((mbs, rows, width), bf16),
            pltpu.VMEM((mbs + 1, rows, width), bf16),
            pltpu.VMEM((mbs // 2, rows, width), bf16),
            pltpu.VMEM((rows, width), bf16),
            pltpu.VMEM((32, piece, cols), bf16),
            pltpu.VMEM((8, feat_rows, feat), bf16),
            pltpu.VMEM((mbs * rows, width), bf16),
            pltpu.VMEM((mbs * rows, cols), f32),
            pltpu.VMEM((cols, mbs * rows), f32),
            pltpu.VMEM((8, rows, feat), bf16),
            pltpu.VMEM((8, rows, feat), bf16),
            pltpu.VMEM((8, rows, feat), bf16),
            pltpu.VMEM((2, 16, part, 128), f32),
            pltpu.VMEM((16, part, 128), bf16),
            pltpu.VMEM((16, part, 128), bf16),
            pltpu.VMEM((16, part, 128), bf16),
            pltpu.VMEM((16, part, 128), bf16),
            pltpu.VMEM((2, 16, part, 128), bf16),
            dma,
            dma((129,)),
            dma((32,)),
            dma((32,)),
            dma((32,)),
            dma((8,)),
            dma((8,)),
            dma((32,)),
            dma((32,)),
            dma(((mbs + 1) * 6,)),
            dma((mbs * 6,)),
            dma((mbs // 2,)),
            dma,
            dma((32,)),
            dma((32,)),
            dma((8,)),
            dma((8,)),
            dma,
            dma,
            dma((8,)),
            dma((8,)),
            dma((8,)),
            dma((8,)),
            dma,
            dma,
            dma((16,)),
            dma((16,)),
            dma((16,)),
            dma((16,)),
            dma((16,)),
            dma((16,)),
            dma((8,)),
            dma((8,)),
        ],
        compiler_params=pltpu.CompilerParams(
            collective_id=0, has_side_effects=True, vmem_limit_bytes=56 * 1024 * 1024
        ),
    )(
        noise,
        ids,
        sched,
        frequency,
        time_weight,
        block,
        block_mod,
        student_shard,
        feature_shard,
        student_mod,
        lin,
        token,
        table,
    )


def local(
    noise,
    sched_index,
    text_ids,
    text_table,
    time_weight,
    block_weight,
    block_mod,
    student_weight,
    student_mod,
    feature_weight,
    lin_weight,
    token_weight,
):
    batches, tokens, model_width = noise.shape
    sections = lax.axis_size(SECTION)
    row_count = batches * tokens
    share_rows = row_count // sections
    half_freq = time_weight.shape[0] // 2
    frequency = np.exp(-math.log(10000.0) * np.arange(half_freq, dtype=np.float32) / half_freq)
    teacher, token_distance, student_grad = run_train(
        noise.reshape(sections, share_rows, model_width),
        text_ids.T,
        sched_index,
        jnp.asarray(frequency[None, :], jnp.float32),
        time_weight,
        block_weight[0],
        jnp.moveaxis(block_mod, 0, 1),
        student_weight,
        feature_weight,
        student_mod,
        lin_weight[None, :],
        token_weight[None, :],
        text_table,
    )
    return (
        teacher.reshape(noise.shape),
        student_grad.T,
        token_distance.reshape(share_rows),
    )


def solution(mesh):
    torus = Mesh(mesh.devices.reshape(2, 8, 2, 4, 2), DP + SECTION)
    in_specs = (
        P(DP, None, None),
        P(DP, None),
        P(),
        P(DP, None),
        P(),
        P(SECTION, DP, None),
        P(SECTION, None, None),
        P(DP, SECTION),
        P(),
        P(SECTION, None),
        P(),
        P(DP),
    )
    out_specs = (P(DP, None, None), P(None, SECTION), P(DP + SECTION))
    return jax.shard_map(local, mesh=torus, in_specs=in_specs, out_specs=out_specs, check_vma=False)
```
